128 devices in a mesh: region: 16 (over x, z), orbit: 8 (over y, core).
Axes of the slice: x: 4, y: 4, z: 4, core: 2. Of those that a mesh axis runs over, the one named last changes fastest.
Arguments:
- queries: bfloat16 [8, 48, 256, 512], P('orbit', 'region'), may hold values from -24 to 24
- keys: bfloat16 [8, 16, 512, 512], P('orbit', 'region'), may hold values from -24 to 24
- values: bfloat16 [8, 16, 512, 512], P('orbit', 'region'), may hold values from -6 to 6
- block_lists: int32 [8, 48, 8], P('orbit', 'region'), may hold values from 0 to 15, as said below
- band_counts: int32 [8, 48], P('orbit', 'region'), may hold values from 4 to 8, as said below
- cotangent: bfloat16 [8, 48, 256, 1024], P('orbit', 'region'), may hold values from -6 to 6
- out_weight: bfloat16 [512, 1024], replicated, may hold values from -0.25 to 0.25
Outputs:
- layer_out: bfloat16 [8, 48, 256, 1024], P('orbit', 'region')
- d_queries: bfloat16 [8, 48, 256, 512], P('orbit', 'region')
- d_keys: bfloat16 [8, 16, 512, 512], P('orbit', 'region')
- d_values: bfloat16 [8, 16, 512, 512], P('orbit', 'region')
- d_weight: float32 [512, 1024], replicated
The draws below stay inside these ranges and needn't reach their ends.
Inputs may be any that keep to these rules, and one draw needn't show every extreme that they name: `block_lists`: each tile's row holds 8 different band numbers; only the first band_counts entries are read. `band_counts`: tiles of the outermost regions read the most bands.
All inputs are finite; a program needn't handle non-finite values.
Results may differ from the reference program's by a relative error of at most 0.035.
Values may be sent and summed in bfloat16 or wider, within the bound.
No kernel may reach another device: no remote copies, remote signals or barrier semaphores. Data moves between devices by JAX's collectives and lax.ppermute only.
A program may use at most 192 MiB of HBM per device.

```python
import jax
import jax.numpy as jnp
from jax import lax

HEADS = 8
HEAD_DIM = 64
D = 1024
BT = 512
QROWS = 256
MAXB = 8
MINB = 4
TILES_DEV = 3
HW = 512
SAMPLES = 8
BANDS = 16
TILES = 48


def tile_plan(key):
    count_key, list_key = jax.random.split(key)
    region = jnp.arange(TILES) // TILES_DEV
    level = jnp.abs(2 * region + 1 - BANDS) * (MAXB - MINB + 1) // BANDS
    extra = jax.random.randint(count_key, (SAMPLES, TILES), 0, 1 << 20) % (level + 1)[None, :]
    counts = MINB + extra
    counts = counts.at[:, 0].set(MINB + level[0])
    list_keys = jax.random.split(list_key, SAMPLES * TILES)
    perms = jax.vmap(lambda one: jax.random.permutation(one, BANDS))(list_keys)
    lists = perms[:, :MAXB].reshape(SAMPLES, TILES, MAXB)
    return (lists.astype(jnp.int32), counts.astype(jnp.int32))


def draw_block_lists(key, part):
    return tile_plan(key)[0]


def draw_band_counts(key, part):
    return tile_plan(key)[1]


def draw_queries(key, part):
    key = jax.random.fold_in(key, 11)
    shape = (SAMPLES, TILES, QROWS, HW)
    return jnp.clip(jax.random.normal(key, shape, jnp.float32), -6.0, 6.0).astype(jnp.bfloat16)


def draw_keys(key, part):
    key = jax.random.fold_in(key, 23)
    shape = (SAMPLES, BANDS, BT, HW)
    return jnp.clip(jax.random.normal(key, shape, jnp.float32), -6.0, 6.0).astype(jnp.bfloat16)


def block_levels(rng, extent, cuts, least, largest):
    gain, own = 1.0, jax.random.fold_in(rng, 6)
    for axis_at, shards_of in cuts:
        steps = jnp.exp(jax.random.uniform(jax.random.fold_in(own, axis_at), (shards_of,), jnp.float32, least / len(cuts), largest / len(cuts)))
        gain = gain * jnp.repeat(steps, extent[axis_at] // shards_of).reshape([-1 if axis == axis_at else 1 for axis in range(len(extent))])
    return gain


def normal_values(own_key, shape, width, limit, cuts=(), kind=jnp.bfloat16):
    drawn = width * jax.random.normal(own_key, shape, jnp.float32)
    if cuts:
        drawn = drawn * block_levels(own_key, shape, cuts, -0.22, 0.18)
    return jnp.clip(drawn, -limit, limit).astype(kind)


def setup_inputs(seed: int = 0) -> dict:
    arg_keys = jax.random.split(jax.random.key(seed), 8)
    queries = draw_queries(jax.random.fold_in(arg_keys[7], 71), 0)
    keys = draw_keys(jax.random.fold_in(arg_keys[7], 71), 0)
    values = normal_values(arg_keys[2], (SAMPLES, BANDS, BT, HW), 1.0, 6.0, ((0, 8), (1, 16)))
    block_lists = draw_block_lists(jax.random.fold_in(arg_keys[7], 71), 0)
    band_counts = draw_band_counts(jax.random.fold_in(arg_keys[7], 71), 0)
    cotangent = normal_values(arg_keys[5], (SAMPLES, TILES, QROWS, D), 1.0, 6.0, ((0, 8), (1, 16)))
    out_weight = normal_values(arg_keys[6], (HW, D), HW ** -0.5, 0.25)
    return {"queries": queries, "keys": keys, "values": values, "block_lists": block_lists, "band_counts": band_counts, "cotangent": cotangent, "out_weight": out_weight}


def tile_terms(query_tile, grad_tile, band_ids, band_count, keys_s, values_s, out_weight):
    scale = HEAD_DIM ** -0.5
    rows = query_tile.shape[0]
    slot_keys = keys_s[band_ids].reshape(MAXB * BT, HEADS, HEAD_DIM).astype(jnp.float32)
    slot_values = values_s[band_ids].reshape(MAXB * BT, HEADS, HEAD_DIM).astype(jnp.float32)
    valid = jnp.repeat(jnp.arange(MAXB) < band_count, BT)
    query_heads = query_tile.reshape(rows, HEADS, HEAD_DIM).astype(jnp.float32)
    scores = jnp.einsum('qhd,khd->hqk', query_heads, slot_keys) * scale
    scores = jnp.where(valid[None, None, :], scores, -jnp.inf)
    top = jnp.max(scores, axis=-1, keepdims=True)
    lse = top + jnp.log(jnp.sum(jnp.exp(scores - top), axis=-1, keepdims=True))
    probs = jnp.exp(scores - lse).astype(jnp.bfloat16)
    attn = jnp.einsum('hqk,khd->qhd', probs.astype(jnp.float32), slot_values).reshape(rows, HW).astype(jnp.bfloat16)
    layer = jnp.dot(attn, out_weight, preferred_element_type=jnp.float32).astype(jnp.bfloat16)
    weight_term = jnp.dot(attn.T, grad_tile, preferred_element_type=jnp.float32)
    d_attn = jnp.dot(grad_tile, out_weight.T, preferred_element_type=jnp.float32).astype(jnp.bfloat16)
    attn_heads = attn.reshape(rows, HEADS, HEAD_DIM).astype(jnp.float32)
    dattn_heads = d_attn.reshape(rows, HEADS, HEAD_DIM).astype(jnp.float32)
    delta = jnp.einsum('qhd,qhd->hq', attn_heads, dattn_heads)
    d_probs = jnp.einsum('qhd,khd->hqk', dattn_heads, slot_values)
    d_scores = (probs.astype(jnp.float32) * (d_probs - delta[:, :, None]) * scale).astype(jnp.bfloat16)
    d_scores_f = d_scores.astype(jnp.float32)
    d_query = jnp.einsum('hqk,khd->qhd', d_scores_f, slot_keys).reshape(rows, HW).astype(jnp.bfloat16)
    key_part = jnp.einsum('hqk,qhd->khd', d_scores_f, query_heads).reshape(MAXB, BT, HW)
    value_part = jnp.einsum('hqk,qhd->khd', probs.astype(jnp.float32), dattn_heads).reshape(MAXB, BT, HW)
    return layer, d_query, weight_term, key_part, value_part


def reference(queries, keys, values, block_lists, band_counts, cotangent, out_weight):
    groups = TILES // TILES_DEV

    def one_sample(packed):
        query_s, keys_s, values_s, lists_s, counts_s, grads_s = packed

        def one_group(carry, group):
            total_k, total_v, total_w = carry
            part_k = jnp.zeros((BANDS, BT, HW), jnp.float32)
            part_v = jnp.zeros((BANDS, BT, HW), jnp.float32)
            layers = []
            dqs = []
            for inner in range(TILES_DEV):
                tile = (group * TILES_DEV + inner).astype(jnp.int32)
                query_tile = lax.dynamic_index_in_dim(query_s, tile, 0, keepdims=False)
                grad_tile = lax.dynamic_index_in_dim(grads_s, tile, 0, keepdims=False)
                band_ids = lax.dynamic_index_in_dim(lists_s, tile, 0, keepdims=False)
                band_count = lax.dynamic_index_in_dim(counts_s, tile, 0, keepdims=False)
                layer, d_query, weight_term, key_part, value_part = tile_terms(
                    query_tile, grad_tile, band_ids, band_count, keys_s, values_s, out_weight)
                part_k = part_k.at[band_ids].add(key_part)
                part_v = part_v.at[band_ids].add(value_part)
                total_w = total_w + weight_term
                layers.append(layer)
                dqs.append(d_query)
            rounded_k = lax.optimization_barrier(part_k.astype(jnp.bfloat16)).astype(jnp.float32)
            rounded_v = lax.optimization_barrier(part_v.astype(jnp.bfloat16)).astype(jnp.float32)
            return (total_k + rounded_k, total_v + rounded_v, total_w), (jnp.stack(layers), jnp.stack(dqs))

        start = (jnp.zeros((BANDS, BT, HW), jnp.float32), jnp.zeros((BANDS, BT, HW), jnp.float32),
                 jnp.zeros((HW, D), jnp.float32))
        final, stacked = lax.scan(one_group, start, jnp.arange(groups).astype(jnp.int32))
        layer_s = stacked[0].reshape(TILES, QROWS, D)
        dq_s = stacked[1].reshape(TILES, QROWS, HW)
        return layer_s, dq_s, final[0].astype(jnp.bfloat16), final[1].astype(jnp.bfloat16), final[2]

    layer_out, d_queries, d_keys, d_values, weight_terms = lax.map(
        one_sample, (queries, keys, values, block_lists, band_counts, cotangent))
    d_weight = jnp.sum(weight_terms, axis=0)
    return layer_out, d_queries, d_keys, d_values, d_weight
```

```python
import functools

import jax
import jax.numpy as jnp
from jax import lax
from jax.experimental import pallas as pl
from jax.experimental.pallas import tpu as pltpu
from jax.sharding import PartitionSpec as P

HEADS = 8
HEAD_DIM = 64
BANDS = 16
BT = 512
QROWS = 256
HALF = 128
TILES_DEV = 3
TILES = 48
MAXB = 8
D = 1024
HW = 512
CHUNKS = 2
PAIRS = 208
SCALE = HEAD_DIM**-0.5
LOW = -1e30
BF16 = jnp.bfloat16
F32 = jnp.float32

NT = (((1,), (1,)), ((), ()))


def dot(a, b, dims=(((1,), (0,)), ((), ()))):
    return lax.dot_general(a, b, dims, preferred_element_type=F32)


def params(mib=56):
    return pltpu.CompilerParams(vmem_limit_bytes=mib << 20)


def cost(flops, nbytes, exps=0):
    return pl.CostEstimate(flops=int(flops), bytes_accessed=int(nbytes), transcendentals=int(exps))


VMEM = pl.BlockSpec(memory_space=pltpu.VMEM)
SMEM = pl.BlockSpec(memory_space=pltpu.SMEM)


def pack_body(q_ref, k_ref, v_ref, out_ref):
    kt = k_ref[...].T
    vt = v_ref[...].T
    qt = (q_ref[...].astype(F32) * SCALE).astype(BF16).T
    for head in range(2):
        rows = slice(head * 64, head * 64 + 64)
        for half in range(2):
            dest = 2 * head + half
            for j in range(4):
                lanes = slice(j * 128, j * 128 + 128)
                out_ref[dest, j * 128 : j * 128 + 64, :] = kt[rows, lanes]
                out_ref[dest, j * 128 + 64 : j * 128 + 128, :] = vt[rows, lanes]
            for t in range(TILES_DEV):
                low = t * QROWS + half * HALF
                out_ref[dest, BT + t * 64 : BT + t * 64 + 64, :] = qt[rows, low : low + HALF]


def pack(q, k, v):
    rows = BT + TILES_DEV * 64
    return pl.pallas_call(
        pack_body,
        grid=(4,),
        in_specs=[
            pl.BlockSpec((TILES_DEV * QROWS, 128), lambda p: (0, p)),
            pl.BlockSpec((BT, 128), lambda p: (0, p)),
            pl.BlockSpec((BT, 128), lambda p: (0, p)),
        ],
        out_specs=pl.BlockSpec((4, rows, 128), lambda p: (p, 0, 0)),
        out_shape=jax.ShapeDtypeStruct((16, rows, 128), BF16),
        compiler_params=params(24),
        cost_estimate=cost(0, 8e6),
        name="pack",
    )(q, k, v)


def dattn_body(w_ref, g_ref, out_ref):
    dt = dot(w_ref[...], g_ref[...], NT).astype(BF16)
    for head in range(2):
        for half in range(2):
            for t in range(TILES_DEV):
                low = t * QROWS + half * HALF
                out_ref[2 * head + half, t * 64 : t * 64 + 64, :] = dt[
                    head * 64 : head * 64 + 64, low : low + HALF
                ]


def dattn(w, g):
    rows = TILES_DEV * QROWS
    return pl.pallas_call(
        dattn_body,
        grid=(4,),
        in_specs=[
            pl.BlockSpec((128, D), lambda p: (p, 0)),
            pl.BlockSpec((rows, D), lambda p: (0, 0)),
        ],
        out_specs=pl.BlockSpec((4, TILES_DEV * 64, 128), lambda p: (p, 0, 0)),
        out_shape=jax.ShapeDtypeStruct((16, TILES_DEV * 64, 128), BF16),
        compiler_params=params(24),
        cost_estimate=cost(2 * rows * D * HW, 4e6),
        name="dattn",
    )(w, g)


def plan_of(lists, counts):
    slots = jnp.arange(MAXB)[None, :] < counts[:, None]
    member = (
        (lists[:, :, None] == jnp.arange(BANDS)[None, None, :]) & slots[:, :, None]
    ).any(axis=1)
    member = member.T.astype(jnp.int32)
    place = jnp.cumsum(member, axis=1) - member
    size = (member.sum(axis=1) + 1) // 2
    base = jnp.cumsum(size) - size
    flat = jnp.where(member > 0, 2 * base[:, None] + place, -1)
    hit = flat[None] == jnp.arange(2 * PAIRS)[:, None, None]
    tile = jnp.arange(TILES)[None, None, :]
    band = jnp.arange(BANDS)[None, :, None]
    code = jnp.sum(jnp.where(hit, band * 64 + tile + 1, 0), axis=(1, 2)).reshape(PAIRS, 2)
    who = jnp.where(code > 0, (code & 63) - 1, TILES)
    number = (size.sum() + 1) // 2
    return jnp.stack(
        [who[:, 0], who[:, 1], code[:, 0] >> 6, jnp.full((PAIRS,), number, jnp.int32)]
    ).astype(jnp.int32)


def forward_body(plan, recv, attn_ref, lse_ref, kv_ref, kt_ref, qt_ref, vt, top, total, acc, s0, s1):
    def unpack_band(b, carry):
        kvt = jnp.concatenate([recv[b, j * 128 : j * 128 + 128, :] for j in range(4)], axis=1)
        kv_ref[b] = kvt.T
        kt_ref[b] = kvt[:64]
        vt[b] = kvt[64:]
        for t in range(TILES_DEV):
            qt_ref[b * TILES_DEV + t] = recv[b, BT + t * 64 : BT + t * 64 + 64, :]
        return carry

    lax.fori_loop(0, BANDS, unpack_band, 0)
    qt_ref[TILES] = jnp.zeros((64, HALF), BF16)
    top[...] = jnp.full(top.shape, LOW, F32)
    total[...] = jnp.zeros(total.shape, F32)
    acc[...] = jnp.zeros(acc.shape, F32)
    blank = jnp.zeros((64, 2 * HALF), BF16)

    def scores(i, dst):
        w = jnp.concatenate([qt_ref[plan[0, i]], qt_ref[plan[1, i]]], axis=1)
        dst[...] = dot(kv_ref[plan[2, i]], jnp.concatenate([w, blank], axis=0))

    def absorb(i, src):
        a, c, b = plan[0, i], plan[1, i], plan[2, i]
        old = jnp.concatenate([top[a], top[c]], axis=1)
        new = jnp.maximum(old, jnp.max(src[...], axis=0, keepdims=True))
        fade = jnp.exp(old - new)
        p = jnp.exp(src[...] - new)
        part = jnp.sum(p, axis=0, keepdims=True)
        o = dot(vt[b], p.astype(BF16))
        for x, lanes in ((a, slice(0, HALF)), (c, slice(HALF, 2 * HALF))):
            top[x] = new[:, lanes]
            total[x] = total[x] * fade[:, lanes] + part[:, lanes]
            acc[x] = acc[x] * fade[:, lanes] + o[:, lanes]

    scores(0, s0)

    def two(j, carry):
        scores(2 * j + 1, s1)
        absorb(2 * j, s0)
        scores(2 * j + 2, s0)
        absorb(2 * j + 1, s1)
        return carry

    lax.fori_loop(0, plan[3, 0], two, 0)

    def finish(x, carry):
        attn_ref[x] = (acc[x] / total[x]).astype(BF16)
        lse_ref[x] = top[x] + jnp.log(total[x])
        return carry

    lax.fori_loop(0, TILES, finish, 0)
    lse_ref[TILES] = jnp.full((1, HALF), -LOW, F32)


def forward(plan, recv):
    return pl.pallas_call(
        forward_body,
        in_specs=[SMEM, VMEM],
        out_specs=[VMEM] * 5,
        out_shape=[
            jax.ShapeDtypeStruct((TILES, 64, HALF), BF16),
            jax.ShapeDtypeStruct((TILES + 1, 1, HALF), F32),
            jax.ShapeDtypeStruct((BANDS, BT, 128), BF16),
            jax.ShapeDtypeStruct((BANDS, 64, BT), BF16),
            jax.ShapeDtypeStruct((TILES + 1, 64, HALF), BF16),
        ],
        scratch_shapes=[
            pltpu.VMEM((BANDS, 64, BT), BF16),
            pltpu.VMEM((TILES + 1, 1, HALF), F32),
            pltpu.VMEM((TILES + 1, 1, HALF), F32),
            pltpu.VMEM((TILES + 1, 64, HALF), F32),
            pltpu.VMEM((BT, 2 * HALF), F32),
            pltpu.VMEM((BT, 2 * HALF), F32),
        ],
        compiler_params=params(40),
        cost_estimate=cost(2.4e10, 2e7, 16e6),
        name="forward",
    )(plan, recv)


def backward_body(last, plan, kv, kt, qt, dot_, attn, lse, dq_in, dkv_ref, dq_ref, w1, delta, dkv, dq, a0, c0, a1, c1):
    rows = kv.shape[1]

    def prepare(x, carry):
        blank = jnp.zeros((64, HALF), BF16)
        w1[x] = jnp.concatenate(
            [jnp.concatenate([qt[x], blank], axis=1), jnp.concatenate([blank, dot_[x]], axis=1)], axis=0
        )
        delta[x] = jnp.sum(attn[x].astype(F32) * dot_[x].astype(F32), axis=0, keepdims=True)
        return carry

    lax.fori_loop(0, TILES, prepare, 0)
    w1[TILES] = jnp.zeros((128, 2 * HALF), BF16)
    delta[TILES] = jnp.zeros((1, HALF), F32)
    dkv[...] = jnp.zeros(dkv.shape, F32)
    if dq_in is None:
        dq[...] = jnp.zeros(dq.shape, F32)
    else:
        dq[...] = dq_in[...]

    def scores(i, dst_a, dst_c):
        band = kv[plan[2, i]]
        dst_a[...] = dot(band, w1[plan[0, i]])
        dst_c[...] = dot(band, w1[plan[1, i]])

    def absorb(i, src_a, src_c):
        a, c, b = plan[0, i], plan[1, i], plan[2, i]
        both = []
        for x, src in ((a, src_a), (c, src_c)):
            p = jnp.exp(src[:, :HALF] - lse[x])
            ds = p * (src[:, HALF:] - delta[x])
            both.append((ds.astype(BF16), p.astype(BF16)))
        (ds_a, p_a), (ds_c, p_c) = both
        dkv[b] += dot(
            jnp.concatenate([ds_a, p_a, ds_c, p_c], axis=1),
            jnp.concatenate([w1[a], w1[c]], axis=1),
            NT,
        )
        part = dot(kt[b], jnp.concatenate([ds_a, ds_c], axis=1))
        dq[a] += part[:, :HALF]
        dq[c] += part[:, HALF:]

    scores(0, a0, c0)

    def two(j, carry):
        scores(2 * j + 1, a1, c1)
        absorb(2 * j, a0, c0)
        scores(2 * j + 2, a0, c0)
        absorb(2 * j + 1, a1, c1)
        return carry

    lax.fori_loop(0, plan[3, 0], two, 0)

    def finish(b, carry):
        dkv_ref[b] = dkv[b].astype(BF16)
        return carry

    lax.fori_loop(0, BANDS, finish, 0)
    if last:

        def finish_q(x, carry):
            dq_ref[x] = (dq[x] * SCALE).astype(BF16)
            return carry

        lax.fori_loop(0, TILES, finish_q, 0)
    else:
        dq_ref[...] = dq[...]


def backward(chunk, plan, kv, kt, qt, dot_, attn, lse, dq_in):
    rows = BT // CHUNKS
    last = chunk == CHUNKS - 1
    first = dq_in is None
    body = functools.partial(backward_body, last)
    if first:
        inner = body

        def body(plan, kv, kt, qt, dot_, attn, lse, *rest):
            return inner(plan, kv, kt, qt, dot_, attn, lse, None, *rest)

    specs = [
        SMEM,
        pl.BlockSpec((BANDS, rows, 128), lambda i: (0, chunk, 0)),
        pl.BlockSpec((BANDS, 64, rows), lambda i: (0, 0, chunk)),
        VMEM,
        VMEM,
        VMEM,
        VMEM,
    ]
    args = [plan, kv, kt, qt, dot_, attn, lse]
    if not first:
        specs.append(VMEM)
        args.append(dq_in)
    dq_shape = (
        jax.ShapeDtypeStruct((TILES, 64, HALF), BF16)
        if last
        else jax.ShapeDtypeStruct((TILES + 1, 64, HALF), F32)
    )
    return pl.pallas_call(
        body,
        grid=(1,),
        in_specs=specs,
        out_specs=[VMEM, VMEM],
        out_shape=[jax.ShapeDtypeStruct((BANDS, rows, 128), BF16), dq_shape],
        scratch_shapes=[
            pltpu.VMEM((TILES + 1, 128, 2 * HALF), BF16),
            pltpu.VMEM((TILES + 1, 1, HALF), F32),
            pltpu.VMEM((BANDS, rows, 128), F32),
            pltpu.VMEM((TILES + 1, 64, HALF), F32),
        ]
        + [pltpu.VMEM((rows, 2 * HALF), F32)] * 4,
        compiler_params=params(40),
        cost_estimate=cost(5e10 / CHUNKS, 2e7, 16e6 / CHUNKS),
        name="backward",
    )(*args)


def project_body(recv, w_ref, g_ref, layer_ref, dw_ref, acc):
    t = pl.program_id(0)
    low = pl.multiple_of(t * 64, 64)
    heads = [
        jnp.concatenate([recv[2 * h, pl.ds(low, 64), :], recv[2 * h + 1, pl.ds(low, 64), :]], axis=1)
        for h in range(HEADS)
    ]
    attn_t = jnp.concatenate(heads, axis=0)
    layer_ref[...] = dot(attn_t.T, w_ref[...]).astype(BF16)
    term = dot(attn_t, g_ref[...])

    @pl.when(t == 0)
    def _():
        acc[...] = term

    @pl.when(t > 0)
    def _():
        acc[...] += term

    @pl.when(t == TILES_DEV - 1)
    def _():
        dw_ref[...] = acc[...].astype(BF16)


def project(recv, w, g):
    rows = TILES_DEV * QROWS
    return pl.pallas_call(
        project_body,
        grid=(TILES_DEV,),
        in_specs=[
            pl.BlockSpec((16, TILES_DEV * 64, 128), lambda t: (0, 0, 0)),
            pl.BlockSpec((HW, D), lambda t: (0, 0)),
            pl.BlockSpec((QROWS, D), lambda t: (t, 0)),
        ],
        out_specs=[
            pl.BlockSpec((QROWS, D), lambda t: (t, 0)),
            pl.BlockSpec((HW, D), lambda t: (0, 0)),
        ],
        out_shape=[jax.ShapeDtypeStruct((rows, D), BF16), jax.ShapeDtypeStruct((HW, D), BF16)],
        scratch_shapes=[pltpu.VMEM((HW, D), F32)],
        compiler_params=params(40),
        cost_estimate=cost(4 * rows * D * HW, 8e6),
        name="project",
    )(recv, w, g)


def unpack_body(*refs):
    dq_in, parts = refs[0], refs[1 : 1 + CHUNKS]
    dq_ref, dk_ref, dv_ref = refs[1 + CHUNKS :]
    heads = []
    for head in range(2):
        blocks = []
        for t in range(TILES_DEV):
            for half in range(2):
                blocks.append(dq_in[2 * head + half, t * 64 : t * 64 + 64, :])
        heads.append(jnp.concatenate(blocks, axis=1))
    dq_ref[...] = jnp.concatenate(heads, axis=0).T
    rows = BT // CHUNKS
    left = lax.broadcasted_iota(jnp.int32, (rows, 128), 1) < 64
    for chunk in range(CHUNKS):
        part = parts[chunk]
        x = part[0].astype(F32) + part[1].astype(F32)
        y = part[2].astype(F32) + part[3].astype(F32)
        at = slice(chunk * rows, chunk * rows + rows)
        dk_ref[at, :] = jnp.where(left, x, pltpu.roll(y, 64, 1)).astype(BF16)
        dv_ref[at, :] = jnp.where(left, pltpu.roll(x, 64, 1), y).astype(BF16)


def unpack(dq, parts):
    rows = TILES_DEV * QROWS
    return pl.pallas_call(
        unpack_body,
        grid=(4,),
        in_specs=[pl.BlockSpec((4, TILES_DEV * 64, 128), lambda p: (p, 0, 0))]
        + [pl.BlockSpec((4, BT // CHUNKS, 128), lambda p: (p, 0, 0))] * CHUNKS,
        out_specs=[
            pl.BlockSpec((rows, 128), lambda p: (0, p)),
            pl.BlockSpec((BT, 128), lambda p: (0, p)),
            pl.BlockSpec((BT, 128), lambda p: (0, p)),
        ],
        out_shape=[
            jax.ShapeDtypeStruct((rows, HW), BF16),
            jax.ShapeDtypeStruct((BT, HW), BF16),
            jax.ShapeDtypeStruct((BT, HW), BF16),
        ],
        compiler_params=params(24),
        cost_estimate=cost(0, 8e6),
        name="unpack",
    )(dq, *parts)


def swap(x, axes="region"):
    return lax.all_to_all(x, axes, 0, 0, tiled=True)


def per_device(devices, queries, keys, values, block_lists, band_counts, cotangent, out_weight):
    rows = TILES_DEV * QROWS
    q, g = queries.reshape(rows, HW), cotangent.reshape(rows, D)
    recv1 = swap(pack(q, keys.reshape(BT, HW), values.reshape(BT, HW)))
    recv2 = swap(dattn(out_weight, g)).reshape(TILES, 64, HALF)
    where = jnp.concatenate([block_lists[0], band_counts[0][:, None]], axis=1)
    where = lax.all_gather(where, "region", axis=0, tiled=True)
    plan = plan_of(where[:, :MAXB], where[:, MAXB])

    attn, lse, kv, kt, qt = forward(plan, recv1)
    recv3 = swap(attn.reshape(16, TILES_DEV * 64, HALF))
    dq = None
    parts = []
    for chunk in range(CHUNKS):
        part, dq = backward(chunk, plan, kv, kt, qt, recv2, attn, lse, dq)
        parts.append(swap(part))
    layer, dw = project(recv3, out_weight, g)
    dw = swap(dw.reshape(devices, HW // devices, D), ("region", "orbit"))
    dw = jnp.sum(dw.astype(F32), axis=0, keepdims=True).astype(BF16)
    dw = swap(jnp.broadcast_to(dw, (devices, HW // devices, D)), ("region", "orbit"))
    d_weight = dw.reshape(HW, D).astype(F32)
    dq = swap(dq.reshape(16, TILES_DEV * 64, HALF))
    d_q, d_k, d_v = unpack(dq, parts)
    return (
        layer.reshape(1, TILES_DEV, QROWS, D),
        d_q.reshape(1, TILES_DEV, QROWS, HW),
        d_k.reshape(1, 1, BT, HW),
        d_v.reshape(1, 1, BT, HW),
        d_weight,
    )


def solution(mesh):
    four = P("orbit", "region", None, None)
    return jax.shard_map(
        functools.partial(per_device, mesh.devices.size),
        mesh=mesh,
        in_specs=(four, four, four, P("orbit", "region", None), P("orbit", "region"), four, P()),
        out_specs=(four, four, four, four, P()),
        check_vma=False,
    )
```

```python
import jax
import jax.numpy as jnp
from jax import lax
from jax.experimental import pallas as pl
from jax.experimental.pallas import tpu as pltpu
from jax.sharding import PartitionSpec as P

HEADS = 8
HEAD_DIM = 64
BANDS = 16
BT = 512
QROWS = 256
HALF = 128
TILES_DEV = 3
TILES = 48
MAXB = 8
D = 1024
HW = 512
CHUNKS = 2
ROWS = BT // CHUNKS
QUERY_ROWS = TILES_DEV * 64
LIST_ROW = BT + QUERY_ROWS
SEND_ROWS = LIST_ROW + 16
DW_ROWS = HW * D // 16 // 128
MID_ROWS = ROWS + DW_ROWS
END_ROWS = QUERY_ROWS + ROWS + DW_ROWS
PAIRS = 208
SCALE = HEAD_DIM**-0.5
LOW = -1e30
BF16 = jnp.bfloat16
F32 = jnp.float32

NT = (((1,), (1,)), ((), ()))


def dot(a, b, dims=(((1,), (0,)), ((), ()))):
    return lax.dot_general(a, b, dims, preferred_element_type=F32)


def params(mib=56):
    return pltpu.CompilerParams(vmem_limit_bytes=mib << 20)


def cost(flops, nbytes, exps=0):
    return pl.CostEstimate(flops=int(flops), bytes_accessed=int(nbytes), transcendentals=int(exps))


def whole(*shape):
    return pl.BlockSpec(shape, lambda *_: (0,) * len(shape))


SMEM = pl.BlockSpec(memory_space=pltpu.SMEM)


def pack_body(q_ref, k_ref, v_ref, list_ref, out_ref):
    kt = k_ref[...].T
    vt = v_ref[...].T
    qt = (q_ref[...].astype(F32) * SCALE).astype(BF16).T
    for head in range(2):
        rows = slice(head * 64, head * 64 + 64)
        for half in range(2):
            dest = 2 * head + half
            out_ref[dest, LIST_ROW:SEND_ROWS, :] = list_ref[...]
            for j in range(4):
                lanes = slice(j * 128, j * 128 + 128)
                out_ref[dest, j * 128 : j * 128 + 64, :] = kt[rows, lanes]
                out_ref[dest, j * 128 + 64 : j * 128 + 128, :] = vt[rows, lanes]
            for t in range(TILES_DEV):
                low = t * QROWS + half * HALF
                out_ref[dest, BT + t * 64 : BT + t * 64 + 64, :] = qt[rows, low : low + HALF]


def pack(q, k, v, lists):
    return pl.pallas_call(
        pack_body,
        grid=(4,),
        in_specs=[
            pl.BlockSpec((TILES_DEV * QROWS, 128), lambda p: (0, p)),
            pl.BlockSpec((BT, 128), lambda p: (0, p)),
            pl.BlockSpec((BT, 128), lambda p: (0, p)),
            pl.BlockSpec((16, 128), lambda p: (0, 0)),
        ],
        out_specs=pl.BlockSpec((4, SEND_ROWS, 128), lambda p: (p, 0, 0)),
        out_shape=jax.ShapeDtypeStruct((16, SEND_ROWS, 128), BF16),
        compiler_params=params(60),
        cost_estimate=cost(0, 8e6),
        name="pack",
    )(q, k, v, lists)


def dattn_body(w_ref, g_ref, out_ref):
    dt = dot(w_ref[...], g_ref[...], NT).astype(BF16)
    for head in range(2):
        for half in range(2):
            for t in range(TILES_DEV):
                low = t * QROWS + half * HALF
                out_ref[2 * head + half, t * 64 : t * 64 + 64, :] = dt[
                    head * 64 : head * 64 + 64, low : low + HALF
                ]


def dattn(w, g):
    rows = TILES_DEV * QROWS
    return pl.pallas_call(
        dattn_body,
        grid=(4,),
        in_specs=[
            pl.BlockSpec((128, D), lambda p: (p, 0)),
            pl.BlockSpec((rows, D), lambda p: (0, 0)),
        ],
        out_specs=pl.BlockSpec((4, TILES_DEV * 64, 128), lambda p: (p, 0, 0)),
        out_shape=jax.ShapeDtypeStruct((16, TILES_DEV * 64, 128), BF16),
        compiler_params=params(60),
        cost_estimate=cost(2 * rows * D * HW, 4e6),
        name="dattn",
    )(w, g)


def plan_of(lists, counts):
    slots = jnp.arange(MAXB)[None, :] < counts[:, None]
    member = (
        (lists[:, :, None] == jnp.arange(BANDS)[None, None, :]) & slots[:, :, None]
    ).any(axis=1)
    member = member.T.astype(jnp.int32)
    place = jnp.cumsum(member, axis=1) - member
    size = (member.sum(axis=1) + 1) // 2
    base = jnp.cumsum(size) - size
    flat = jnp.where(member > 0, 2 * base[:, None] + place, -1)
    hit = flat[None] == jnp.arange(2 * PAIRS)[:, None, None]
    tile = jnp.arange(TILES)[None, None, :]
    band = jnp.arange(BANDS)[None, :, None]
    code = jnp.sum(jnp.where(hit, band * 64 + tile + 1, 0), axis=(1, 2)).reshape(PAIRS, 2)
    who = jnp.where(code > 0, (code & 63) - 1, TILES)
    number = (size.sum() + 1) // 2
    return jnp.stack(
        [who[:, 0], who[:, 1], code[:, 0] >> 6, jnp.full((PAIRS,), number, jnp.int32)]
    ).astype(jnp.int32)


def forward_body(plan, recv, attn_ref, lse_ref, kv_ref, kt_ref, qt_ref, vt, top, total, acc, s0, s1):
    def unpack_band(b, carry):
        kvt = jnp.concatenate([recv[b, j * 128 : j * 128 + 128, :] for j in range(4)], axis=1)
        kv_ref[b] = kvt.T
        kt_ref[b] = kvt[:64]
        vt[b] = kvt[64:]
        for t in range(TILES_DEV):
            qt_ref[b * TILES_DEV + t] = recv[b, BT + t * 64 : BT + t * 64 + 64, :]
        return carry

    lax.fori_loop(0, BANDS, unpack_band, 0)
    qt_ref[TILES] = jnp.zeros((64, HALF), BF16)
    top[...] = jnp.full(top.shape, LOW, F32)
    total[...] = jnp.zeros(total.shape, F32)
    acc[...] = jnp.zeros(acc.shape, F32)
    blank = jnp.zeros((64, 2 * HALF), BF16)

    def scores(i, dst):
        w = jnp.concatenate([qt_ref[plan[0, i]], qt_ref[plan[1, i]]], axis=1)
        dst[...] = dot(kv_ref[plan[2, i]], jnp.concatenate([w, blank], axis=0))

    def absorb(i, src):
        a, c, b = plan[0, i], plan[1, i], plan[2, i]
        old = jnp.concatenate([top[a], top[c]], axis=1)
        new = jnp.maximum(old, jnp.max(src[...], axis=0, keepdims=True))
        fade = jnp.exp(old - new)
        p = jnp.exp(src[...] - new)
        part = jnp.sum(p, axis=0, keepdims=True)
        o = dot(vt[b], p.astype(BF16))
        for x, lanes in ((a, slice(0, HALF)), (c, slice(HALF, 2 * HALF))):
            top[x] = new[:, lanes]
            total[x] = total[x] * fade[:, lanes] + part[:, lanes]
            acc[x] = acc[x] * fade[:, lanes] + o[:, lanes]

    scores(0, s0)

    def two(j, carry):
        scores(2 * j + 1, s1)
        absorb(2 * j, s0)
        scores(2 * j + 2, s0)
        absorb(2 * j + 1, s1)
        return carry

    lax.fori_loop(0, plan[3, 0], two, 0)

    def finish(x, carry):
        attn_ref[x] = (acc[x] / total[x]).astype(BF16)
        lse_ref[x] = top[x] + jnp.log(total[x])
        return carry

    lax.fori_loop(0, TILES, finish, 0)
    lse_ref[TILES] = jnp.full((1, HALF), -LOW, F32)


def forward(plan, recv):
    return pl.pallas_call(
        forward_body,
        grid=(1,),
        in_specs=[SMEM, whole(16, SEND_ROWS, 128)],
        out_specs=[
            whole(TILES, 64, HALF),
            whole(TILES + 1, 1, HALF),
            whole(BANDS, BT, 128),
            whole(BANDS, 64, BT),
            whole(TILES + 1, 64, HALF),
        ],
        out_shape=[
            jax.ShapeDtypeStruct((TILES, 64, HALF), BF16),
            jax.ShapeDtypeStruct((TILES + 1, 1, HALF), F32),
            jax.ShapeDtypeStruct((BANDS, BT, 128), BF16),
            jax.ShapeDtypeStruct((BANDS, 64, BT), BF16),
            jax.ShapeDtypeStruct((TILES + 1, 64, HALF), BF16),
        ],
        scratch_shapes=[
            pltpu.VMEM((BANDS, 64, BT), BF16),
            pltpu.VMEM((TILES + 1, 1, HALF), F32),
            pltpu.VMEM((TILES + 1, 1, HALF), F32),
            pltpu.VMEM((TILES + 1, 64, HALF), F32),
            pltpu.VMEM((BT, 2 * HALF), F32),
            pltpu.VMEM((BT, 2 * HALF), F32),
        ],
        compiler_params=params(60),
        cost_estimate=cost(2.4e10, 2e7, 16e6),
        name="forward",
    )(plan, recv)


def backward_body(last, plan, kv, kt, qt, dot_, attn, lse, dq_in, send_ref, dq_ref, w1, delta, dkv, dq, a0, c0, a1, c1):
    rows = kv.shape[1]

    def prepare(x, carry):
        blank = jnp.zeros((64, HALF), BF16)
        w1[x] = jnp.concatenate(
            [jnp.concatenate([qt[x], blank], axis=1), jnp.concatenate([blank, dot_[x]], axis=1)], axis=0
        )
        delta[x] = jnp.sum(attn[x].astype(F32) * dot_[x].astype(F32), axis=0, keepdims=True)
        return carry

    lax.fori_loop(0, TILES, prepare, 0)
    w1[TILES] = jnp.zeros((128, 2 * HALF), BF16)
    delta[TILES] = jnp.zeros((1, HALF), F32)
    dkv[...] = jnp.zeros(dkv.shape, F32)
    if dq_in is None:
        dq[...] = jnp.zeros(dq.shape, F32)
    else:
        dq[...] = dq_in[...]

    def scores(i, dst_a, dst_c):
        band = kv[plan[2, i]]
        dst_a[...] = dot(band, w1[plan[0, i]])
        dst_c[...] = dot(band, w1[plan[1, i]])

    def absorb(i, src_a, src_c):
        a, c, b = plan[0, i], plan[1, i], plan[2, i]
        both = []
        for x, src in ((a, src_a), (c, src_c)):
            p = jnp.exp(src[:, :HALF] - lse[x])
            ds = p * (src[:, HALF:] - delta[x])
            both.append((ds.astype(BF16), p.astype(BF16)))
        (ds_a, p_a), (ds_c, p_c) = both
        dkv[b] += dot(
            jnp.concatenate([ds_a, p_a, ds_c, p_c], axis=1),
            jnp.concatenate([w1[a], w1[c]], axis=1),
            NT,
        )
        part = dot(kt[b], jnp.concatenate([ds_a, ds_c], axis=1))
        dq[a] += part[:, :HALF]
        dq[c] += part[:, HALF:]

    scores(0, a0, c0)

    def two(j, carry):
        scores(2 * j + 1, a1, c1)
        absorb(2 * j, a0, c0)
        scores(2 * j + 2, a0, c0)
        absorb(2 * j + 1, a1, c1)
        return carry

    lax.fori_loop(0, plan[3, 0], two, 0)

    first = QUERY_ROWS if last else 0

    def finish(b, carry):
        send_ref[b, first : first + rows, :] = dkv[b].astype(BF16)
        if last:
            for t in range(TILES_DEV):
                send_ref[b, t * 64 : t * 64 + 64, :] = (dq[b * TILES_DEV + t] * SCALE).astype(BF16)
        return carry

    lax.fori_loop(0, BANDS, finish, 0)
    if not last:
        dq_ref[...] = dq[...]


def backward(chunk, plan, kv, kt, qt, dot_, attn, lse, dq_in=None):
    last = chunk == CHUNKS - 1
    if last:

        def body(*refs):
            return backward_body(True, *refs[:9], None, *refs[9:])
    else:

        def body(*refs):
            return backward_body(False, *refs[:7], None, *refs[7:])

    specs = [
        SMEM,
        pl.BlockSpec((BANDS, ROWS, 128), lambda i: (0, chunk, 0)),
        pl.BlockSpec((BANDS, 64, ROWS), lambda i: (0, 0, chunk)),
        whole(TILES + 1, 64, HALF),
        whole(TILES, 64, HALF),
        whole(TILES, 64, HALF),
        whole(TILES + 1, 1, HALF),
    ]
    args = [plan, kv, kt, qt, dot_, attn, lse]
    if last:
        specs.append(whole(TILES + 1, 64, HALF))
        args.append(dq_in)
        out_specs = [whole(BANDS, QUERY_ROWS + ROWS, 128)]
        out_shape = [jax.ShapeDtypeStruct((BANDS, END_ROWS, 128), BF16)]
    else:
        out_specs = [whole(BANDS, ROWS, 128), whole(TILES + 1, 64, HALF)]
        out_shape = [
            jax.ShapeDtypeStruct((BANDS, MID_ROWS, 128), BF16),
            jax.ShapeDtypeStruct((TILES + 1, 64, HALF), F32),
        ]
    return pl.pallas_call(
        body,
        grid=(1,),
        in_specs=specs,
        out_specs=out_specs,
        out_shape=out_shape,
        scratch_shapes=[
            pltpu.VMEM((TILES + 1, 128, 2 * HALF), BF16),
            pltpu.VMEM((TILES + 1, 1, HALF), F32),
            pltpu.VMEM((BANDS, ROWS, 128), F32),
            pltpu.VMEM((TILES + 1, 64, HALF), F32),
        ]
        + [pltpu.VMEM((ROWS, 2 * HALF), F32)] * 4,
        compiler_params=params(60),
        cost_estimate=cost(5e10 / CHUNKS, 2e7, 16e6 / CHUNKS),
        name="backward",
    )(*args)


def project_body(recv, w_ref, g_ref, unused, layer_ref, send_ref, acc):
    t = pl.program_id(0)
    low = pl.multiple_of(t * 64, 64)
    heads = [
        jnp.concatenate([recv[2 * h, pl.ds(low, 64), :], recv[2 * h + 1, pl.ds(low, 64), :]], axis=1)
        for h in range(HEADS)
    ]
    attn_t = jnp.concatenate(heads, axis=0)
    layer_ref[...] = dot(attn_t.T, w_ref[...]).astype(BF16)
    term = dot(attn_t, g_ref[...])

    @pl.when(t == 0)
    def _():
        acc[...] = term

    @pl.when(t > 0)
    def _():
        acc[...] += term

    @pl.when(t == TILES_DEV - 1)
    def _():
        wide = D // 128
        for dest in range(16):
            for j in range(wide):
                send_ref[dest, j * 32 : j * 32 + 32, :] = acc[
                    dest * 32 : dest * 32 + 32, j * 128 : j * 128 + 128
                ].astype(BF16)


def project(recv, w, g, send):
    rows = TILES_DEV * QROWS
    return pl.pallas_call(
        project_body,
        grid=(TILES_DEV,),
        in_specs=[
            pl.BlockSpec((16, TILES_DEV * 64, 128), lambda t: (0, 0, 0)),
            pl.BlockSpec((HW, D), lambda t: (0, 0)),
            pl.BlockSpec((QROWS, D), lambda t: (t, 0)),
            pl.BlockSpec(memory_space=pl.ANY),
        ],
        out_specs=[
            pl.BlockSpec((QROWS, D), lambda t: (t, 0)),
            pl.BlockSpec((16, DW_ROWS, 128), lambda t: (0, ROWS // DW_ROWS, 0)),
        ],
        out_shape=[
            jax.ShapeDtypeStruct((rows, D), BF16),
            jax.ShapeDtypeStruct((BANDS, MID_ROWS, 128), BF16),
        ],
        input_output_aliases={3: 1},
        scratch_shapes=[pltpu.VMEM((HW, D), F32)],
        compiler_params=params(60),
        cost_estimate=cost(4 * rows * D * HW, 8e6),
        name="project",
    )(recv, w, g, send)


def spread_body(part_ref, unused, send_ref):
    total = jnp.sum(part_ref[...].astype(F32), axis=0).astype(BF16)
    for dest in range(16):
        send_ref[dest] = total


def spread(part, send):
    return pl.pallas_call(
        spread_body,
        grid=(DW_ROWS // 64,),
        in_specs=[
            pl.BlockSpec((part.shape[0], 64, 128), lambda i: (0, i, 0)),
            pl.BlockSpec(memory_space=pl.ANY),
        ],
        out_specs=pl.BlockSpec((16, 64, 128), lambda i: (0, (END_ROWS - DW_ROWS) // 64 + i, 0)),
        out_shape=jax.ShapeDtypeStruct((BANDS, END_ROWS, 128), BF16),
        input_output_aliases={1: 0},
        compiler_params=params(60),
        cost_estimate=cost(0, 2e6),
        name="spread",
    )(part, send)


def unpack_body(mid, end, dq_ref, dk_ref, dv_ref, dw_ref):
    heads = []
    for head in range(2):
        blocks = []
        for t in range(TILES_DEV):
            for half in range(2):
                blocks.append(end[2 * head + half, t * 64 : t * 64 + 64, :])
        heads.append(jnp.concatenate(blocks, axis=1))
    dq_ref[...] = jnp.concatenate(heads, axis=0).T
    left = lax.broadcasted_iota(jnp.int32, (ROWS, 128), 1) < 64
    for chunk, part, low in ((0, mid, 0), (1, end, QUERY_ROWS)):
        take = [part[r, low : low + ROWS, :].astype(F32) for r in range(4)]
        x, y = take[0] + take[1], take[2] + take[3]
        at = slice(chunk * ROWS, chunk * ROWS + ROWS)
        dk_ref[at, :] = jnp.where(left, x, pltpu.roll(y, 64, 1)).astype(BF16)
        dv_ref[at, :] = jnp.where(left, pltpu.roll(x, 64, 1), y).astype(BF16)
    for r in range(4):
        for j in range(D // 128):
            at = END_ROWS - DW_ROWS + j * 32
            dw_ref[r * 32 : r * 32 + 32, j * 128 : j * 128 + 128] = end[r, at : at + 32, :].astype(F32)


def unpack(mid, end):
    rows = TILES_DEV * QROWS
    return pl.pallas_call(
        unpack_body,
        grid=(4,),
        in_specs=[
            pl.BlockSpec((4, ROWS, 128), lambda p: (p, 0, 0)),
            pl.BlockSpec((4, END_ROWS, 128), lambda p: (p, 0, 0)),
        ],
        out_specs=[
            pl.BlockSpec((rows, 128), lambda p: (0, p)),
            pl.BlockSpec((BT, 128), lambda p: (0, p)),
            pl.BlockSpec((BT, 128), lambda p: (0, p)),
            pl.BlockSpec((128, D), lambda p: (p, 0)),
        ],
        out_shape=[
            jax.ShapeDtypeStruct((rows, HW), BF16),
            jax.ShapeDtypeStruct((BT, HW), BF16),
            jax.ShapeDtypeStruct((BT, HW), BF16),
            jax.ShapeDtypeStruct((HW, D), F32),
        ],
        compiler_params=params(60),
        cost_estimate=cost(0, 8e6),
        name="unpack",
    )(mid, end)


def swap(x, axes="region"):
    return lax.all_to_all(x, axes, 0, 0, tiled=True)


def per_device(queries, keys, values, block_lists, band_counts, cotangent, out_weight):
    rows = TILES_DEV * QROWS
    q, g = queries.reshape(rows, HW), cotangent.reshape(rows, D)
    lists = jnp.concatenate([block_lists[0], band_counts[0][:, None]], axis=1).astype(BF16)
    lists = lists.reshape(1, -1)
    lists = jnp.pad(lists, ((0, 15), (0, 128 - lists.shape[1])))
    recv = swap(pack(q, keys.reshape(BT, HW), values.reshape(BT, HW), lists))
    lists = recv[:, LIST_ROW, : TILES_DEV * (MAXB + 1)].astype(jnp.int32).reshape(TILES, MAXB + 1)
    plan = plan_of(lists[:, :MAXB], lists[:, MAXB])
    d_attn = dattn(out_weight, g)
    recv, d_attn = lax.optimization_barrier((recv, d_attn))
    d_attn = swap(d_attn).reshape(TILES, 64, HALF)

    attn, lse, kv, kt, qt = forward(plan, recv)
    attn_home = swap(attn.reshape(16, QUERY_ROWS, HALF))
    mid, dq = backward(0, plan, kv, kt, qt, d_attn, attn, lse)
    attn_home, mid = lax.optimization_barrier((attn_home, mid))
    layer, mid = project(attn_home, out_weight, g, mid)
    mid, dq = lax.optimization_barrier((mid, dq))
    mid = swap(mid)
    (end,) = backward(1, plan, kv, kt, qt, d_attn, attn, lse, dq)
    mid, end = lax.optimization_barrier((mid, end))
    share = jnp.sum(mid[:, ROWS:].astype(F32), axis=0, keepdims=True).astype(BF16)
    orbits = lax.axis_size("orbit")
    share = swap(jnp.broadcast_to(share, (orbits, DW_ROWS, 128)), "orbit")
    end = swap(spread(share, end))
    d_q, d_k, d_v, d_weight = unpack(mid, end)
    return (
        layer.reshape(1, TILES_DEV, QROWS, D),
        d_q.reshape(1, TILES_DEV, QROWS, HW),
        d_k.reshape(1, 1, BT, HW),
        d_v.reshape(1, 1, BT, HW),
        d_weight,
    )


def solution(mesh):
    four = P("orbit", "region", None, None)
    return jax.shard_map(
        per_device,
        mesh=mesh,
        in_specs=(four, four, four, P("orbit", "region", None), P("orbit", "region"), four, P()),
        out_specs=(four, four, four, four, P()),
        check_vma=False,
    )
```

```python
import functools

import jax
import jax.numpy as jnp
from jax import lax
from jax.experimental import pallas as pl
from jax.experimental.pallas import tpu as pltpu
from jax.sharding import PartitionSpec as P

HEADS = 8
HEAD_DIM = 64
BANDS = 16
BT = 512
QROWS = 256
HALF = 128
TILES_DEV = 3
TILES = 48
MAXB = 8
D = 1024
HW = 512
CHUNKS = 2
UNROLL = 8
BACK_UNROLL = 8
SUB = 64
BACK_SUB = 256
SUM_ROWS = 16
ROWS = BT // CHUNKS
QUERY_ROWS = TILES_DEV * 64
LIST_ROW = BT + QUERY_ROWS
SEND_ROWS = LIST_ROW + 16
DW_ROWS = HW * D // 16 // 128
MID_ROWS = ROWS + DW_ROWS
END_ROWS = QUERY_ROWS + ROWS + DW_ROWS
PAIRS = 208
SCALE = HEAD_DIM**-0.5
LOW = -1e30
BF16 = jnp.bfloat16
F32 = jnp.float32

NT = (((1,), (1,)), ((), ()))


def dot(a, b, dims=(((1,), (0,)), ((), ()))):
    return lax.dot_general(a, b, dims, preferred_element_type=F32)


def params(mib=56):
    return pltpu.CompilerParams(vmem_limit_bytes=mib << 20)


def cost(flops, nbytes, exps=0):
    return pl.CostEstimate(flops=int(flops), bytes_accessed=int(nbytes), transcendentals=int(exps))


def whole(*shape):
    return pl.BlockSpec(shape, lambda *_: (0,) * len(shape))


SMEM = pl.BlockSpec(memory_space=pltpu.SMEM)


def pack_body(q_ref, k_ref, v_ref, list_ref, out_ref):
    kt = k_ref[...].T
    vt = v_ref[...].T
    qt = (q_ref[...].astype(F32) * SCALE).astype(BF16).T
    for head in range(2):
        rows = slice(head * 64, head * 64 + 64)
        for half in range(2):
            dest = 2 * head + half
            out_ref[dest, LIST_ROW:SEND_ROWS, :] = list_ref[...]
            for j in range(4):
                lanes = slice(j * 128, j * 128 + 128)
                out_ref[dest, j * 128 : j * 128 + 64, :] = kt[rows, lanes]
                out_ref[dest, j * 128 + 64 : j * 128 + 128, :] = vt[rows, lanes]
            for t in range(TILES_DEV):
                low = t * QROWS + half * HALF
                out_ref[dest, BT + t * 64 : BT + t * 64 + 64, :] = qt[rows, low : low + HALF]


def pack(q, k, v, lists):
    return pl.pallas_call(
        pack_body,
        grid=(4,),
        in_specs=[
            pl.BlockSpec((TILES_DEV * QROWS, 128), lambda p: (0, p)),
            pl.BlockSpec((BT, 128), lambda p: (0, p)),
            pl.BlockSpec((BT, 128), lambda p: (0, p)),
            pl.BlockSpec((16, 128), lambda p: (0, 0)),
        ],
        out_specs=pl.BlockSpec((4, SEND_ROWS, 128), lambda p: (p, 0, 0)),
        out_shape=jax.ShapeDtypeStruct((16, SEND_ROWS, 128), BF16),
        compiler_params=params(60),
        cost_estimate=cost(0, 8e6),
        name="pack",
    )(q, k, v, lists)


def dattn_body(w_ref, g_ref, out_ref):
    dt = dot(w_ref[...], g_ref[...], NT).astype(BF16)
    for head in range(2):
        for half in range(2):
            for t in range(TILES_DEV):
                low = t * QROWS + half * HALF
                out_ref[2 * head + half, t * 64 : t * 64 + 64, :] = dt[
                    head * 64 : head * 64 + 64, low : low + HALF
                ]


def dattn(w, g):
    rows = TILES_DEV * QROWS
    return pl.pallas_call(
        dattn_body,
        grid=(4,),
        in_specs=[
            pl.BlockSpec((128, D), lambda p: (p, 0)),
            pl.BlockSpec((rows, D), lambda p: (0, 0)),
        ],
        out_specs=pl.BlockSpec((4, TILES_DEV * 64, 128), lambda p: (p, 0, 0)),
        out_shape=jax.ShapeDtypeStruct((16, TILES_DEV * 64, 128), BF16),
        compiler_params=params(60),
        cost_estimate=cost(2 * rows * D * HW, 4e6),
        name="dattn",
    )(w, g)


def plan_of(lists, counts):
    slots = jnp.arange(MAXB)[None, :] < counts[:, None]
    member = (
        (lists[:, :, None] == jnp.arange(BANDS)[None, None, :]) & slots[:, :, None]
    ).any(axis=1)
    member = member.T.astype(jnp.int32)
    place = jnp.cumsum(member, axis=1) - member
    size = (member.sum(axis=1) + 1) // 2
    base = jnp.cumsum(size) - size
    flat = jnp.where(member > 0, 2 * base[:, None] + place, -1)
    hit = flat[None] == jnp.arange(2 * PAIRS)[:, None, None]
    tile = jnp.arange(TILES)[None, None, :]
    band = jnp.arange(BANDS)[None, :, None]
    code = jnp.sum(jnp.where(hit, band * 64 + tile + 1, 0), axis=(1, 2)).reshape(PAIRS, 2)
    who = jnp.where(code > 0, (code & 63) - 1, TILES)
    number = size.sum()
    return jnp.stack(
        [who[:, 0], who[:, 1], code[:, 0] >> 6, jnp.full((PAIRS,), number, jnp.int32)]
    ).astype(jnp.int32)


def forward_body(plan, recv, attn_ref, lse_ref, kv_ref, kt_ref, qt_ref, vt, top, acc, s0, s1, p0, p1, h0, h1):
    def unpack_band(b, carry):
        kvt = jnp.concatenate([recv[b, j * 128 : j * 128 + 128, :] for j in range(4)], axis=1)
        kv_ref[b] = kvt.T
        kt_ref[b] = kvt[:64]
        vt[b] = jnp.concatenate([kvt[64:], jnp.ones((SUM_ROWS, BT), BF16)], axis=0)
        for t in range(TILES_DEV):
            qt_ref[b * TILES_DEV + t] = recv[b, BT + t * 64 : BT + t * 64 + 64, :]
        return carry

    lax.fori_loop(0, BANDS, unpack_band, 0)
    qt_ref[TILES] = jnp.zeros((64, HALF), BF16)
    top[...] = jnp.full(top.shape, LOW, F32)
    acc[...] = jnp.zeros(acc.shape, F32)
    blank = jnp.zeros((64, 2 * HALF), BF16)

    def scores(i, s, h, weigh=None):
        a, c = plan[0, i], plan[1, i]
        w = jnp.concatenate([jnp.concatenate([qt_ref[a], qt_ref[c]], axis=1), blank], axis=0)
        peak = None
        for low in range(0, BT, SUB):
            rows = slice(low, low + SUB)
            st = dot(kv_ref[plan[2, i], rows, :], w)
            s[rows, :] = st
            high = jnp.max(st.reshape(SUB // 8, 8, 2 * HALF), axis=0)
            peak = high if peak is None else jnp.maximum(peak, high)
            if weigh is not None:
                weigh(rows)
        old = jnp.concatenate([top[a], top[c]], axis=1)
        new = jnp.maximum(old, jnp.max(peak, axis=0, keepdims=True))
        top[a] = new[:, :HALF]
        top[c] = new[:, HALF:]
        h[0:1, :] = new
        h[1:2, :] = jnp.exp(old - new)

    def weigh(s, h, p, rows):
        p[rows, :] = jnp.exp(s[rows, :] - h[0:1, :]).astype(BF16)

    def gather(i, fade, p):
        o = dot(vt[plan[2, i]], p[...])
        for x, lanes in ((plan[0, i], slice(0, HALF)), (plan[1, i], slice(HALF, 2 * HALF))):
            acc[x] = acc[x] * fade[:, lanes] + o[:, lanes]

    scores(0, s0, h0)
    scores(1, s1, h1)
    weigh(s0, h0, p0, slice(0, BT))

    even, odd = (s0, h0, p0), (s1, h1, p1)

    def step(j, carry):
        for k in range(UNROLL):
            i = UNROLL * j + k
            (s, h, p), (s_next, h_next, p_next) = (even, odd) if k % 2 == 0 else (odd, even)
            fade = h[1:2, :]
            scores(i + 2, s, h, functools.partial(weigh, s_next, h_next, p_next))
            gather(i, fade, p)
        return carry

    lax.fori_loop(0, (plan[3, 0] + UNROLL - 1) // UNROLL, step, 0)

    def finish(x, carry):
        total = acc[x, 64:65, :]
        attn_ref[x] = (acc[x, :64, :] / total).astype(BF16)
        lse_ref[x] = top[x] + jnp.log(total)
        return carry

    lax.fori_loop(0, TILES, finish, 0)
    lse_ref[TILES] = jnp.full((1, HALF), -LOW, F32)


def forward(plan, recv):
    return pl.pallas_call(
        forward_body,
        grid=(1,),
        in_specs=[SMEM, whole(16, SEND_ROWS, 128)],
        out_specs=[
            whole(TILES, 64, HALF),
            whole(TILES + 1, 1, HALF),
            whole(BANDS, BT, 128),
            whole(BANDS, 64, BT),
            whole(TILES + 1, 64, HALF),
        ],
        out_shape=[
            jax.ShapeDtypeStruct((TILES, 64, HALF), BF16),
            jax.ShapeDtypeStruct((TILES + 1, 1, HALF), F32),
            jax.ShapeDtypeStruct((BANDS, BT, 128), BF16),
            jax.ShapeDtypeStruct((BANDS, 64, BT), BF16),
            jax.ShapeDtypeStruct((TILES + 1, 64, HALF), BF16),
        ],
        scratch_shapes=[
            pltpu.VMEM((BANDS, 64 + SUM_ROWS, BT), BF16),
            pltpu.VMEM((TILES + 1, 1, HALF), F32),
            pltpu.VMEM((TILES + 1, 64 + SUM_ROWS, HALF), F32),
            pltpu.VMEM((BT, 2 * HALF), F32),
            pltpu.VMEM((BT, 2 * HALF), F32),
            pltpu.VMEM((BT, 2 * HALF), BF16),
            pltpu.VMEM((BT, 2 * HALF), BF16),
            pltpu.VMEM((8, 2 * HALF), F32),
            pltpu.VMEM((8, 2 * HALF), F32),
        ],
        compiler_params=params(60),
        cost_estimate=cost(2.4e10, 2e7, 16e6),
        name="forward",
    )(plan, recv)


def backward_body(last, plan, kv, kt, qt, dot_, attn, lse, dq_in, send_ref, dq_ref, gt, delta, dkv, dq, s0, t0, s1, t1, p0, d0, p1, d1):
    rows = kv.shape[1]

    def prepare(x, carry):
        gt[x] = dot_[x]
        delta[x] = jnp.sum(attn[x].astype(F32) * dot_[x].astype(F32), axis=0, keepdims=True)
        return carry

    lax.fori_loop(0, TILES, prepare, 0)
    gt[TILES] = jnp.zeros((64, HALF), BF16)
    delta[TILES] = jnp.zeros((1, HALF), F32)
    dkv[...] = jnp.zeros(dkv.shape, F32)
    if dq_in is None:
        dq[...] = jnp.zeros(dq.shape, F32)
    else:
        dq[...] = dq_in[...]
    blank = jnp.zeros((64, 2 * HALF), BF16)

    def pair(ref, i):
        return jnp.concatenate([ref[plan[0, i]], ref[plan[1, i]]], axis=1)

    def scores(i, s, t, weigh=None):
        wq = jnp.concatenate([pair(qt, i), blank], axis=0)
        wg = jnp.concatenate([blank, pair(gt, i)], axis=0)
        for low in range(0, rows, BACK_SUB):
            at = slice(low, low + BACK_SUB)
            band = kv[plan[2, i], at, :]
            s[at, :] = dot(band, wq)
            t[at, :] = dot(band, wg)
            if weigh is not None:
                weigh(at)

    def weigh(i, s, t, p_ref, d_ref, at):
        p = jnp.exp(s[at, :] - pair(lse, i))
        p_ref[at, :] = p.astype(BF16)
        d_ref[at, :] = (p * (t[at, :] - pair(delta, i))).astype(BF16)

    def gather(i, p_ref, d_ref):
        a, c, b = plan[0, i], plan[1, i], plan[2, i]
        part = dot(kt[b], d_ref[...])
        dq[a] += part[:, :HALF]
        dq[c] += part[:, HALF:]
        dkv[b, :64, :] += dot(pair(qt, i), d_ref[...], NT)
        dkv[b, 64:, :] += dot(pair(gt, i), p_ref[...], NT)

    scores(0, s0, t0)
    scores(1, s1, t1)
    weigh(0, s0, t0, p0, d0, slice(0, rows))

    even, odd = (s0, t0, p0, d0), (s1, t1, p1, d1)

    def step(j, carry):
        for k in range(BACK_UNROLL):
            i = BACK_UNROLL * j + k
            now, later = (even, odd) if k % 2 == 0 else (odd, even)
            scores(i + 2, *now[:2], functools.partial(weigh, i + 1, *later))
            gather(i, *now[2:])
        return carry

    lax.fori_loop(0, (plan[3, 0] + BACK_UNROLL - 1) // BACK_UNROLL, step, 0)

    first = QUERY_ROWS if last else 0

    def finish(b, carry):
        for j in range(rows // 128):
            at = first + j * 128
            send_ref[b, at : at + 128, :] = dkv[b, :, j * 128 : j * 128 + 128].astype(BF16)
        if last:
            for t in range(TILES_DEV):
                send_ref[b, t * 64 : t * 64 + 64, :] = (dq[b * TILES_DEV + t] * SCALE).astype(BF16)
        return carry

    lax.fori_loop(0, BANDS, finish, 0)
    if not last:
        dq_ref[...] = dq[...]


def backward(chunk, plan, kv, kt, qt, dot_, attn, lse, dq_in=None):
    last = chunk == CHUNKS - 1
    if last:

        def body(*refs):
            return backward_body(True, *refs[:9], None, *refs[9:])
    else:

        def body(*refs):
            return backward_body(False, *refs[:7], None, *refs[7:])

    specs = [
        SMEM,
        pl.BlockSpec((BANDS, ROWS, 128), lambda i: (0, chunk, 0)),
        pl.BlockSpec((BANDS, 64, ROWS), lambda i: (0, 0, chunk)),
        whole(TILES + 1, 64, HALF),
        whole(TILES, 64, HALF),
        whole(TILES, 64, HALF),
        whole(TILES + 1, 1, HALF),
    ]
    args = [plan, kv, kt, qt, dot_, attn, lse]
    if last:
        specs.append(whole(TILES + 1, 64, HALF))
        args.append(dq_in)
        out_specs = [whole(BANDS, QUERY_ROWS + ROWS, 128)]
        out_shape = [jax.ShapeDtypeStruct((BANDS, END_ROWS, 128), BF16)]
    else:
        out_specs = [whole(BANDS, ROWS, 128), whole(TILES + 1, 64, HALF)]
        out_shape = [
            jax.ShapeDtypeStruct((BANDS, MID_ROWS, 128), BF16),
            jax.ShapeDtypeStruct((TILES + 1, 64, HALF), F32),
        ]
    return pl.pallas_call(
        body,
        grid=(1,),
        in_specs=specs,
        out_specs=out_specs,
        out_shape=out_shape,
        scratch_shapes=[
            pltpu.VMEM((TILES + 1, 64, HALF), BF16),
            pltpu.VMEM((TILES + 1, 1, HALF), F32),
            pltpu.VMEM((BANDS, 128, ROWS), F32),
            pltpu.VMEM((TILES + 1, 64, HALF), F32),
        ]
        + [pltpu.VMEM((ROWS, 2 * HALF), F32)] * 4
        + [pltpu.VMEM((ROWS, 2 * HALF), BF16)] * 4,
        compiler_params=params(60),
        cost_estimate=cost(5e10 / CHUNKS, 2e7, 16e6 / CHUNKS),
        name="backward",
    )(*args)


def project_body(recv, w_ref, g_ref, unused, layer_ref, send_ref, acc):
    t = pl.program_id(0)
    low = pl.multiple_of(t * 64, 64)
    heads = [
        jnp.concatenate([recv[2 * h, pl.ds(low, 64), :], recv[2 * h + 1, pl.ds(low, 64), :]], axis=1)
        for h in range(HEADS)
    ]
    attn_t = jnp.concatenate(heads, axis=0)
    layer_ref[...] = dot(attn_t.T, w_ref[...]).astype(BF16)
    term = dot(attn_t, g_ref[...])

    @pl.when(t == 0)
    def _():
        acc[...] = term

    @pl.when(t > 0)
    def _():
        acc[...] += term

    @pl.when(t == TILES_DEV - 1)
    def _():
        wide = D // 128
        for dest in range(16):
            for j in range(wide):
                send_ref[dest, j * 32 : j * 32 + 32, :] = acc[
                    dest * 32 : dest * 32 + 32, j * 128 : j * 128 + 128
                ].astype(BF16)


def project(recv, w, g, send):
    rows = TILES_DEV * QROWS
    return pl.pallas_call(
        project_body,
        grid=(TILES_DEV,),
        in_specs=[
            pl.BlockSpec((16, TILES_DEV * 64, 128), lambda t: (0, 0, 0)),
            pl.BlockSpec((HW, D), lambda t: (0, 0)),
            pl.BlockSpec((QROWS, D), lambda t: (t, 0)),
            pl.BlockSpec(memory_space=pl.ANY),
        ],
        out_specs=[
            pl.BlockSpec((QROWS, D), lambda t: (t, 0)),
            pl.BlockSpec((16, DW_ROWS, 128), lambda t: (0, ROWS // DW_ROWS, 0)),
        ],
        out_shape=[
            jax.ShapeDtypeStruct((rows, D), BF16),
            jax.ShapeDtypeStruct((BANDS, MID_ROWS, 128), BF16),
        ],
        input_output_aliases={3: 1},
        scratch_shapes=[pltpu.VMEM((HW, D), F32)],
        compiler_params=params(60),
        cost_estimate=cost(4 * rows * D * HW, 8e6),
        name="project",
    )(recv, w, g, send)


def spread_body(part_ref, unused, send_ref):
    total = jnp.sum(part_ref[...].astype(F32), axis=0).astype(BF16)
    for dest in range(16):
        send_ref[dest] = total


def spread(part, send):
    return pl.pallas_call(
        spread_body,
        grid=(DW_ROWS // 64,),
        in_specs=[
            pl.BlockSpec((part.shape[0], 64, 128), lambda i: (0, i, 0)),
            pl.BlockSpec(memory_space=pl.ANY),
        ],
        out_specs=pl.BlockSpec((16, 64, 128), lambda i: (0, (END_ROWS - DW_ROWS) // 64 + i, 0)),
        out_shape=jax.ShapeDtypeStruct((BANDS, END_ROWS, 128), BF16),
        input_output_aliases={1: 0},
        compiler_params=params(60),
        cost_estimate=cost(0, 2e6),
        name="spread",
    )(part, send)


def unpack_body(mid, end, dq_ref, dk_ref, dv_ref, dw_ref):
    heads = []
    for head in range(2):
        blocks = []
        for t in range(TILES_DEV):
            for half in range(2):
                blocks.append(end[2 * head + half, t * 64 : t * 64 + 64, :])
        heads.append(jnp.concatenate(blocks, axis=1))
    dq_ref[...] = jnp.concatenate(heads, axis=0).T
    for chunk, part, low in ((0, mid, 0), (1, end, QUERY_ROWS)):
        for j in range(ROWS // 128):
            block = slice(low + j * 128, low + j * 128 + 128)
            take = [part[r, block, :].astype(F32) for r in range(4)]
            x, y = take[0] + take[1], take[2] + take[3]
            at = slice(chunk * ROWS + j * 128, chunk * ROWS + j * 128 + 128)
            dk_ref[at, :] = jnp.concatenate([x[:64], y[:64]], axis=0).astype(BF16).T
            dv_ref[at, :] = jnp.concatenate([x[64:], y[64:]], axis=0).astype(BF16).T
    for r in range(4):
        for j in range(D // 128):
            at = END_ROWS - DW_ROWS + j * 32
            dw_ref[r * 32 : r * 32 + 32, j * 128 : j * 128 + 128] = end[r, at : at + 32, :].astype(F32)


def unpack(mid, end):
    rows = TILES_DEV * QROWS
    return pl.pallas_call(
        unpack_body,
        grid=(4,),
        in_specs=[
            pl.BlockSpec((4, ROWS, 128), lambda p: (p, 0, 0)),
            pl.BlockSpec((4, END_ROWS, 128), lambda p: (p, 0, 0)),
        ],
        out_specs=[
            pl.BlockSpec((rows, 128), lambda p: (0, p)),
            pl.BlockSpec((BT, 128), lambda p: (0, p)),
            pl.BlockSpec((BT, 128), lambda p: (0, p)),
            pl.BlockSpec((128, D), lambda p: (p, 0)),
        ],
        out_shape=[
            jax.ShapeDtypeStruct((rows, HW), BF16),
            jax.ShapeDtypeStruct((BT, HW), BF16),
            jax.ShapeDtypeStruct((BT, HW), BF16),
            jax.ShapeDtypeStruct((HW, D), F32),
        ],
        compiler_params=params(60),
        cost_estimate=cost(0, 8e6),
        name="unpack",
    )(mid, end)


def swap(x, axes="region"):
    return lax.all_to_all(x, axes, 0, 0, tiled=True)


def per_device(queries, keys, values, block_lists, band_counts, cotangent, out_weight):
    rows = TILES_DEV * QROWS
    q, g = queries.reshape(rows, HW), cotangent.reshape(rows, D)
    lists = jnp.concatenate([block_lists[0], band_counts[0][:, None]], axis=1).astype(BF16)
    lists = lists.reshape(1, -1)
    lists = jnp.pad(lists, ((0, 15), (0, 128 - lists.shape[1])))
    recv = swap(pack(q, keys.reshape(BT, HW), values.reshape(BT, HW), lists))
    lists = recv[:, LIST_ROW, : TILES_DEV * (MAXB + 1)].astype(jnp.int32).reshape(TILES, MAXB + 1)
    plan = plan_of(lists[:, :MAXB], lists[:, MAXB])
    d_attn = dattn(out_weight, g)
    recv, d_attn = lax.optimization_barrier((recv, d_attn))
    d_attn = swap(d_attn).reshape(TILES, 64, HALF)

    attn, lse, kv, kt, qt = forward(plan, recv)
    attn_home = swap(attn.reshape(16, QUERY_ROWS, HALF))
    mid, dq = backward(0, plan, kv, kt, qt, d_attn, attn, lse)
    attn_home, mid = lax.optimization_barrier((attn_home, mid))
    layer, mid = project(attn_home, out_weight, g, mid)
    mid, dq = lax.optimization_barrier((mid, dq))
    mid = swap(mid)
    (end,) = backward(1, plan, kv, kt, qt, d_attn, attn, lse, dq)
    mid, end = lax.optimization_barrier((mid, end))
    share = jnp.sum(mid[:, ROWS:].astype(F32), axis=0, keepdims=True).astype(BF16)
    orbits = lax.axis_size("orbit")
    share = swap(jnp.broadcast_to(share, (orbits, DW_ROWS, 128)), "orbit")
    end = swap(spread(share, end))
    d_q, d_k, d_v, d_weight = unpack(mid, end)
    return (
        layer.reshape(1, TILES_DEV, QROWS, D),
        d_q.reshape(1, TILES_DEV, QROWS, HW),
        d_k.reshape(1, 1, BT, HW),
        d_v.reshape(1, 1, BT, HW),
        d_weight,
    )


def solution(mesh):
    four = P("orbit", "region", None, None)
    return jax.shard_map(
        per_device,
        mesh=mesh,
        in_specs=(four, four, four, P("orbit", "region", None), P("orbit", "region"), four, P()),
        out_specs=(four, four, four, four, P()),
        check_vma=False,
    )
```

```python
import functools

import jax
import jax.numpy as jnp
from jax import lax
from jax.experimental import pallas as pl
from jax.experimental.pallas import tpu as pltpu
from jax.sharding import PartitionSpec as P

HEADS = 8
HEAD_DIM = 64
BANDS = 16
BT = 512
QROWS = 256
HALF = 128
TILES_DEV = 3
TILES = 48
MAXB = 8
D = 1024
HW = 512
CHUNKS = 2
UNROLL = 8
BACK_UNROLL = 8
SUB = 64
BACK_SUB = 256
SUM_ROWS = 16
ROWS = BT // CHUNKS
QUERY_ROWS = TILES_DEV * 64
LIST_ROW = BT + QUERY_ROWS
SEND_ROWS = LIST_ROW + 16
DW_ROWS = HW * D // 16 // 128
MID_ROWS = ROWS + DW_ROWS
END_ROWS = QUERY_ROWS + ROWS
PAIRS = 208
SCALE = HEAD_DIM**-0.5
LOW = -1e30
BF16 = jnp.bfloat16
F32 = jnp.float32

NT = (((1,), (1,)), ((), ()))


def dot(a, b, dims=(((1,), (0,)), ((), ()))):
    return lax.dot_general(a, b, dims, preferred_element_type=F32)


def params(mib=56):
    return pltpu.CompilerParams(vmem_limit_bytes=mib << 20)


def cost(flops, nbytes, exps=0):
    return pl.CostEstimate(flops=int(flops), bytes_accessed=int(nbytes), transcendentals=int(exps))


def whole(*shape):
    return pl.BlockSpec(shape, lambda *_: (0,) * len(shape))


SMEM = pl.BlockSpec(memory_space=pltpu.SMEM)


def pack_body(q_ref, k_ref, v_ref, list_ref, count_ref, out_ref, rows_ref):
    rows_ref[...] = jnp.zeros(rows_ref.shape, F32)
    rows_ref[:TILES_DEV, :MAXB] = list_ref[...].astype(F32)
    rows_ref[8:9, :TILES_DEV] = count_ref[...].astype(F32)
    lists = rows_ref[...].astype(BF16)
    kt = k_ref[...].T
    vt = v_ref[...].T
    qt = (q_ref[...].astype(F32) * SCALE).astype(BF16).T
    for head in range(2):
        rows = slice(head * 64, head * 64 + 64)
        for half in range(2):
            dest = 2 * head + half
            out_ref[dest, LIST_ROW:SEND_ROWS, :] = lists
            for j in range(4):
                lanes = slice(j * 128, j * 128 + 128)
                out_ref[dest, j * 128 : j * 128 + 64, :] = kt[rows, lanes]
                out_ref[dest, j * 128 + 64 : j * 128 + 128, :] = vt[rows, lanes]
            for t in range(TILES_DEV):
                low = t * QROWS + half * HALF
                out_ref[dest, BT + t * 64 : BT + t * 64 + 64, :] = qt[rows, low : low + HALF]


def pack(q, k, v, lists, counts):
    return pl.pallas_call(
        pack_body,
        grid=(4,),
        in_specs=[
            pl.BlockSpec((TILES_DEV * QROWS, 128), lambda p: (0, p)),
            pl.BlockSpec((BT, 128), lambda p: (0, p)),
            pl.BlockSpec((BT, 128), lambda p: (0, p)),
            pl.BlockSpec((TILES_DEV, MAXB), lambda p: (0, 0)),
            pl.BlockSpec((1, TILES_DEV), lambda p: (0, 0)),
        ],
        out_specs=pl.BlockSpec((4, SEND_ROWS, 128), lambda p: (p, 0, 0)),
        out_shape=jax.ShapeDtypeStruct((16, SEND_ROWS, 128), BF16),
        scratch_shapes=[pltpu.VMEM((16, 128), F32)],
        compiler_params=params(60),
        cost_estimate=cost(0, 8e6),
        name="pack",
    )(q, k, v, lists, counts)


def dattn_body(w_ref, g_ref, out_ref):
    dt = dot(w_ref[...], g_ref[...], NT).astype(BF16)
    for head in range(2):
        for half in range(2):
            for t in range(TILES_DEV):
                low = t * QROWS + half * HALF
                out_ref[2 * head + half, t * 64 : t * 64 + 64, :] = dt[
                    head * 64 : head * 64 + 64, low : low + HALF
                ]


def dattn(w, g):
    rows = TILES_DEV * QROWS
    return pl.pallas_call(
        dattn_body,
        grid=(4,),
        in_specs=[
            pl.BlockSpec((128, D), lambda p: (p, 0)),
            pl.BlockSpec((rows, D), lambda p: (0, 0)),
        ],
        out_specs=pl.BlockSpec((4, TILES_DEV * 64, 128), lambda p: (p, 0, 0)),
        out_shape=jax.ShapeDtypeStruct((16, TILES_DEV * 64, 128), BF16),
        compiler_params=params(60),
        cost_estimate=cost(2 * rows * D * HW, 4e6),
        name="dattn",
    )(w, g)


def plan_of(lists, counts):
    slots = jnp.arange(MAXB)[None, :] < counts[:, None]
    member = (
        (lists[:, :, None] == jnp.arange(BANDS)[None, None, :]) & slots[:, :, None]
    ).any(axis=1)
    member = member.T.astype(jnp.int32)
    place = jnp.cumsum(member, axis=1) - member
    size = (member.sum(axis=1) + 1) // 2
    base = jnp.cumsum(size) - size
    flat = jnp.where(member > 0, 2 * base[:, None] + place, -1)
    hit = flat[None] == jnp.arange(2 * PAIRS)[:, None, None]
    tile = jnp.arange(TILES)[None, None, :]
    band = jnp.arange(BANDS)[None, :, None]
    code = jnp.sum(jnp.where(hit, band * 64 + tile + 1, 0), axis=(1, 2)).reshape(PAIRS, 2)
    who = jnp.where(code > 0, (code & 63) - 1, TILES)
    number = size.sum()
    return jnp.stack(
        [who[:, 0], who[:, 1], code[:, 0] >> 6, jnp.full((PAIRS,), number, jnp.int32)]
    ).astype(jnp.int32)


def forward_body(plan, recv, attn_ref, lse_ref, kv_ref, kt_ref, qt_ref, vt, top, acc, s0, s1, p0, p1, h0, h1):
    def unpack_band(b, carry):
        kvt = jnp.concatenate([recv[b, j * 128 : j * 128 + 128, :] for j in range(4)], axis=1)
        kv_ref[b] = kvt.T
        kt_ref[b] = kvt[:64]
        vt[b] = jnp.concatenate([kvt[64:], jnp.ones((SUM_ROWS, BT), BF16)], axis=0)
        for t in range(TILES_DEV):
            qt_ref[b * TILES_DEV + t] = recv[b, BT + t * 64 : BT + t * 64 + 64, :]
        return carry

    lax.fori_loop(0, BANDS, unpack_band, 0)
    qt_ref[TILES] = jnp.zeros((64, HALF), BF16)
    top[...] = jnp.full(top.shape, LOW, F32)
    acc[...] = jnp.zeros(acc.shape, F32)
    blank = jnp.zeros((64, 2 * HALF), BF16)

    def scores(i, s, h, weigh=None):
        a, c = plan[0, i], plan[1, i]
        w = jnp.concatenate([jnp.concatenate([qt_ref[a], qt_ref[c]], axis=1), blank], axis=0)
        peak = None
        for low in range(0, BT, SUB):
            rows = slice(low, low + SUB)
            st = dot(kv_ref[plan[2, i], rows, :], w)
            s[rows, :] = st
            high = jnp.max(st.reshape(SUB // 8, 8, 2 * HALF), axis=0)
            peak = high if peak is None else jnp.maximum(peak, high)
            if weigh is not None:
                weigh(rows)
        old = jnp.concatenate([top[a], top[c]], axis=1)
        new = jnp.maximum(old, jnp.max(peak, axis=0, keepdims=True))
        top[a] = new[:, :HALF]
        top[c] = new[:, HALF:]
        h[0:1, :] = new
        h[1:2, :] = jnp.exp(old - new)

    def weigh(s, h, p, rows):
        p[rows, :] = jnp.exp(s[rows, :] - h[0:1, :]).astype(BF16)

    def gather(i, fade, p):
        o = dot(vt[plan[2, i]], p[...])
        for x, lanes in ((plan[0, i], slice(0, HALF)), (plan[1, i], slice(HALF, 2 * HALF))):
            acc[x] = acc[x] * fade[:, lanes] + o[:, lanes]

    scores(0, s0, h0)
    scores(1, s1, h1)
    weigh(s0, h0, p0, slice(0, BT))

    even, odd = (s0, h0, p0), (s1, h1, p1)

    def step(j, carry):
        for k in range(UNROLL):
            i = UNROLL * j + k
            (s, h, p), (s_next, h_next, p_next) = (even, odd) if k % 2 == 0 else (odd, even)
            fade = h[1:2, :]
            scores(i + 2, s, h, functools.partial(weigh, s_next, h_next, p_next))
            gather(i, fade, p)
        return carry

    lax.fori_loop(0, (plan[3, 0] + UNROLL - 1) // UNROLL, step, 0)

    def finish(x, carry):
        total = acc[x, 64:65, :]
        attn_ref[x] = (acc[x, :64, :] / total).astype(BF16)
        lse_ref[x] = top[x] + jnp.log(total)
        return carry

    lax.fori_loop(0, TILES, finish, 0)
    lse_ref[TILES] = jnp.full((1, HALF), -LOW, F32)


def forward(plan, recv):
    return pl.pallas_call(
        forward_body,
        grid=(1,),
        in_specs=[SMEM, whole(16, SEND_ROWS, 128)],
        out_specs=[
            whole(TILES, 64, HALF),
            whole(TILES + 1, 1, HALF),
            whole(BANDS, BT, 128),
            whole(BANDS, 64, BT),
            whole(TILES + 1, 64, HALF),
        ],
        out_shape=[
            jax.ShapeDtypeStruct((TILES, 64, HALF), BF16),
            jax.ShapeDtypeStruct((TILES + 1, 1, HALF), F32),
            jax.ShapeDtypeStruct((BANDS, BT, 128), BF16),
            jax.ShapeDtypeStruct((BANDS, 64, BT), BF16),
            jax.ShapeDtypeStruct((TILES + 1, 64, HALF), BF16),
        ],
        scratch_shapes=[
            pltpu.VMEM((BANDS, 64 + SUM_ROWS, BT), BF16),
            pltpu.VMEM((TILES + 1, 1, HALF), F32),
            pltpu.VMEM((TILES + 1, 64 + SUM_ROWS, HALF), F32),
            pltpu.VMEM((BT, 2 * HALF), F32),
            pltpu.VMEM((BT, 2 * HALF), F32),
            pltpu.VMEM((BT, 2 * HALF), BF16),
            pltpu.VMEM((BT, 2 * HALF), BF16),
            pltpu.VMEM((8, 2 * HALF), F32),
            pltpu.VMEM((8, 2 * HALF), F32),
        ],
        compiler_params=params(60),
        cost_estimate=cost(2.4e10, 2e7, 16e6),
        name="forward",
    )(plan, recv)


def backward_body(last, plan, kv, kt, qt, dot_, attn, lse, dq_in, send_ref, dq_ref, gt, delta, dkv, dq, s0, t0, s1, t1, p0, d0, p1, d1):
    rows = kv.shape[1]

    def prepare(x, carry):
        gt[x] = dot_[x]
        delta[x] = jnp.sum(attn[x].astype(F32) * dot_[x].astype(F32), axis=0, keepdims=True)
        return carry

    lax.fori_loop(0, TILES, prepare, 0)
    gt[TILES] = jnp.zeros((64, HALF), BF16)
    delta[TILES] = jnp.zeros((1, HALF), F32)
    dkv[...] = jnp.zeros(dkv.shape, F32)
    if dq_in is None:
        dq[...] = jnp.zeros(dq.shape, F32)
    else:
        dq[...] = dq_in[...]
    blank = jnp.zeros((64, 2 * HALF), BF16)

    def pair(ref, i):
        return jnp.concatenate([ref[plan[0, i]], ref[plan[1, i]]], axis=1)

    def scores(i, s, t, weigh=None):
        wq = jnp.concatenate([pair(qt, i), blank], axis=0)
        wg = jnp.concatenate([blank, pair(gt, i)], axis=0)
        for low in range(0, rows, BACK_SUB):
            at = slice(low, low + BACK_SUB)
            band = kv[plan[2, i], at, :]
            s[at, :] = dot(band, wq)
            t[at, :] = dot(band, wg)
            if weigh is not None:
                weigh(at)

    def weigh(i, s, t, p_ref, d_ref, at):
        p = jnp.exp(s[at, :] - pair(lse, i))
        p_ref[at, :] = p.astype(BF16)
        d_ref[at, :] = (p * (t[at, :] - pair(delta, i))).astype(BF16)

    def gather(i, p_ref, d_ref):
        a, c, b = plan[0, i], plan[1, i], plan[2, i]
        part = dot(kt[b], d_ref[...])
        dq[a] += part[:, :HALF]
        dq[c] += part[:, HALF:]
        dkv[b, :64, :] += dot(pair(qt, i), d_ref[...], NT)
        dkv[b, 64:, :] += dot(pair(gt, i), p_ref[...], NT)

    scores(0, s0, t0)
    scores(1, s1, t1)
    weigh(0, s0, t0, p0, d0, slice(0, rows))

    even, odd = (s0, t0, p0, d0), (s1, t1, p1, d1)

    def step(j, carry):
        for k in range(BACK_UNROLL):
            i = BACK_UNROLL * j + k
            now, later = (even, odd) if k % 2 == 0 else (odd, even)
            scores(i + 2, *now[:2], functools.partial(weigh, i + 1, *later))
            gather(i, *now[2:])
        return carry

    lax.fori_loop(0, (plan[3, 0] + BACK_UNROLL - 1) // BACK_UNROLL, step, 0)

    first = QUERY_ROWS if last else 0

    def finish(b, carry):
        for j in range(rows // 128):
            at = first + j * 128
            send_ref[b, at : at + 128, :] = dkv[b, :, j * 128 : j * 128 + 128].astype(BF16)
        if last:
            for t in range(TILES_DEV):
                send_ref[b, t * 64 : t * 64 + 64, :] = (dq[b * TILES_DEV + t] * SCALE).astype(BF16)
        return carry

    lax.fori_loop(0, BANDS, finish, 0)
    if not last:
        dq_ref[...] = dq[...]


def backward(chunk, plan, kv, kt, qt, dot_, attn, lse, dq_in=None):
    last = chunk == CHUNKS - 1
    if last:

        def body(*refs):
            return backward_body(True, *refs[:9], None, *refs[9:])
    else:

        def body(*refs):
            return backward_body(False, *refs[:7], None, *refs[7:])

    specs = [
        SMEM,
        pl.BlockSpec((BANDS, ROWS, 128), lambda i: (0, chunk, 0)),
        pl.BlockSpec((BANDS, 64, ROWS), lambda i: (0, 0, chunk)),
        whole(TILES + 1, 64, HALF),
        whole(TILES, 64, HALF),
        whole(TILES, 64, HALF),
        whole(TILES + 1, 1, HALF),
    ]
    args = [plan, kv, kt, qt, dot_, attn, lse]
    if last:
        specs.append(whole(TILES + 1, 64, HALF))
        args.append(dq_in)
        out_specs = [whole(BANDS, QUERY_ROWS + ROWS, 128)]
        out_shape = [jax.ShapeDtypeStruct((BANDS, END_ROWS, 128), BF16)]
    else:
        out_specs = [whole(BANDS, ROWS, 128), whole(TILES + 1, 64, HALF)]
        out_shape = [
            jax.ShapeDtypeStruct((BANDS, MID_ROWS, 128), BF16),
            jax.ShapeDtypeStruct((TILES + 1, 64, HALF), F32),
        ]
    return pl.pallas_call(
        body,
        grid=(1,),
        in_specs=specs,
        out_specs=out_specs,
        out_shape=out_shape,
        scratch_shapes=[
            pltpu.VMEM((TILES + 1, 64, HALF), BF16),
            pltpu.VMEM((TILES + 1, 1, HALF), F32),
            pltpu.VMEM((BANDS, 128, ROWS), F32),
            pltpu.VMEM((TILES + 1, 64, HALF), F32),
        ]
        + [pltpu.VMEM((ROWS, 2 * HALF), F32)] * 4
        + [pltpu.VMEM((ROWS, 2 * HALF), BF16)] * 4,
        compiler_params=params(60),
        cost_estimate=cost(5e10 / CHUNKS, 2e7, 16e6 / CHUNKS),
        name="backward",
    )(*args)


def attn_columns(recv, low):
    heads = [
        jnp.concatenate([recv[2 * h, pl.ds(low, 64), :], recv[2 * h + 1, pl.ds(low, 64), :]], axis=1)
        for h in range(HEADS)
    ]
    return jnp.concatenate(heads, axis=0)


def weight_body(recv, g_ref, unused, send_ref):
    g = g_ref[...]
    for t in range(TILES_DEV):
        term = dot(attn_columns(recv, t * 64), g[t * QROWS : (t + 1) * QROWS])
        total = term if t == 0 else total + term
    total = total.astype(BF16)
    for dest in range(16):
        send_ref[dest] = total[dest * 32 : dest * 32 + 32]


def weight_grad(recv, g, send):
    rows = TILES_DEV * QROWS
    steps = D // 128
    return pl.pallas_call(
        weight_body,
        grid=(steps,),
        in_specs=[
            pl.BlockSpec((16, QUERY_ROWS, 128), lambda j: (0, 0, 0)),
            pl.BlockSpec((rows, 128), lambda j: (0, j)),
            pl.BlockSpec(memory_space=pl.ANY),
        ],
        out_specs=pl.BlockSpec((16, 32, 128), lambda j: (0, ROWS // 32 + j, 0)),
        out_shape=jax.ShapeDtypeStruct((BANDS, MID_ROWS, 128), BF16),
        input_output_aliases={2: 0},
        compiler_params=params(60),
        cost_estimate=cost(2 * rows * D * HW, 5e6),
        name="weight_grad",
    )(recv, g, send)


def layer_body(recv, w_ref, layer_ref):
    low = pl.multiple_of(pl.program_id(0) * 64, 64)
    layer_ref[...] = dot(attn_columns(recv, low).T, w_ref[...]).astype(BF16)


def layer_output(recv, w):
    rows = TILES_DEV * QROWS
    return pl.pallas_call(
        layer_body,
        grid=(TILES_DEV,),
        in_specs=[
            pl.BlockSpec((16, QUERY_ROWS, 128), lambda t: (0, 0, 0)),
            pl.BlockSpec((HW, D), lambda t: (0, 0)),
        ],
        out_specs=pl.BlockSpec((QROWS, D), lambda t: (t, 0)),
        out_shape=jax.ShapeDtypeStruct((rows, D), BF16),
        compiler_params=params(60),
        cost_estimate=cost(2 * rows * D * HW, 4e6),
        name="layer_output",
    )(recv, w)


def unpack_body(mid, end, dq_ref, dk_ref, dv_ref):
    heads = []
    for head in range(2):
        blocks = []
        for t in range(TILES_DEV):
            for half in range(2):
                blocks.append(end[2 * head + half, t * 64 : t * 64 + 64, :])
        heads.append(jnp.concatenate(blocks, axis=1))
    dq_ref[...] = jnp.concatenate(heads, axis=0).T
    for chunk, part, low in ((0, mid, 0), (1, end, QUERY_ROWS)):
        for j in range(ROWS // 128):
            block = slice(low + j * 128, low + j * 128 + 128)
            take = [part[r, block, :].astype(F32) for r in range(4)]
            x, y = take[0] + take[1], take[2] + take[3]
            at = slice(chunk * ROWS + j * 128, chunk * ROWS + j * 128 + 128)
            dk_ref[at, :] = jnp.concatenate([x[:64], y[:64]], axis=0).astype(BF16).T
            dv_ref[at, :] = jnp.concatenate([x[64:], y[64:]], axis=0).astype(BF16).T


def weight_out_body(part, dw_ref):
    for r in range(4):
        for j in range(D // 128):
            dw_ref[r * 32 : r * 32 + 32, j * 128 : j * 128 + 128] = part[
                r, j * 32 : j * 32 + 32, :
            ].astype(F32)


def weight_out(part):
    return pl.pallas_call(
        weight_out_body,
        grid=(4,),
        in_specs=[pl.BlockSpec((4, DW_ROWS, 128), lambda p: (p, 0, 0))],
        out_specs=pl.BlockSpec((128, D), lambda p: (p, 0)),
        out_shape=jax.ShapeDtypeStruct((HW, D), F32),
        compiler_params=params(60),
        cost_estimate=cost(0, 3e6),
        name="weight_out",
    )(part)


def unpack(mid, end):
    rows = TILES_DEV * QROWS
    return pl.pallas_call(
        unpack_body,
        grid=(4,),
        in_specs=[
            pl.BlockSpec((4, ROWS, 128), lambda p: (p, 0, 0)),
            pl.BlockSpec((4, END_ROWS, 128), lambda p: (p, 0, 0)),
        ],
        out_specs=[
            pl.BlockSpec((rows, 128), lambda p: (0, p)),
            pl.BlockSpec((BT, 128), lambda p: (0, p)),
            pl.BlockSpec((BT, 128), lambda p: (0, p)),
        ],
        out_shape=[
            jax.ShapeDtypeStruct((rows, HW), BF16),
            jax.ShapeDtypeStruct((BT, HW), BF16),
            jax.ShapeDtypeStruct((BT, HW), BF16),
        ],
        compiler_params=params(60),
        cost_estimate=cost(0, 8e6),
        name="unpack",
    )(mid, end)


def swap(x, axes="region"):
    return lax.all_to_all(x, axes, 0, 0, tiled=True)


def orbit_sum(share):
    size = lax.axis_size("orbit")
    total = share.astype(F32)
    for shift in range(1, size):
        total += lax.ppermute(share, "orbit", [(i, (i + shift) % size) for i in range(size)]).astype(F32)
    return total


def per_device(queries, keys, values, block_lists, band_counts, cotangent, out_weight):
    rows = TILES_DEV * QROWS
    q, g = queries.reshape(rows, HW), cotangent.reshape(rows, D)
    k, v = keys.reshape(BT, HW), values.reshape(BT, HW)
    recv = swap(pack(q, k, v, block_lists[0], band_counts))
    lists = recv[:, LIST_ROW : LIST_ROW + TILES_DEV, :MAXB].astype(jnp.int32).reshape(TILES, MAXB)
    counts = recv[:, LIST_ROW + 8, :TILES_DEV].astype(jnp.int32).reshape(TILES)
    plan = plan_of(lists, counts)
    d_attn = dattn(out_weight, g)
    recv, d_attn = lax.optimization_barrier((recv, d_attn))
    d_attn = swap(d_attn).reshape(TILES, 64, HALF)

    attn, lse, kv, kt, qt = forward(plan, recv)
    attn_home = swap(attn.reshape(16, QUERY_ROWS, HALF))
    mid, dq = backward(0, plan, kv, kt, qt, d_attn, attn, lse)
    attn_home, mid = lax.optimization_barrier((attn_home, mid))
    mid = weight_grad(attn_home, g, mid)
    mid, dq = lax.optimization_barrier((mid, dq))
    mid = swap(mid)
    (end,) = backward(1, plan, kv, kt, qt, d_attn, attn, lse, dq)
    mid, end, attn_home = lax.optimization_barrier((mid, end, attn_home))
    end = swap(end)
    share = jnp.sum(mid[:, ROWS:].astype(F32), axis=0).astype(BF16)
    total = orbit_sum(share).astype(BF16)
    layer = layer_output(attn_home, out_weight)
    end, total, layer = lax.optimization_barrier((end, total, layer))
    total = swap(jnp.broadcast_to(total[None], (16, DW_ROWS, 128)))
    d_q, d_k, d_v = unpack(mid, end)
    return (
        layer.reshape(1, TILES_DEV, QROWS, D),
        d_q.reshape(1, TILES_DEV, QROWS, HW),
        d_k.reshape(1, 1, BT, HW),
        d_v.reshape(1, 1, BT, HW),
        weight_out(total),
    )


def solution(mesh):
    four = P("orbit", "region", None, None)
    return jax.shard_map(
        per_device,
        mesh=mesh,
        in_specs=(four, four, four, P("orbit", "region", None), P("orbit", "region"), four, P()),
        out_specs=(four, four, four, four, P()),
        check_vma=False,
    )
```

```python
import functools

import jax
import jax.numpy as jnp
from jax import lax
from jax.experimental import pallas as pl
from jax.experimental.pallas import tpu as pltpu
from jax.sharding import PartitionSpec as P

HEADS = 8
HEAD_DIM = 64
BANDS = 16
BT = 512
QROWS = 256
HALF = 128
TILES_DEV = 3
TILES = 48
MAXB = 8
D = 1024
HW = 512
CHUNKS = 2
UNROLL = 8
BACK_UNROLL = 8
SUB = 64
BACK_SUB = 256
SUM_ROWS = 16
ROWS = BT // CHUNKS
QUERY_ROWS = TILES_DEV * 64
SEND_ROWS = BT + QUERY_ROWS
DW_ROWS = HW * D // 16 // 128
MID_ROWS = ROWS + DW_ROWS
END_ROWS = QUERY_ROWS + ROWS
PAIRS = 208
SCALE = HEAD_DIM**-0.5
LOW = -1e30
BF16 = jnp.bfloat16
F32 = jnp.float32

NT = (((1,), (1,)), ((), ()))


def dot(a, b, dims=(((1,), (0,)), ((), ()))):
    return lax.dot_general(a, b, dims, preferred_element_type=F32)


def params(mib=56):
    return pltpu.CompilerParams(vmem_limit_bytes=mib << 20)


def cost(flops, nbytes, exps=0):
    return pl.CostEstimate(flops=int(flops), bytes_accessed=int(nbytes), transcendentals=int(exps))


def whole(*shape):
    return pl.BlockSpec(shape, lambda *_: (0,) * len(shape))


SMEM = pl.BlockSpec(memory_space=pltpu.SMEM)


def pack_body(q_ref, k_ref, v_ref, out_ref):
    kt = k_ref[...].T
    vt = v_ref[...].T
    qt = (q_ref[...].astype(F32) * SCALE).astype(BF16).T
    for head in range(2):
        rows = slice(head * 64, head * 64 + 64)
        for half in range(2):
            dest = 2 * head + half
            for j in range(4):
                lanes = slice(j * 128, j * 128 + 128)
                out_ref[dest, j * 128 : j * 128 + 64, :] = kt[rows, lanes]
                out_ref[dest, j * 128 + 64 : j * 128 + 128, :] = vt[rows, lanes]
            for t in range(TILES_DEV):
                low = t * QROWS + half * HALF
                out_ref[dest, BT + t * 64 : BT + t * 64 + 64, :] = qt[rows, low : low + HALF]


def pack(q, k, v):
    return pl.pallas_call(
        pack_body,
        grid=(4,),
        in_specs=[
            pl.BlockSpec((TILES_DEV * QROWS, 128), lambda p: (0, p)),
            pl.BlockSpec((BT, 128), lambda p: (0, p)),
            pl.BlockSpec((BT, 128), lambda p: (0, p)),
        ],
        out_specs=pl.BlockSpec((4, SEND_ROWS, 128), lambda p: (p, 0, 0)),
        out_shape=jax.ShapeDtypeStruct((16, SEND_ROWS, 128), BF16),
        compiler_params=params(60),
        cost_estimate=cost(0, 8e6),
        name="pack",
    )(q, k, v)


def dattn_body(w_ref, g_ref, out_ref):
    dt = dot(w_ref[...], g_ref[...], NT).astype(BF16)
    for head in range(2):
        for half in range(2):
            for t in range(TILES_DEV):
                low = t * QROWS + half * HALF
                out_ref[2 * head + half, t * 64 : t * 64 + 64, :] = dt[
                    head * 64 : head * 64 + 64, low : low + HALF
                ]


def dattn(w, g):
    rows = TILES_DEV * QROWS
    return pl.pallas_call(
        dattn_body,
        grid=(4,),
        in_specs=[
            pl.BlockSpec((128, D), lambda p: (p, 0)),
            pl.BlockSpec((rows, D), lambda p: (0, 0)),
        ],
        out_specs=pl.BlockSpec((4, TILES_DEV * 64, 128), lambda p: (p, 0, 0)),
        out_shape=jax.ShapeDtypeStruct((16, TILES_DEV * 64, 128), BF16),
        compiler_params=params(60),
        cost_estimate=cost(2 * rows * D * HW, 4e6),
        name="dattn",
    )(w, g)


def plan_of(lists, counts, tiles):
    slots = jnp.arange(MAXB)[None, :] < counts[:, None]
    member = (
        (lists[:, :, None] == jnp.arange(BANDS)[None, None, :]) & slots[:, :, None]
    ).any(axis=1)
    member = member.T.astype(jnp.int32)
    place = jnp.cumsum(member, axis=1) - member
    size = (member.sum(axis=1) + 1) // 2
    base = jnp.cumsum(size) - size
    flat = jnp.where(member > 0, 2 * base[:, None] + place, -1)
    hit = flat[None] == jnp.arange(2 * PAIRS)[:, None, None]
    tile = tiles[None, None, :]
    band = jnp.arange(BANDS)[None, :, None]
    code = jnp.sum(jnp.where(hit, band * 64 + tile + 1, 0), axis=(1, 2)).reshape(PAIRS, 2)
    who = jnp.where(code > 0, (code & 63) - 1, TILES)
    number = size.sum()
    return jnp.stack(
        [who[:, 0], who[:, 1], code[:, 0] >> 6, jnp.full((PAIRS,), number, jnp.int32)]
    ).astype(jnp.int32)


def gather_lists(mine):
    size = lax.axis_size("region")
    step, rows = 1, mine
    while step < size:
        other = lax.ppermute(rows, "region", [((i + step) % size, i) for i in range(size)])
        rows = jnp.concatenate([rows, other], axis=0)
        step *= 2
    tiles = (jnp.arange(TILES) + lax.axis_index("region") * TILES_DEV) % TILES
    return rows, tiles


def batched(count, width, body):
    def step(j, carry):
        for k in range(width):
            body(j * width + k)
        return carry

    lax.fori_loop(0, count // width, step, 0)


def forward_body(plan, recv, attn_ref, lse_ref, kv_ref, kt_ref, qt_ref, vt, top, acc, s0, s1, p0, p1, h0, h1):
    def unpack_band(b):
        kvt = jnp.concatenate([recv[b, j * 128 : j * 128 + 128, :] for j in range(4)], axis=1)
        kv_ref[b] = kvt.T
        kt_ref[b] = kvt[:64]
        vt[b] = jnp.concatenate([kvt[64:], jnp.ones((SUM_ROWS, BT), BF16)], axis=0)
        for t in range(TILES_DEV):
            qt_ref[b * TILES_DEV + t] = recv[b, BT + t * 64 : BT + t * 64 + 64, :]

    batched(BANDS, 4, unpack_band)
    qt_ref[TILES] = jnp.zeros((64, HALF), BF16)
    top[...] = jnp.full(top.shape, LOW, F32)
    acc[...] = jnp.zeros(acc.shape, F32)
    blank = jnp.zeros((64, 2 * HALF), BF16)

    def scores(i, s, h, weigh=None):
        a, c = plan[0, i], plan[1, i]
        w = jnp.concatenate([jnp.concatenate([qt_ref[a], qt_ref[c]], axis=1), blank], axis=0)
        peak = None
        for low in range(0, BT, SUB):
            rows = slice(low, low + SUB)
            st = dot(kv_ref[plan[2, i], rows, :], w)
            s[rows, :] = st
            high = jnp.max(st.reshape(SUB // 8, 8, 2 * HALF), axis=0)
            peak = high if peak is None else jnp.maximum(peak, high)
            if weigh is not None:
                weigh(rows)
        old = jnp.concatenate([top[a], top[c]], axis=1)
        new = jnp.maximum(old, jnp.max(peak, axis=0, keepdims=True))
        top[a] = new[:, :HALF]
        top[c] = new[:, HALF:]
        h[0:1, :] = new
        h[1:2, :] = jnp.exp(old - new)

    def weigh(s, h, p, rows):
        p[rows, :] = jnp.exp(s[rows, :] - h[0:1, :]).astype(BF16)

    def gather(i, fade, p):
        o = dot(vt[plan[2, i]], p[...])
        for x, lanes in ((plan[0, i], slice(0, HALF)), (plan[1, i], slice(HALF, 2 * HALF))):
            acc[x] = acc[x] * fade[:, lanes] + o[:, lanes]

    scores(0, s0, h0)
    scores(1, s1, h1)
    weigh(s0, h0, p0, slice(0, BT))

    even, odd = (s0, h0, p0), (s1, h1, p1)

    def step(j, carry):
        for k in range(UNROLL):
            i = UNROLL * j + k
            (s, h, p), (s_next, h_next, p_next) = (even, odd) if k % 2 == 0 else (odd, even)
            fade = h[1:2, :]
            scores(i + 2, s, h, functools.partial(weigh, s_next, h_next, p_next))
            gather(i, fade, p)
        return carry

    lax.fori_loop(0, (plan[3, 0] + UNROLL - 1) // UNROLL, step, 0)

    def finish(x):
        total = acc[x, 64:65, :]
        attn_ref[x] = (acc[x, :64, :] * (1.0 / total)).astype(BF16)
        lse_ref[x] = top[x] + jnp.log(total)

    batched(TILES, 8, finish)
    lse_ref[TILES] = jnp.full((1, HALF), -LOW, F32)


def forward(plan, recv):
    return pl.pallas_call(
        forward_body,
        grid=(1,),
        in_specs=[SMEM, whole(16, SEND_ROWS, 128)],
        out_specs=[
            whole(TILES, 64, HALF),
            whole(TILES + 1, 1, HALF),
            whole(BANDS, BT, 128),
            whole(BANDS, 64, BT),
            whole(TILES + 1, 64, HALF),
        ],
        out_shape=[
            jax.ShapeDtypeStruct((TILES, 64, HALF), BF16),
            jax.ShapeDtypeStruct((TILES + 1, 1, HALF), F32),
            jax.ShapeDtypeStruct((BANDS, BT, 128), BF16),
            jax.ShapeDtypeStruct((BANDS, 64, BT), BF16),
            jax.ShapeDtypeStruct((TILES + 1, 64, HALF), BF16),
        ],
        scratch_shapes=[
            pltpu.VMEM((BANDS, 64 + SUM_ROWS, BT), BF16),
            pltpu.VMEM((TILES + 1, 1, HALF), F32),
            pltpu.VMEM((TILES + 1, 64 + SUM_ROWS, HALF), F32),
            pltpu.VMEM((BT, 2 * HALF), F32),
            pltpu.VMEM((BT, 2 * HALF), F32),
            pltpu.VMEM((BT, 2 * HALF), BF16),
            pltpu.VMEM((BT, 2 * HALF), BF16),
            pltpu.VMEM((8, 2 * HALF), F32),
            pltpu.VMEM((8, 2 * HALF), F32),
        ],
        compiler_params=params(60),
        cost_estimate=cost(2.4e10, 2e7, 16e6),
        name="forward",
    )(plan, recv)


def backward_body(last, plan, kv, kt, qt, dot_, attn, lse, dq_in, send_ref, dq_ref, delta, dkv, dq, s0, t0, s1, t1, p0, d0, p1, d1):
    rows = kv.shape[1]

    def prepare(x):
        delta[x] = jnp.sum(attn[x].astype(F32) * dot_[x].astype(F32), axis=0, keepdims=True)

    batched(TILES, 8, prepare)
    delta[TILES] = jnp.zeros((1, HALF), F32)
    dkv[...] = jnp.zeros(dkv.shape, F32)
    if dq_in is None:
        dq[...] = jnp.zeros(dq.shape, F32)
    else:
        dq[...] = dq_in[...]
    blank = jnp.zeros((64, 2 * HALF), BF16)

    def pair(ref, i):
        return jnp.concatenate([ref[plan[0, i]], ref[plan[1, i]]], axis=1)

    def pair_g(i):
        a, c = jnp.minimum(plan[0, i], TILES - 1), jnp.minimum(plan[1, i], TILES - 1)
        return jnp.concatenate([dot_[a], dot_[c]], axis=1)

    def scores(i, s, t, weigh=None):
        wq = jnp.concatenate([pair(qt, i), blank], axis=0)
        wg = jnp.concatenate([blank, pair_g(i)], axis=0)
        for low in range(0, rows, BACK_SUB):
            at = slice(low, low + BACK_SUB)
            band = kv[plan[2, i], at, :]
            s[at, :] = dot(band, wq)
            t[at, :] = dot(band, wg)
            if weigh is not None:
                weigh(at)

    def weigh(i, s, t, p_ref, d_ref, at):
        p = jnp.exp(s[at, :] - pair(lse, i))
        p_ref[at, :] = p.astype(BF16)
        d_ref[at, :] = (p * (t[at, :] - pair(delta, i))).astype(BF16)

    def gather(i, p_ref, d_ref):
        a, c, b = plan[0, i], plan[1, i], plan[2, i]
        part = dot(kt[b], d_ref[...])
        dq[a] += part[:, :HALF]
        dq[c] += part[:, HALF:]
        dkv[b, :64, :] += dot(pair(qt, i), d_ref[...], NT)
        dkv[b, 64:, :] += dot(pair_g(i), p_ref[...], NT)

    scores(0, s0, t0)
    scores(1, s1, t1)
    weigh(0, s0, t0, p0, d0, slice(0, rows))

    even, odd = (s0, t0, p0, d0), (s1, t1, p1, d1)

    def step(j, carry):
        for k in range(BACK_UNROLL):
            i = BACK_UNROLL * j + k
            now, later = (even, odd) if k % 2 == 0 else (odd, even)
            scores(i + 2, *now[:2], functools.partial(weigh, i + 1, *later))
            gather(i, *now[2:])
        return carry

    lax.fori_loop(0, (plan[3, 0] + BACK_UNROLL - 1) // BACK_UNROLL, step, 0)

    first = QUERY_ROWS if last else 0

    def finish(b):
        for j in range(rows // 128):
            at = first + j * 128
            send_ref[b, at : at + 128, :] = dkv[b, :, j * 128 : j * 128 + 128].astype(BF16)
        if last:
            for t in range(TILES_DEV):
                send_ref[b, t * 64 : t * 64 + 64, :] = (dq[b * TILES_DEV + t] * SCALE).astype(BF16)

    batched(BANDS, 4, finish)
    if not last:
        dq_ref[...] = dq[...]


def backward(chunk, plan, kv, kt, qt, dot_, attn, lse, dq_in=None):
    last = chunk == CHUNKS - 1
    if last:

        def body(*refs):
            return backward_body(True, *refs[:9], None, *refs[9:])
    else:

        def body(*refs):
            return backward_body(False, *refs[:7], None, *refs[7:])

    specs = [
        SMEM,
        pl.BlockSpec((BANDS, ROWS, 128), lambda i: (0, chunk, 0)),
        pl.BlockSpec((BANDS, 64, ROWS), lambda i: (0, 0, chunk)),
        whole(TILES + 1, 64, HALF),
        whole(TILES, 64, HALF),
        whole(TILES, 64, HALF),
        whole(TILES + 1, 1, HALF),
    ]
    args = [plan, kv, kt, qt, dot_, attn, lse]
    if last:
        specs.append(whole(TILES + 1, 64, HALF))
        args.append(dq_in)
        out_specs = [whole(BANDS, QUERY_ROWS + ROWS, 128)]
        out_shape = [jax.ShapeDtypeStruct((BANDS, END_ROWS, 128), BF16)]
    else:
        out_specs = [whole(BANDS, ROWS, 128), whole(TILES + 1, 64, HALF)]
        out_shape = [
            jax.ShapeDtypeStruct((BANDS, MID_ROWS, 128), BF16),
            jax.ShapeDtypeStruct((TILES + 1, 64, HALF), F32),
        ]
    return pl.pallas_call(
        body,
        grid=(1,),
        in_specs=specs,
        out_specs=out_specs,
        out_shape=out_shape,
        scratch_shapes=[
            pltpu.VMEM((TILES + 1, 1, HALF), F32),
            pltpu.VMEM((BANDS, 128, ROWS), F32),
            pltpu.VMEM((TILES + 1, 64, HALF), F32),
        ]
        + [pltpu.VMEM((ROWS, 2 * HALF), F32)] * 4
        + [pltpu.VMEM((ROWS, 2 * HALF), BF16)] * 4,
        compiler_params=params(60),
        cost_estimate=cost(5e10 / CHUNKS, 2e7, 16e6 / CHUNKS),
        name="backward",
    )(*args)


def attn_columns(recv, low):
    heads = [
        jnp.concatenate([recv[2 * h, pl.ds(low, 64), :], recv[2 * h + 1, pl.ds(low, 64), :]], axis=1)
        for h in range(HEADS)
    ]
    return jnp.concatenate(heads, axis=0)


def weight_body(recv, g_ref, unused, send_ref):
    g = g_ref[...]
    for t in range(TILES_DEV):
        term = dot(attn_columns(recv, t * 64), g[t * QROWS : (t + 1) * QROWS])
        total = term if t == 0 else total + term
    total = total.astype(BF16)
    for dest in range(16):
        for j in range(4):
            send_ref[dest, j * 32 : j * 32 + 32, :] = total[
                dest * 32 : dest * 32 + 32, j * 128 : j * 128 + 128
            ]


def weight_grad(recv, g, send):
    rows = TILES_DEV * QROWS
    steps = D // 512
    return pl.pallas_call(
        weight_body,
        grid=(steps,),
        in_specs=[
            pl.BlockSpec((16, QUERY_ROWS, 128), lambda j: (0, 0, 0)),
            pl.BlockSpec((rows, 512), lambda j: (0, j)),
            pl.BlockSpec(memory_space=pl.ANY),
        ],
        out_specs=pl.BlockSpec((16, 128, 128), lambda j: (0, ROWS // 128 + j, 0)),
        out_shape=jax.ShapeDtypeStruct((BANDS, MID_ROWS, 128), BF16),
        input_output_aliases={2: 0},
        compiler_params=params(60),
        cost_estimate=cost(2 * rows * D * HW, 5e6),
        name="weight_grad",
    )(recv, g, send)


def layer_body(recv, w_ref, layer_ref):
    low = pl.multiple_of(pl.program_id(0) * 64, 64)
    layer_ref[...] = dot(attn_columns(recv, low).T, w_ref[...]).astype(BF16)


def layer_output(recv, w):
    rows = TILES_DEV * QROWS
    return pl.pallas_call(
        layer_body,
        grid=(TILES_DEV,),
        in_specs=[
            pl.BlockSpec((16, QUERY_ROWS, 128), lambda t: (0, 0, 0)),
            pl.BlockSpec((HW, D), lambda t: (0, 0)),
        ],
        out_specs=pl.BlockSpec((QROWS, D), lambda t: (t, 0)),
        out_shape=jax.ShapeDtypeStruct((rows, D), BF16),
        compiler_params=params(60),
        cost_estimate=cost(2 * rows * D * HW, 4e6),
        name="layer_output",
    )(recv, w)


def unpack_body(mid, end, dq_ref, dk_ref, dv_ref):
    heads = []
    for head in range(2):
        blocks = []
        for t in range(TILES_DEV):
            for half in range(2):
                blocks.append(end[2 * head + half, t * 64 : t * 64 + 64, :])
        heads.append(jnp.concatenate(blocks, axis=1))
    dq_ref[...] = jnp.concatenate(heads, axis=0).T
    for chunk, part, low in ((0, mid, 0), (1, end, QUERY_ROWS)):
        for j in range(ROWS // 128):
            block = slice(low + j * 128, low + j * 128 + 128)
            take = [part[r, block, :].astype(F32) for r in range(4)]
            x, y = take[0] + take[1], take[2] + take[3]
            at = slice(chunk * ROWS + j * 128, chunk * ROWS + j * 128 + 128)
            dk_ref[at, :] = jnp.concatenate([x[:64], y[:64]], axis=0).astype(BF16).T
            dv_ref[at, :] = jnp.concatenate([x[64:], y[64:]], axis=0).astype(BF16).T


def unpack(mid, end):
    rows = TILES_DEV * QROWS
    return pl.pallas_call(
        unpack_body,
        grid=(4,),
        in_specs=[
            pl.BlockSpec((4, ROWS, 128), lambda p: (p, 0, 0)),
            pl.BlockSpec((4, END_ROWS, 128), lambda p: (p, 0, 0)),
        ],
        out_specs=[
            pl.BlockSpec((rows, 128), lambda p: (0, p)),
            pl.BlockSpec((BT, 128), lambda p: (0, p)),
            pl.BlockSpec((BT, 128), lambda p: (0, p)),
        ],
        out_shape=[
            jax.ShapeDtypeStruct((rows, HW), BF16),
            jax.ShapeDtypeStruct((BT, HW), BF16),
            jax.ShapeDtypeStruct((BT, HW), BF16),
        ],
        compiler_params=params(60),
        cost_estimate=cost(0, 8e6),
        name="unpack",
    )(mid, end)


def swap(x, axes="region"):
    return lax.all_to_all(x, axes, 0, 0, tiled=True)


def orbit_sum(share):
    size = lax.axis_size("orbit")
    total = share.astype(F32)
    for shift in range(1, size):
        total += lax.ppermute(share, "orbit", [(i, (i + shift) % size) for i in range(size)]).astype(F32)
    return total


def per_device(queries, keys, values, block_lists, band_counts, cotangent, out_weight):
    rows = TILES_DEV * QROWS
    q, g = queries.reshape(rows, HW), cotangent.reshape(rows, D)
    packed = pack(q, keys.reshape(BT, HW), values.reshape(BT, HW))
    lists = jnp.concatenate([block_lists[0], band_counts[0][:, None]], axis=1)
    packed, lists = lax.optimization_barrier((packed, lists))
    recv = swap(packed)
    lists, tiles = gather_lists(lists)
    plan = plan_of(lists[:, :MAXB], lists[:, MAXB], tiles)
    d_attn = dattn(out_weight, g)
    recv, d_attn, plan = lax.optimization_barrier((recv, d_attn, plan))
    d_attn = swap(d_attn).reshape(TILES, 64, HALF)

    attn, lse, kv, kt, qt = forward(plan, recv)
    attn_home = swap(attn.reshape(16, QUERY_ROWS, HALF))
    mid, dq = backward(0, plan, kv, kt, qt, d_attn, attn, lse)
    attn_home, mid = lax.optimization_barrier((attn_home, mid))
    mid = weight_grad(attn_home, g, mid)
    mid, dq = lax.optimization_barrier((mid, dq))
    mid = swap(mid)
    (end,) = backward(1, plan, kv, kt, qt, d_attn, attn, lse, dq)
    mid, end, attn_home = lax.optimization_barrier((mid, end, attn_home))
    end = swap(end)
    share = jnp.sum(mid[:, ROWS:].astype(F32), axis=0).astype(BF16)
    total = orbit_sum(share).astype(BF16)
    total = total.reshape(D // 128, 32, 128).transpose(1, 0, 2).reshape(1, 32, D)
    total = jnp.broadcast_to(total, (16, 32, D))
    layer = layer_output(attn_home, out_weight)
    end, total, layer = lax.optimization_barrier((end, total, layer))
    total = swap(total)
    d_q, d_k, d_v = unpack(mid, end)
    return (
        layer.reshape(1, TILES_DEV, QROWS, D),
        d_q.reshape(1, TILES_DEV, QROWS, HW),
        d_k.reshape(1, 1, BT, HW),
        d_v.reshape(1, 1, BT, HW),
        total.reshape(HW, D).astype(F32),
    )


def solution(mesh):
    four = P("orbit", "region", None, None)
    return jax.shard_map(
        per_device,
        mesh=mesh,
        in_specs=(four, four, four, P("orbit", "region", None), P("orbit", "region"), four, P()),
        out_specs=(four, four, four, four, P()),
        check_vma=False,
    )
```

```python
import functools

import jax
import jax.numpy as jnp
from jax import lax
from jax.experimental import pallas as pl
from jax.experimental.pallas import tpu as pltpu
from jax.sharding import PartitionSpec as P

HEADS = 8
HEAD_DIM = 64
BANDS = 16
BT = 512
QROWS = 256
HALF = 128
TILES_DEV = 3
TILES = 48
MAXB = 8
D = 1024
HW = 512
CHUNKS = 2
UNROLL = 8
BACK_UNROLL = 8
SUB = 64
BACK_SUB = 256
SUM_ROWS = 16
ROWS = BT // CHUNKS
QUERY_ROWS = TILES_DEV * 64
LIST_ROW = BT + QUERY_ROWS
SEND_ROWS = LIST_ROW + 16
DW_ROWS = HW * D // 16 // 128
MID_ROWS = ROWS + DW_ROWS
END_ROWS = QUERY_ROWS + ROWS
PAIRS = 208
SCALE = HEAD_DIM**-0.5
LOW = -1e30
BF16 = jnp.bfloat16
F32 = jnp.float32

NT = (((1,), (1,)), ((), ()))


def dot(a, b, dims=(((1,), (0,)), ((), ()))):
    return lax.dot_general(a, b, dims, preferred_element_type=F32)


def params(mib=56):
    return pltpu.CompilerParams(vmem_limit_bytes=mib << 20)


def cost(flops, nbytes, exps=0):
    return pl.CostEstimate(flops=int(flops), bytes_accessed=int(nbytes), transcendentals=int(exps))


def whole(*shape):
    return pl.BlockSpec(shape, lambda *_: (0,) * len(shape))


SMEM = pl.BlockSpec(memory_space=pltpu.SMEM)


def pack_body(q_ref, k_ref, v_ref, list_ref, count_ref, out_ref, rows_ref):
    rows_ref[...] = jnp.zeros(rows_ref.shape, F32)
    rows_ref[:TILES_DEV, :MAXB] = list_ref[...].astype(F32)
    rows_ref[8:9, :TILES_DEV] = count_ref[...].astype(F32)
    lists = rows_ref[...].astype(BF16)
    kt = k_ref[...].T
    vt = v_ref[...].T
    qt = (q_ref[...].astype(F32) * SCALE).astype(BF16).T
    for head in range(2):
        rows = slice(head * 64, head * 64 + 64)
        for half in range(2):
            dest = 2 * head + half
            out_ref[dest, LIST_ROW:SEND_ROWS, :] = lists
            for j in range(4):
                lanes = slice(j * 128, j * 128 + 128)
                out_ref[dest, j * 128 : j * 128 + 64, :] = kt[rows, lanes]
                out_ref[dest, j * 128 + 64 : j * 128 + 128, :] = vt[rows, lanes]
            for t in range(TILES_DEV):
                low = t * QROWS + half * HALF
                out_ref[dest, BT + t * 64 : BT + t * 64 + 64, :] = qt[rows, low : low + HALF]


def pack(q, k, v, lists, counts):
    return pl.pallas_call(
        pack_body,
        grid=(4,),
        in_specs=[
            pl.BlockSpec((TILES_DEV * QROWS, 128), lambda p: (0, p)),
            pl.BlockSpec((BT, 128), lambda p: (0, p)),
            pl.BlockSpec((BT, 128), lambda p: (0, p)),
            pl.BlockSpec((TILES_DEV, MAXB), lambda p: (0, 0)),
            pl.BlockSpec((1, TILES_DEV), lambda p: (0, 0)),
        ],
        out_specs=pl.BlockSpec((4, SEND_ROWS, 128), lambda p: (p, 0, 0)),
        out_shape=jax.ShapeDtypeStruct((16, SEND_ROWS, 128), BF16),
        scratch_shapes=[pltpu.VMEM((16, 128), F32)],
        compiler_params=params(60),
        cost_estimate=cost(0, 8e6),
        name="pack",
    )(q, k, v, lists, counts)


def dattn_body(w_ref, g_ref, out_ref):
    dt = dot(w_ref[...], g_ref[...], NT).astype(BF16)
    for head in range(2):
        for half in range(2):
            for t in range(TILES_DEV):
                low = t * QROWS + half * HALF
                out_ref[2 * head + half, t * 64 : t * 64 + 64, :] = dt[
                    head * 64 : head * 64 + 64, low : low + HALF
                ]


def dattn(w, g):
    rows = TILES_DEV * QROWS
    return pl.pallas_call(
        dattn_body,
        grid=(4,),
        in_specs=[
            pl.BlockSpec((128, D), lambda p: (p, 0)),
            pl.BlockSpec((rows, D), lambda p: (0, 0)),
        ],
        out_specs=pl.BlockSpec((4, TILES_DEV * 64, 128), lambda p: (p, 0, 0)),
        out_shape=jax.ShapeDtypeStruct((16, TILES_DEV * 64, 128), BF16),
        compiler_params=params(60),
        cost_estimate=cost(2 * rows * D * HW, 4e6),
        name="dattn",
    )(w, g)


def plan_of(lists, counts):
    slots = jnp.arange(MAXB)[None, :] < counts[:, None]
    member = (
        (lists[:, :, None] == jnp.arange(BANDS)[None, None, :]) & slots[:, :, None]
    ).any(axis=1)
    member = member.T.astype(jnp.int32)
    place = jnp.cumsum(member, axis=1) - member
    size = (member.sum(axis=1) + 1) // 2
    base = jnp.cumsum(size) - size
    flat = jnp.where(member > 0, 2 * base[:, None] + place, -1)
    hit = flat[None] == jnp.arange(2 * PAIRS)[:, None, None]
    tile = jnp.arange(TILES)[None, None, :]
    band = jnp.arange(BANDS)[None, :, None]
    code = jnp.sum(jnp.where(hit, band * 64 + tile + 1, 0), axis=(1, 2)).reshape(PAIRS, 2)
    who = jnp.where(code > 0, (code & 63) - 1, TILES)
    number = size.sum()
    return jnp.stack(
        [who[:, 0], who[:, 1], code[:, 0] >> 6, jnp.full((PAIRS,), number, jnp.int32)]
    ).astype(jnp.int32)


def batched(count, width, body):
    def step(j, carry):
        for k in range(width):
            body(j * width + k)
        return carry

    lax.fori_loop(0, count // width, step, 0)


def forward_body(plan, recv, attn_ref, lse_ref, kv_ref, kt_ref, qt_ref, vt, top, acc, s0, s1, p0, p1, h0, h1):
    def unpack_band(b):
        kvt = jnp.concatenate([recv[b, j * 128 : j * 128 + 128, :] for j in range(4)], axis=1)
        kv_ref[b] = kvt.T
        kt_ref[b] = kvt[:64]
        vt[b] = jnp.concatenate([kvt[64:], jnp.ones((SUM_ROWS, BT), BF16)], axis=0)
        for t in range(TILES_DEV):
            qt_ref[b * TILES_DEV + t] = recv[b, BT + t * 64 : BT + t * 64 + 64, :]

    batched(BANDS, 4, unpack_band)
    qt_ref[TILES] = jnp.zeros((64, HALF), BF16)
    top[...] = jnp.full(top.shape, LOW, F32)
    acc[...] = jnp.zeros(acc.shape, F32)
    blank = jnp.zeros((64, 2 * HALF), BF16)

    def scores(i, s, h, weigh=None):
        a, c = plan[0, i], plan[1, i]
        w = jnp.concatenate([jnp.concatenate([qt_ref[a], qt_ref[c]], axis=1), blank], axis=0)
        peak = None
        for low in range(0, BT, SUB):
            rows = slice(low, low + SUB)
            st = dot(kv_ref[plan[2, i], rows, :], w)
            s[rows, :] = st
            high = jnp.max(st.reshape(SUB // 8, 8, 2 * HALF), axis=0)
            peak = high if peak is None else jnp.maximum(peak, high)
            if weigh is not None:
                weigh(rows)
        old = jnp.concatenate([top[a], top[c]], axis=1)
        new = jnp.maximum(old, jnp.max(peak, axis=0, keepdims=True))
        top[a] = new[:, :HALF]
        top[c] = new[:, HALF:]
        h[0:1, :] = new
        h[1:2, :] = jnp.exp(old - new)

    def weigh(s, h, p, rows):
        p[rows, :] = jnp.exp(s[rows, :] - h[0:1, :]).astype(BF16)

    def gather(i, fade, p):
        o = dot(vt[plan[2, i]], p[...])
        for x, lanes in ((plan[0, i], slice(0, HALF)), (plan[1, i], slice(HALF, 2 * HALF))):
            acc[x] = acc[x] * fade[:, lanes] + o[:, lanes]

    scores(0, s0, h0)
    scores(1, s1, h1)
    weigh(s0, h0, p0, slice(0, BT))

    even, odd = (s0, h0, p0), (s1, h1, p1)

    def step(j, carry):
        for k in range(UNROLL):
            i = UNROLL * j + k
            (s, h, p), (s_next, h_next, p_next) = (even, odd) if k % 2 == 0 else (odd, even)
            fade = h[1:2, :]
            scores(i + 2, s, h, functools.partial(weigh, s_next, h_next, p_next))
            gather(i, fade, p)
        return carry

    lax.fori_loop(0, (plan[3, 0] + UNROLL - 1) // UNROLL, step, 0)

    def finish(x):
        total = acc[x, 64:65, :]
        attn_ref[x] = (acc[x, :64, :] * (1.0 / total)).astype(BF16)
        lse_ref[x] = top[x] + jnp.log(total)

    batched(TILES, 8, finish)
    lse_ref[TILES] = jnp.full((1, HALF), -LOW, F32)


def forward(plan, recv):
    return pl.pallas_call(
        forward_body,
        grid=(1,),
        in_specs=[SMEM, whole(16, SEND_ROWS, 128)],
        out_specs=[
            whole(TILES, 64, HALF),
            whole(TILES + 1, 1, HALF),
            whole(BANDS, BT, 128),
            whole(BANDS, 64, BT),
            whole(TILES + 1, 64, HALF),
        ],
        out_shape=[
            jax.ShapeDtypeStruct((TILES, 64, HALF), BF16),
            jax.ShapeDtypeStruct((TILES + 1, 1, HALF), F32),
            jax.ShapeDtypeStruct((BANDS, BT, 128), BF16),
            jax.ShapeDtypeStruct((BANDS, 64, BT), BF16),
            jax.ShapeDtypeStruct((TILES + 1, 64, HALF), BF16),
        ],
        scratch_shapes=[
            pltpu.VMEM((BANDS, 64 + SUM_ROWS, BT), BF16),
            pltpu.VMEM((TILES + 1, 1, HALF), F32),
            pltpu.VMEM((TILES + 1, 64 + SUM_ROWS, HALF), F32),
            pltpu.VMEM((BT, 2 * HALF), F32),
            pltpu.VMEM((BT, 2 * HALF), F32),
            pltpu.VMEM((BT, 2 * HALF), BF16),
            pltpu.VMEM((BT, 2 * HALF), BF16),
            pltpu.VMEM((8, 2 * HALF), F32),
            pltpu.VMEM((8, 2 * HALF), F32),
        ],
        compiler_params=params(60),
        cost_estimate=cost(2.4e10, 2e7, 16e6),
        name="forward",
    )(plan, recv)


def backward_body(last, plan, kv, kt, qt, dot_, attn, lse, dq_in, send_ref, dq_ref, delta, dkv, dq, s0, t0, s1, t1, p0, d0, p1, d1):
    rows = kv.shape[1]

    def prepare(x):
        delta[x] = jnp.sum(attn[x].astype(F32) * dot_[x].astype(F32), axis=0, keepdims=True)

    batched(TILES, 8, prepare)
    delta[TILES] = jnp.zeros((1, HALF), F32)
    dkv[...] = jnp.zeros(dkv.shape, F32)
    if dq_in is None:
        dq[...] = jnp.zeros(dq.shape, F32)
    else:
        dq[...] = dq_in[...]
    blank = jnp.zeros((64, 2 * HALF), BF16)

    def pair(ref, i):
        return jnp.concatenate([ref[plan[0, i]], ref[plan[1, i]]], axis=1)

    def pair_g(i):
        a, c = jnp.minimum(plan[0, i], TILES - 1), jnp.minimum(plan[1, i], TILES - 1)
        return jnp.concatenate([dot_[a], dot_[c]], axis=1)

    def scores(i, s, t, weigh=None):
        wq = jnp.concatenate([pair(qt, i), blank], axis=0)
        wg = jnp.concatenate([blank, pair_g(i)], axis=0)
        for low in range(0, rows, BACK_SUB):
            at = slice(low, low + BACK_SUB)
            band = kv[plan[2, i], at, :]
            s[at, :] = dot(band, wq)
            t[at, :] = dot(band, wg)
            if weigh is not None:
                weigh(at)

    def weigh(i, s, t, p_ref, d_ref, at):
        p = jnp.exp(s[at, :] - pair(lse, i))
        p_ref[at, :] = p.astype(BF16)
        d_ref[at, :] = (p * (t[at, :] - pair(delta, i))).astype(BF16)

    def gather(i, p_ref, d_ref):
        a, c, b = plan[0, i], plan[1, i], plan[2, i]
        part = dot(kt[b], d_ref[...])
        dq[a] += part[:, :HALF]
        dq[c] += part[:, HALF:]
        dkv[b, :64, :] += dot(pair(qt, i), d_ref[...], NT)
        dkv[b, 64:, :] += dot(pair_g(i), p_ref[...], NT)

    scores(0, s0, t0)
    scores(1, s1, t1)
    weigh(0, s0, t0, p0, d0, slice(0, rows))

    even, odd = (s0, t0, p0, d0), (s1, t1, p1, d1)

    def step(j, carry):
        for k in range(BACK_UNROLL):
            i = BACK_UNROLL * j + k
            now, later = (even, odd) if k % 2 == 0 else (odd, even)
            scores(i + 2, *now[:2], functools.partial(weigh, i + 1, *later))
            gather(i, *now[2:])
        return carry

    lax.fori_loop(0, (plan[3, 0] + BACK_UNROLL - 1) // BACK_UNROLL, step, 0)

    first = QUERY_ROWS if last else 0

    def finish(b):
        for j in range(rows // 128):
            at = first + j * 128
            send_ref[b, at : at + 128, :] = dkv[b, :, j * 128 : j * 128 + 128].astype(BF16)
        if last:
            for t in range(TILES_DEV):
                send_ref[b, t * 64 : t * 64 + 64, :] = (dq[b * TILES_DEV + t] * SCALE).astype(BF16)

    batched(BANDS, 4, finish)
    if not last:
        dq_ref[...] = dq[...]


def backward(chunk, plan, kv, kt, qt, dot_, attn, lse, dq_in=None):
    last = chunk == CHUNKS - 1
    if last:

        def body(*refs):
            return backward_body(True, *refs[:9], None, *refs[9:])
    else:

        def body(*refs):
            return backward_body(False, *refs[:7], None, *refs[7:])

    specs = [
        SMEM,
        pl.BlockSpec((BANDS, ROWS, 128), lambda i: (0, chunk, 0)),
        pl.BlockSpec((BANDS, 64, ROWS), lambda i: (0, 0, chunk)),
        whole(TILES + 1, 64, HALF),
        whole(TILES, 64, HALF),
        whole(TILES, 64, HALF),
        whole(TILES + 1, 1, HALF),
    ]
    args = [plan, kv, kt, qt, dot_, attn, lse]
    if last:
        specs.append(whole(TILES + 1, 64, HALF))
        args.append(dq_in)
        out_specs = [whole(BANDS, QUERY_ROWS + ROWS, 128)]
        out_shape = [jax.ShapeDtypeStruct((BANDS, END_ROWS, 128), BF16)]
    else:
        out_specs = [whole(BANDS, ROWS, 128), whole(TILES + 1, 64, HALF)]
        out_shape = [
            jax.ShapeDtypeStruct((BANDS, MID_ROWS, 128), BF16),
            jax.ShapeDtypeStruct((TILES + 1, 64, HALF), F32),
        ]
    return pl.pallas_call(
        body,
        grid=(1,),
        in_specs=specs,
        out_specs=out_specs,
        out_shape=out_shape,
        scratch_shapes=[
            pltpu.VMEM((TILES + 1, 1, HALF), F32),
            pltpu.VMEM((BANDS, 128, ROWS), F32),
            pltpu.VMEM((TILES + 1, 64, HALF), F32),
        ]
        + [pltpu.VMEM((ROWS, 2 * HALF), F32)] * 4
        + [pltpu.VMEM((ROWS, 2 * HALF), BF16)] * 4,
        compiler_params=params(60),
        cost_estimate=cost(5e10 / CHUNKS, 2e7, 16e6 / CHUNKS),
        name="backward",
    )(*args)


def attn_columns(recv, low):
    heads = [
        jnp.concatenate([recv[2 * h, pl.ds(low, 64), :], recv[2 * h + 1, pl.ds(low, 64), :]], axis=1)
        for h in range(HEADS)
    ]
    return jnp.concatenate(heads, axis=0)


def weight_body(recv, g_ref, unused, send_ref):
    g = g_ref[...]
    for t in range(TILES_DEV):
        term = dot(attn_columns(recv, t * 64), g[t * QROWS : (t + 1) * QROWS])
        total = term if t == 0 else total + term
    total = total.astype(BF16)
    for dest in range(16):
        for j in range(4):
            send_ref[dest, j * 32 : j * 32 + 32, :] = total[
                dest * 32 : dest * 32 + 32, j * 128 : j * 128 + 128
            ]


def weight_grad(recv, g, send):
    rows = TILES_DEV * QROWS
    steps = D // 512
    return pl.pallas_call(
        weight_body,
        grid=(steps,),
        in_specs=[
            pl.BlockSpec((16, QUERY_ROWS, 128), lambda j: (0, 0, 0)),
            pl.BlockSpec((rows, 512), lambda j: (0, j)),
            pl.BlockSpec(memory_space=pl.ANY),
        ],
        out_specs=pl.BlockSpec((16, 128, 128), lambda j: (0, ROWS // 128 + j, 0)),
        out_shape=jax.ShapeDtypeStruct((BANDS, MID_ROWS, 128), BF16),
        input_output_aliases={2: 0},
        compiler_params=params(60),
        cost_estimate=cost(2 * rows * D * HW, 5e6),
        name="weight_grad",
    )(recv, g, send)


def layer_body(recv, w_ref, layer_ref):
    low = pl.multiple_of(pl.program_id(0) * 64, 64)
    layer_ref[...] = dot(attn_columns(recv, low).T, w_ref[...]).astype(BF16)


def layer_output(recv, w):
    rows = TILES_DEV * QROWS
    return pl.pallas_call(
        layer_body,
        grid=(TILES_DEV,),
        in_specs=[
            pl.BlockSpec((16, QUERY_ROWS, 128), lambda t: (0, 0, 0)),
            pl.BlockSpec((HW, D), lambda t: (0, 0)),
        ],
        out_specs=pl.BlockSpec((QROWS, D), lambda t: (t, 0)),
        out_shape=jax.ShapeDtypeStruct((rows, D), BF16),
        compiler_params=params(60),
        cost_estimate=cost(2 * rows * D * HW, 4e6),
        name="layer_output",
    )(recv, w)


def unpack_body(mid, end, dq_ref, dk_ref, dv_ref):
    heads = []
    for head in range(2):
        blocks = []
        for t in range(TILES_DEV):
            for half in range(2):
                blocks.append(end[2 * head + half, t * 64 : t * 64 + 64, :])
        heads.append(jnp.concatenate(blocks, axis=1))
    dq_ref[...] = jnp.concatenate(heads, axis=0).T
    for chunk, part, low in ((0, mid, 0), (1, end, QUERY_ROWS)):
        for j in range(ROWS // 128):
            block = slice(low + j * 128, low + j * 128 + 128)
            take = [part[r, block, :].astype(F32) for r in range(4)]
            x, y = take[0] + take[1], take[2] + take[3]
            at = slice(chunk * ROWS + j * 128, chunk * ROWS + j * 128 + 128)
            dk_ref[at, :] = jnp.concatenate([x[:64], y[:64]], axis=0).astype(BF16).T
            dv_ref[at, :] = jnp.concatenate([x[64:], y[64:]], axis=0).astype(BF16).T


def unpack(mid, end):
    rows = TILES_DEV * QROWS
    return pl.pallas_call(
        unpack_body,
        grid=(4,),
        in_specs=[
            pl.BlockSpec((4, ROWS, 128), lambda p: (p, 0, 0)),
            pl.BlockSpec((4, END_ROWS, 128), lambda p: (p, 0, 0)),
        ],
        out_specs=[
            pl.BlockSpec((rows, 128), lambda p: (0, p)),
            pl.BlockSpec((BT, 128), lambda p: (0, p)),
            pl.BlockSpec((BT, 128), lambda p: (0, p)),
        ],
        out_shape=[
            jax.ShapeDtypeStruct((rows, HW), BF16),
            jax.ShapeDtypeStruct((BT, HW), BF16),
            jax.ShapeDtypeStruct((BT, HW), BF16),
        ],
        compiler_params=params(60),
        cost_estimate=cost(0, 8e6),
        name="unpack",
    )(mid, end)


def swap(x, axes="region"):
    return lax.all_to_all(x, axes, 0, 0, tiled=True)


def orbit_sum(share):
    size = lax.axis_size("orbit")
    total = share.astype(F32)
    for shift in range(1, size):
        total += lax.ppermute(share, "orbit", [(i, (i + shift) % size) for i in range(size)]).astype(F32)
    return total


def per_device(queries, keys, values, block_lists, band_counts, cotangent, out_weight):
    rows = TILES_DEV * QROWS
    q, g = queries.reshape(rows, HW), cotangent.reshape(rows, D)
    k, v = keys.reshape(BT, HW), values.reshape(BT, HW)
    recv = swap(pack(q, k, v, block_lists[0], band_counts))
    lists = recv[:, LIST_ROW : LIST_ROW + TILES_DEV, :MAXB].astype(jnp.int32).reshape(TILES, MAXB)
    counts = recv[:, LIST_ROW + 8, :TILES_DEV].astype(jnp.int32).reshape(TILES)
    plan = plan_of(lists, counts)
    d_attn = dattn(out_weight, g)
    recv, d_attn = lax.optimization_barrier((recv, d_attn))
    d_attn = swap(d_attn).reshape(TILES, 64, HALF)

    attn, lse, kv, kt, qt = forward(plan, recv)
    attn_home = swap(attn.reshape(16, QUERY_ROWS, HALF))
    mid, dq = backward(0, plan, kv, kt, qt, d_attn, attn, lse)
    attn_home, mid = lax.optimization_barrier((attn_home, mid))
    mid = weight_grad(attn_home, g, mid)
    mid, dq = lax.optimization_barrier((mid, dq))
    mid = swap(mid)
    (end,) = backward(1, plan, kv, kt, qt, d_attn, attn, lse, dq)
    mid, end, attn_home = lax.optimization_barrier((mid, end, attn_home))
    end = swap(end)
    share = jnp.sum(mid[:, ROWS:].astype(F32), axis=0).astype(BF16)
    total = orbit_sum(share).astype(BF16)
    total = total.reshape(D // 128, 32, 128).transpose(1, 0, 2).reshape(1, 32, D)
    total = jnp.broadcast_to(total, (16, 32, D))
    layer = layer_output(attn_home, out_weight)
    end, total, layer = lax.optimization_barrier((end, total, layer))
    total = swap(total)
    d_q, d_k, d_v = unpack(mid, end)
    return (
        layer.reshape(1, TILES_DEV, QROWS, D),
        d_q.reshape(1, TILES_DEV, QROWS, HW),
        d_k.reshape(1, 1, BT, HW),
        d_v.reshape(1, 1, BT, HW),
        total.reshape(HW, D).astype(F32),
    )


def solution(mesh):
    four = P("orbit", "region", None, None)
    return jax.shard_map(
        per_device,
        mesh=mesh,
        in_specs=(four, four, four, P("orbit", "region", None), P("orbit", "region"), four, P()),
        out_specs=(four, four, four, four, P()),
        check_vma=False,
    )
```

```python
import functools

import jax
import jax.numpy as jnp
from jax import lax
from jax.experimental import pallas as pl
from jax.experimental.pallas import tpu as pltpu
from jax.sharding import PartitionSpec as P

HEADS = 8
HEAD_DIM = 64
BANDS = 16
BT = 512
QROWS = 256
HALF = 128
TILES_DEV = 3
TILES = 48
MAXB = 8
D = 1024
HW = 512
CHUNKS = 2
UNROLL = 8
BACK_UNROLL = 8
SUB = 64
BACK_SUB = 256
SUM_ROWS = 16
ROWS = BT // CHUNKS
QUERY_ROWS = TILES_DEV * 64
LIST_ROW = BT + QUERY_ROWS
SEND_ROWS = LIST_ROW + 16
DW_ROWS = HW * D // 16 // 128
MID_ROWS = ROWS + DW_ROWS
END_ROWS = QUERY_ROWS + ROWS
PAIRS = 208
SCALE = HEAD_DIM**-0.5
LOW = -1e30
BF16 = jnp.bfloat16
F32 = jnp.float32

NT = (((1,), (1,)), ((), ()))


def dot(a, b, dims=(((1,), (0,)), ((), ()))):
    return lax.dot_general(a, b, dims, preferred_element_type=F32)


def params(mib=56):
    return pltpu.CompilerParams(vmem_limit_bytes=mib << 20)


def cost(flops, nbytes, exps=0):
    return pl.CostEstimate(flops=int(flops), bytes_accessed=int(nbytes), transcendentals=int(exps))


def whole(*shape):
    return pl.BlockSpec(shape, lambda *_: (0,) * len(shape))


SMEM = pl.BlockSpec(memory_space=pltpu.SMEM)


def pack_body(q_ref, k_ref, v_ref, list_ref, count_ref, out_ref, rows_ref):
    rows_ref[...] = jnp.zeros(rows_ref.shape, F32)
    for t in range(TILES_DEV):
        rows_ref[t : t + 1, :MAXB] = list_ref[t].astype(F32)
    rows_ref[8:9, :TILES_DEV] = count_ref[...].astype(F32)
    lists = rows_ref[...].astype(BF16)
    kt = k_ref[...].T
    vt = v_ref[...].T
    qt = (q_ref[...].astype(F32) * SCALE).astype(BF16).T
    for head in range(2):
        rows = slice(head * 64, head * 64 + 64)
        for half in range(2):
            dest = 2 * head + half
            out_ref[dest, LIST_ROW:SEND_ROWS, :] = lists
            for j in range(4):
                lanes = slice(j * 128, j * 128 + 128)
                out_ref[dest, j * 128 : j * 128 + 64, :] = kt[rows, lanes]
                out_ref[dest, j * 128 + 64 : j * 128 + 128, :] = vt[rows, lanes]
            for t in range(TILES_DEV):
                low = t * QROWS + half * HALF
                out_ref[dest, BT + t * 64 : BT + t * 64 + 64, :] = qt[rows, low : low + HALF]


def pack(q, k, v, lists, counts):
    return pl.pallas_call(
        pack_body,
        grid=(4,),
        in_specs=[
            pl.BlockSpec((TILES_DEV * QROWS, 128), lambda p: (0, p)),
            pl.BlockSpec((BT, 128), lambda p: (0, p)),
            pl.BlockSpec((BT, 128), lambda p: (0, p)),
            pl.BlockSpec((TILES_DEV, 1, MAXB), lambda p: (0, 0, 0)),
            pl.BlockSpec((1, TILES_DEV), lambda p: (0, 0)),
        ],
        out_specs=pl.BlockSpec((4, SEND_ROWS, 128), lambda p: (p, 0, 0)),
        out_shape=jax.ShapeDtypeStruct((16, SEND_ROWS, 128), BF16),
        scratch_shapes=[pltpu.VMEM((16, 128), F32)],
        compiler_params=params(60),
        cost_estimate=cost(0, 8e6),
        name="pack",
    )(q, k, v, lists, counts)


def dattn_body(w_ref, g_ref, out_ref):
    dt = dot(w_ref[...], g_ref[...], NT).astype(BF16)
    for head in range(2):
        for half in range(2):
            for t in range(TILES_DEV):
                low = t * QROWS + half * HALF
                out_ref[2 * head + half, t * 64 : t * 64 + 64, :] = dt[
                    head * 64 : head * 64 + 64, low : low + HALF
                ]


def dattn(w, g):
    rows = TILES_DEV * QROWS
    return pl.pallas_call(
        dattn_body,
        grid=(4,),
        in_specs=[
            pl.BlockSpec((128, D), lambda p: (p, 0)),
            pl.BlockSpec((rows, D), lambda p: (0, 0)),
        ],
        out_specs=pl.BlockSpec((4, TILES_DEV * 64, 128), lambda p: (p, 0, 0)),
        out_shape=jax.ShapeDtypeStruct((16, TILES_DEV * 64, 128), BF16),
        compiler_params=params(60),
        cost_estimate=cost(2 * rows * D * HW, 4e6),
        name="dattn",
    )(w, g)


def plan_of(lists, counts):
    slots = jnp.arange(MAXB)[None, :] < counts[:, None]
    member = (
        (lists[:, :, None] == jnp.arange(BANDS)[None, None, :]) & slots[:, :, None]
    ).any(axis=1)
    member = member.T.astype(jnp.int32)
    place = jnp.cumsum(member, axis=1) - member
    size = (member.sum(axis=1) + 1) // 2
    base = jnp.cumsum(size) - size
    flat = base[:, None] + (place >> 1) + (place & 1) * PAIRS
    flat = jnp.where(member > 0, flat, -1)
    hit = flat[None] == jnp.arange(2 * PAIRS)[:, None, None]
    tile = jnp.arange(TILES)[None, None, :]
    band = jnp.arange(BANDS)[None, :, None]
    code = jnp.sum(jnp.where(hit, band * 64 + tile - TILES, 0), axis=(1, 2)) + TILES
    return code.astype(jnp.int32), size.sum().astype(jnp.int32).reshape(1)


def first_of(plan, i):
    return plan[i] & 63


def second_of(plan, i):
    return plan[PAIRS + i] & 63


def band_of(plan, i):
    return plan[i] >> 6


def batched(count, width, body):
    def step(j, carry):
        for k in range(width):
            body(j * width + k)
        return carry

    lax.fori_loop(0, count // width, step, 0)


def forward_body(plan, number, recv, attn_ref, lse_ref, kv_ref, kt_ref, qt_ref, vt, top, acc, s0, s1, p0, p1, h0, h1):
    def unpack_band(b):
        kvt = jnp.concatenate([recv[b, j * 128 : j * 128 + 128, :] for j in range(4)], axis=1)
        kv_ref[b] = kvt.T
        kt_ref[b] = kvt[:64]
        vt[b] = jnp.concatenate([kvt[64:], jnp.ones((SUM_ROWS, BT), BF16)], axis=0)
        for t in range(TILES_DEV):
            qt_ref[b * TILES_DEV + t] = recv[b, BT + t * 64 : BT + t * 64 + 64, :]

    batched(BANDS, 4, unpack_band)
    qt_ref[TILES] = jnp.zeros((64, HALF), BF16)
    top[...] = jnp.full(top.shape, LOW, F32)
    acc[...] = jnp.zeros(acc.shape, F32)
    blank = jnp.zeros((64, 2 * HALF), BF16)

    def scores(i, s, h, weigh=None):
        a, c = first_of(plan, i), second_of(plan, i)
        w = jnp.concatenate([jnp.concatenate([qt_ref[a], qt_ref[c]], axis=1), blank], axis=0)
        peak = None
        for low in range(0, BT, SUB):
            rows = slice(low, low + SUB)
            st = dot(kv_ref[band_of(plan, i), rows, :], w)
            s[rows, :] = st
            high = jnp.max(st.reshape(SUB // 8, 8, 2 * HALF), axis=0)
            peak = high if peak is None else jnp.maximum(peak, high)
            if weigh is not None:
                weigh(rows)
        old = jnp.concatenate([top[a], top[c]], axis=1)
        new = jnp.maximum(old, jnp.max(peak, axis=0, keepdims=True))
        top[a] = new[:, :HALF]
        top[c] = new[:, HALF:]
        h[0:1, :] = new
        h[1:2, :] = jnp.exp(old - new)

    def weigh(s, h, p, rows):
        p[rows, :] = jnp.exp(s[rows, :] - h[0:1, :]).astype(BF16)

    def gather(i, fade, p):
        o = dot(vt[band_of(plan, i)], p[...])
        for x, lanes in ((first_of(plan, i), slice(0, HALF)), (second_of(plan, i), slice(HALF, 2 * HALF))):
            acc[x] = acc[x] * fade[:, lanes] + o[:, lanes]

    scores(0, s0, h0)
    scores(1, s1, h1)
    weigh(s0, h0, p0, slice(0, BT))

    even, odd = (s0, h0, p0), (s1, h1, p1)

    def step(j, carry):
        for k in range(UNROLL):
            i = UNROLL * j + k
            (s, h, p), (s_next, h_next, p_next) = (even, odd) if k % 2 == 0 else (odd, even)
            fade = h[1:2, :]
            scores(i + 2, s, h, functools.partial(weigh, s_next, h_next, p_next))
            gather(i, fade, p)
        return carry

    lax.fori_loop(0, (number[0] + UNROLL - 1) // UNROLL, step, 0)

    def finish(x):
        total = acc[x, 64:65, :]
        attn_ref[x] = (acc[x, :64, :] * (1.0 / total)).astype(BF16)
        lse_ref[x] = top[x] + jnp.log(total)

    batched(TILES, 8, finish)
    lse_ref[TILES] = jnp.full((1, HALF), -LOW, F32)


def forward(plan, recv):
    return pl.pallas_call(
        forward_body,
        grid=(1,),
        in_specs=[SMEM, SMEM, whole(16, SEND_ROWS, 128)],
        out_specs=[
            whole(TILES, 64, HALF),
            whole(TILES + 1, 1, HALF),
            whole(BANDS, BT, 128),
            whole(BANDS, 64, BT),
            whole(TILES + 1, 64, HALF),
        ],
        out_shape=[
            jax.ShapeDtypeStruct((TILES, 64, HALF), BF16),
            jax.ShapeDtypeStruct((TILES + 1, 1, HALF), F32),
            jax.ShapeDtypeStruct((BANDS, BT, 128), BF16),
            jax.ShapeDtypeStruct((BANDS, 64, BT), BF16),
            jax.ShapeDtypeStruct((TILES + 1, 64, HALF), BF16),
        ],
        scratch_shapes=[
            pltpu.VMEM((BANDS, 64 + SUM_ROWS, BT), BF16),
            pltpu.VMEM((TILES + 1, 1, HALF), F32),
            pltpu.VMEM((TILES + 1, 64 + SUM_ROWS, HALF), F32),
            pltpu.VMEM((BT, 2 * HALF), F32),
            pltpu.VMEM((BT, 2 * HALF), F32),
            pltpu.VMEM((BT, 2 * HALF), BF16),
            pltpu.VMEM((BT, 2 * HALF), BF16),
            pltpu.VMEM((8, 2 * HALF), F32),
            pltpu.VMEM((8, 2 * HALF), F32),
        ],
        compiler_params=params(60),
        cost_estimate=cost(2.4e10, 2e7, 16e6),
        name="forward",
    )(*plan, recv)


def backward_body(last, plan, number, kv, kt, qt, dot_, attn, lse, dq_in, send_ref, dq_ref, delta, dkv, dq, s0, t0, s1, t1, p0, d0, p1, d1):
    rows = kv.shape[1]

    def prepare(x):
        delta[x] = jnp.sum(attn[x].astype(F32) * dot_[x].astype(F32), axis=0, keepdims=True)

    batched(TILES, 8, prepare)
    delta[TILES] = jnp.zeros((1, HALF), F32)
    dkv[...] = jnp.zeros(dkv.shape, F32)
    if dq_in is None:
        dq[...] = jnp.zeros(dq.shape, F32)
    else:
        dq[...] = dq_in[...]
    blank = jnp.zeros((64, 2 * HALF), BF16)

    def pair(ref, i):
        return jnp.concatenate([ref[first_of(plan, i)], ref[second_of(plan, i)]], axis=1)

    def pair_g(i):
        a, c = jnp.minimum(first_of(plan, i), TILES - 1), jnp.minimum(second_of(plan, i), TILES - 1)
        return jnp.concatenate([dot_[a], dot_[c]], axis=1)

    def scores(i, s, t, weigh=None):
        wq = jnp.concatenate([pair(qt, i), blank], axis=0)
        wg = jnp.concatenate([blank, pair_g(i)], axis=0)
        for low in range(0, rows, BACK_SUB):
            at = slice(low, low + BACK_SUB)
            band = kv[band_of(plan, i), at, :]
            s[at, :] = dot(band, wq)
            t[at, :] = dot(band, wg)
            if weigh is not None:
                weigh(at)

    def weigh(i, s, t, p_ref, d_ref, at):
        p = jnp.exp(s[at, :] - pair(lse, i))
        p_ref[at, :] = p.astype(BF16)
        d_ref[at, :] = (p * (t[at, :] - pair(delta, i))).astype(BF16)

    def gather(i, p_ref, d_ref):
        a, c, b = first_of(plan, i), second_of(plan, i), band_of(plan, i)
        part = dot(kt[b], d_ref[...])
        dq[a] += part[:, :HALF]
        dq[c] += part[:, HALF:]
        dkv[b, :64, :] += dot(pair(qt, i), d_ref[...], NT)
        dkv[b, 64:, :] += dot(pair_g(i), p_ref[...], NT)

    scores(0, s0, t0)
    scores(1, s1, t1)
    weigh(0, s0, t0, p0, d0, slice(0, rows))

    even, odd = (s0, t0, p0, d0), (s1, t1, p1, d1)

    def step(j, carry):
        for k in range(BACK_UNROLL):
            i = BACK_UNROLL * j + k
            now, later = (even, odd) if k % 2 == 0 else (odd, even)
            scores(i + 2, *now[:2], functools.partial(weigh, i + 1, *later))
            gather(i, *now[2:])
        return carry

    lax.fori_loop(0, (number[0] + BACK_UNROLL - 1) // BACK_UNROLL, step, 0)

    first = QUERY_ROWS if last else 0

    def finish(b):
        for j in range(rows // 128):
            at = first + j * 128
            send_ref[b, at : at + 128, :] = dkv[b, :, j * 128 : j * 128 + 128].astype(BF16)
        if last:
            for t in range(TILES_DEV):
                send_ref[b, t * 64 : t * 64 + 64, :] = (dq[b * TILES_DEV + t] * SCALE).astype(BF16)

    batched(BANDS, 4, finish)
    if not last:
        dq_ref[...] = dq[...]


def backward(chunk, plan, kv, kt, qt, dot_, attn, lse, dq_in=None):
    last = chunk == CHUNKS - 1
    if last:

        def body(*refs):
            return backward_body(True, *refs[:10], None, *refs[10:])
    else:

        def body(*refs):
            return backward_body(False, *refs[:8], None, *refs[8:])

    specs = [
        SMEM,
        SMEM,
        pl.BlockSpec((BANDS, ROWS, 128), lambda i: (0, chunk, 0)),
        pl.BlockSpec((BANDS, 64, ROWS), lambda i: (0, 0, chunk)),
        whole(TILES + 1, 64, HALF),
        whole(TILES, 64, HALF),
        whole(TILES, 64, HALF),
        whole(TILES + 1, 1, HALF),
    ]
    args = [*plan, kv, kt, qt, dot_, attn, lse]
    if last:
        specs.append(whole(TILES + 1, 64, HALF))
        args.append(dq_in)
        out_specs = [whole(BANDS, QUERY_ROWS + ROWS, 128)]
        out_shape = [jax.ShapeDtypeStruct((BANDS, END_ROWS, 128), BF16)]
    else:
        out_specs = [whole(BANDS, ROWS, 128), whole(TILES + 1, 64, HALF)]
        out_shape = [
            jax.ShapeDtypeStruct((BANDS, MID_ROWS, 128), BF16),
            jax.ShapeDtypeStruct((TILES + 1, 64, HALF), F32),
        ]
    return pl.pallas_call(
        body,
        grid=(1,),
        in_specs=specs,
        out_specs=out_specs,
        out_shape=out_shape,
        scratch_shapes=[
            pltpu.VMEM((TILES + 1, 1, HALF), F32),
            pltpu.VMEM((BANDS, 128, ROWS), F32),
            pltpu.VMEM((TILES + 1, 64, HALF), F32),
        ]
        + [pltpu.VMEM((ROWS, 2 * HALF), F32)] * 4
        + [pltpu.VMEM((ROWS, 2 * HALF), BF16)] * 4,
        compiler_params=params(60),
        cost_estimate=cost(5e10 / CHUNKS, 2e7, 16e6 / CHUNKS),
        name="backward",
    )(*args)


def attn_columns(recv, low):
    heads = [
        jnp.concatenate([recv[2 * h, pl.ds(low, 64), :], recv[2 * h + 1, pl.ds(low, 64), :]], axis=1)
        for h in range(HEADS)
    ]
    return jnp.concatenate(heads, axis=0)


def weight_body(recv, g_ref, unused, send_ref):
    g = g_ref[...]
    for t in range(TILES_DEV):
        term = dot(attn_columns(recv, t * 64), g[t * QROWS : (t + 1) * QROWS])
        total = term if t == 0 else total + term
    total = total.astype(BF16)
    for dest in range(16):
        for j in range(4):
            send_ref[dest, j * 32 : j * 32 + 32, :] = total[
                dest * 32 : dest * 32 + 32, j * 128 : j * 128 + 128
            ]


def weight_grad(recv, g, send):
    rows = TILES_DEV * QROWS
    steps = D // 512
    return pl.pallas_call(
        weight_body,
        grid=(steps,),
        in_specs=[
            pl.BlockSpec((16, QUERY_ROWS, 128), lambda j: (0, 0, 0)),
            pl.BlockSpec((rows, 512), lambda j: (0, j)),
            pl.BlockSpec(memory_space=pl.ANY),
        ],
        out_specs=pl.BlockSpec((16, 128, 128), lambda j: (0, ROWS // 128 + j, 0)),
        out_shape=jax.ShapeDtypeStruct((BANDS, MID_ROWS, 128), BF16),
        input_output_aliases={2: 0},
        compiler_params=params(60),
        cost_estimate=cost(2 * rows * D * HW, 5e6),
        name="weight_grad",
    )(recv, g, send)


def layer_body(recv, w_ref, layer_ref):
    low = pl.multiple_of(pl.program_id(0) * 64, 64)
    layer_ref[...] = dot(attn_columns(recv, low).T, w_ref[...]).astype(BF16)


def layer_output(recv, w):
    rows = TILES_DEV * QROWS
    return pl.pallas_call(
        layer_body,
        grid=(TILES_DEV,),
        in_specs=[
            pl.BlockSpec((16, QUERY_ROWS, 128), lambda t: (0, 0, 0)),
            pl.BlockSpec((HW, D), lambda t: (0, 0)),
        ],
        out_specs=pl.BlockSpec((QROWS, D), lambda t: (t, 0)),
        out_shape=jax.ShapeDtypeStruct((rows, D), BF16),
        compiler_params=params(60),
        cost_estimate=cost(2 * rows * D * HW, 4e6),
        name="layer_output",
    )(recv, w)


def unpack_body(mid, end, dq_ref, dk_ref, dv_ref):
    heads = []
    for head in range(2):
        blocks = []
        for t in range(TILES_DEV):
            for half in range(2):
                blocks.append(end[2 * head + half, t * 64 : t * 64 + 64, :])
        heads.append(jnp.concatenate(blocks, axis=1))
    dq_ref[...] = jnp.concatenate(heads, axis=0).T
    for chunk, part, low in ((0, mid, 0), (1, end, QUERY_ROWS)):
        for j in range(ROWS // 128):
            block = slice(low + j * 128, low + j * 128 + 128)
            take = [part[r, block, :].astype(F32) for r in range(4)]
            x, y = take[0] + take[1], take[2] + take[3]
            at = slice(chunk * ROWS + j * 128, chunk * ROWS + j * 128 + 128)
            dk_ref[at, :] = jnp.concatenate([x[:64], y[:64]], axis=0).astype(BF16).T
            dv_ref[at, :] = jnp.concatenate([x[64:], y[64:]], axis=0).astype(BF16).T


def unpack(mid, end):
    rows = TILES_DEV * QROWS
    return pl.pallas_call(
        unpack_body,
        grid=(4,),
        in_specs=[
            pl.BlockSpec((4, ROWS, 128), lambda p: (p, 0, 0)),
            pl.BlockSpec((4, END_ROWS, 128), lambda p: (p, 0, 0)),
        ],
        out_specs=[
            pl.BlockSpec((rows, 128), lambda p: (0, p)),
            pl.BlockSpec((BT, 128), lambda p: (0, p)),
            pl.BlockSpec((BT, 128), lambda p: (0, p)),
        ],
        out_shape=[
            jax.ShapeDtypeStruct((rows, HW), BF16),
            jax.ShapeDtypeStruct((BT, HW), BF16),
            jax.ShapeDtypeStruct((BT, HW), BF16),
        ],
        compiler_params=params(60),
        cost_estimate=cost(0, 8e6),
        name="unpack",
    )(mid, end)


def swap(x, axes="region"):
    return lax.all_to_all(x, axes, 0, 0, tiled=True)


def spread_body(*refs):
    shares, send_ref = refs[:-1], refs[-1]
    total = shares[0][...].astype(F32)
    for share in shares[1:]:
        total = total + share[...].astype(F32)
    total = total.astype(BF16)
    wide = jnp.concatenate([total[j * 32 : j * 32 + 32] for j in range(D // 128)], axis=1)
    for dest in range(16):
        send_ref[dest] = wide


def orbit_sum(share):
    size = lax.axis_size("orbit")
    shares = [share]
    for shift in range(1, size):
        shares.append(lax.ppermute(share, "orbit", [(i, (i + shift) % size) for i in range(size)]))
    return pl.pallas_call(
        spread_body,
        grid=(1,),
        in_specs=[whole(DW_ROWS, 128)] * size,
        out_specs=whole(16, 32, D),
        out_shape=jax.ShapeDtypeStruct((16, 32, D), BF16),
        compiler_params=params(16),
        cost_estimate=cost(0, 4e6),
        name="spread",
    )(*shares)


def per_device(queries, keys, values, block_lists, band_counts, cotangent, out_weight):
    rows = TILES_DEV * QROWS
    q, g = queries.reshape(rows, HW), cotangent.reshape(rows, D)
    k, v = keys.reshape(BT, HW), values.reshape(BT, HW)
    recv = swap(pack(q, k, v, block_lists.transpose(1, 0, 2), band_counts))
    lists = recv[:, LIST_ROW : LIST_ROW + TILES_DEV, :MAXB].astype(jnp.int32).reshape(TILES, MAXB)
    counts = recv[:, LIST_ROW + 8, :TILES_DEV].astype(jnp.int32).reshape(TILES)
    plan = plan_of(lists, counts)
    d_attn = dattn(out_weight, g)
    recv, d_attn = lax.optimization_barrier((recv, d_attn))
    d_attn = swap(d_attn).reshape(TILES, 64, HALF)

    attn, lse, kv, kt, qt = forward(plan, recv)
    attn_home = swap(attn.reshape(16, QUERY_ROWS, HALF))
    mid, dq = backward(0, plan, kv, kt, qt, d_attn, attn, lse)
    attn_home, mid = lax.optimization_barrier((attn_home, mid))
    mid = weight_grad(attn_home, g, mid)
    mid, dq = lax.optimization_barrier((mid, dq))
    mid = swap(mid)
    (end,) = backward(1, plan, kv, kt, qt, d_attn, attn, lse, dq)
    mid, end, attn_home = lax.optimization_barrier((mid, end, attn_home))
    end = swap(end)
    share = jnp.sum(mid[:, ROWS:].astype(F32), axis=0).astype(BF16)
    total = orbit_sum(share)
    layer = layer_output(attn_home, out_weight)
    end, total, layer = lax.optimization_barrier((end, total, layer))
    total = swap(total)
    d_q, d_k, d_v = unpack(mid, end)
    return (
        layer.reshape(1, TILES_DEV, QROWS, D),
        d_q.reshape(1, TILES_DEV, QROWS, HW),
        d_k.reshape(1, 1, BT, HW),
        d_v.reshape(1, 1, BT, HW),
        total.reshape(HW, D).astype(F32),
    )


def solution(mesh):
    four = P("orbit", "region", None, None)
    return jax.shard_map(
        per_device,
        mesh=mesh,
        in_specs=(four, four, four, P("orbit", "region", None), P("orbit", "region"), four, P()),
        out_specs=(four, four, four, four, P()),
        check_vma=False,
    )
```

```python
import functools

import jax
import jax.numpy as jnp
from jax import lax
from jax.experimental import pallas as pl
from jax.experimental.pallas import tpu as pltpu
from jax.sharding import PartitionSpec as P

HEADS = 8
HEAD_DIM = 64
BANDS = 16
BT = 512
QROWS = 256
HALF = 128
TILES_DEV = 3
TILES = 48
MAXB = 8
D = 1024
HW = 512
CHUNKS = 2
UNROLL = 16
BACK_UNROLL = 16
SUB = 128
BACK_SUB = 256
SUM_ROWS = 16
ROWS = BT // CHUNKS
QUERY_ROWS = TILES_DEV * 64
LIST_ROW = BT + QUERY_ROWS
SEND_ROWS = LIST_ROW + 16
DW_ROWS = HW * D // 16 // 128
MID_ROWS = ROWS + DW_ROWS
END_ROWS = QUERY_ROWS + ROWS
PAIRS = 224
SCALE = HEAD_DIM**-0.5
LOW = -1e30
BF16 = jnp.bfloat16
F32 = jnp.float32

NT = (((1,), (1,)), ((), ()))


def dot(a, b, dims=(((1,), (0,)), ((), ()))):
    return lax.dot_general(a, b, dims, preferred_element_type=F32)


def params(mib=56):
    return pltpu.CompilerParams(vmem_limit_bytes=mib << 20)


def cost(flops, nbytes, exps=0):
    return pl.CostEstimate(flops=int(flops), bytes_accessed=int(nbytes), transcendentals=int(exps))


def whole(*shape):
    return pl.BlockSpec(shape, lambda *_: (0,) * len(shape))


SMEM = pl.BlockSpec(memory_space=pltpu.SMEM)


def pack_body(q_ref, k_ref, v_ref, list_ref, count_ref, out_ref, rows_ref):
    rows_ref[...] = jnp.zeros(rows_ref.shape, F32)
    for t in range(TILES_DEV):
        rows_ref[t : t + 1, :MAXB] = list_ref[t].astype(F32)
    rows_ref[8:9, :TILES_DEV] = count_ref[...].astype(F32)
    lists = rows_ref[...].astype(BF16)
    kt = k_ref[...].T
    vt = v_ref[...].T
    qt = (q_ref[...].astype(F32) * SCALE).astype(BF16).T
    for head in range(2):
        rows = slice(head * 64, head * 64 + 64)
        for half in range(2):
            dest = 2 * head + half
            out_ref[dest, LIST_ROW:SEND_ROWS, :] = lists
            for j in range(4):
                lanes = slice(j * 128, j * 128 + 128)
                out_ref[dest, j * 128 : j * 128 + 64, :] = kt[rows, lanes]
                out_ref[dest, j * 128 + 64 : j * 128 + 128, :] = vt[rows, lanes]
            for t in range(TILES_DEV):
                low = t * QROWS + half * HALF
                out_ref[dest, BT + t * 64 : BT + t * 64 + 64, :] = qt[rows, low : low + HALF]


def pack(q, k, v, lists, counts):
    return pl.pallas_call(
        pack_body,
        grid=(4,),
        in_specs=[
            pl.BlockSpec((TILES_DEV * QROWS, 128), lambda p: (0, p)),
            pl.BlockSpec((BT, 128), lambda p: (0, p)),
            pl.BlockSpec((BT, 128), lambda p: (0, p)),
            pl.BlockSpec((TILES_DEV, 1, MAXB), lambda p: (0, 0, 0)),
            pl.BlockSpec((1, TILES_DEV), lambda p: (0, 0)),
        ],
        out_specs=pl.BlockSpec((4, SEND_ROWS, 128), lambda p: (p, 0, 0)),
        out_shape=jax.ShapeDtypeStruct((16, SEND_ROWS, 128), BF16),
        scratch_shapes=[pltpu.VMEM((16, 128), F32)],
        compiler_params=params(60),
        cost_estimate=cost(0, 8e6),
        name="pack",
    )(q, k, v, lists, counts)


def dattn_body(w_ref, g_ref, out_ref):
    dt = dot(w_ref[...], g_ref[...], NT).astype(BF16)
    for head in range(2):
        for half in range(2):
            for t in range(TILES_DEV):
                low = t * QROWS + half * HALF
                out_ref[2 * head + half, t * 64 : t * 64 + 64, :] = dt[
                    head * 64 : head * 64 + 64, low : low + HALF
                ]


def dattn(w, g):
    rows = TILES_DEV * QROWS
    return pl.pallas_call(
        dattn_body,
        grid=(4,),
        in_specs=[
            pl.BlockSpec((128, D), lambda p: (p, 0)),
            pl.BlockSpec((rows, D), lambda p: (0, 0)),
        ],
        out_specs=pl.BlockSpec((4, TILES_DEV * 64, 128), lambda p: (p, 0, 0)),
        out_shape=jax.ShapeDtypeStruct((16, TILES_DEV * 64, 128), BF16),
        compiler_params=params(60),
        cost_estimate=cost(2 * rows * D * HW, 4e6),
        name="dattn",
    )(w, g)


def plan_of(lists, counts):
    slots = jnp.arange(MAXB)[None, :] < counts[:, None]
    member = (
        (lists[:, :, None] == jnp.arange(BANDS)[None, None, :]) & slots[:, :, None]
    ).any(axis=1)
    member = member.T.astype(jnp.int32)
    place = jnp.cumsum(member, axis=1) - member
    size = (member.sum(axis=1) + 1) // 2
    base = jnp.cumsum(size) - size
    flat = base[:, None] + (place >> 1) + (place & 1) * PAIRS
    flat = jnp.where(member > 0, flat, -1)
    hit = flat[None] == jnp.arange(2 * PAIRS)[:, None, None]
    tile = jnp.arange(TILES)[None, None, :]
    band = jnp.arange(BANDS)[None, :, None]
    code = jnp.sum(jnp.where(hit, band * 64 + tile - TILES, 0), axis=(1, 2)) + TILES
    return code.astype(jnp.int32), size.sum().astype(jnp.int32).reshape(1)


def first_of(plan, i):
    return plan[i] & 63


def second_of(plan, i):
    return plan[PAIRS + i] & 63


def band_of(plan, i):
    return plan[i] >> 6


def batched(count, width, body):
    def step(j, carry):
        for k in range(width):
            body(j * width + k)
        return carry

    lax.fori_loop(0, count // width, step, 0)


def forward_body(plan, number, recv, attn_ref, lse_ref, kv_ref, kt_ref, qt_ref, vt, top, acc, s0, s1, p0, p1, h0, h1):
    def unpack_band(b):
        kvt = jnp.concatenate([recv[b, j * 128 : j * 128 + 128, :] for j in range(4)], axis=1)
        kv_ref[b] = kvt.T
        kt_ref[b] = kvt[:64]
        vt[b] = jnp.concatenate([kvt[64:], jnp.ones((SUM_ROWS, BT), BF16)], axis=0)
        for t in range(TILES_DEV):
            qt_ref[b * TILES_DEV + t] = recv[b, BT + t * 64 : BT + t * 64 + 64, :]

    batched(BANDS, 4, unpack_band)
    qt_ref[TILES] = jnp.zeros((64, HALF), BF16)
    top[...] = jnp.full(top.shape, LOW, F32)
    acc[...] = jnp.zeros(acc.shape, F32)
    blank = jnp.zeros((64, 2 * HALF), BF16)

    def scores(i, s, h, weigh=None):
        a, c = first_of(plan, i), second_of(plan, i)
        w = jnp.concatenate([jnp.concatenate([qt_ref[a], qt_ref[c]], axis=1), blank], axis=0)
        peak = None
        for low in range(0, BT, SUB):
            rows = slice(low, low + SUB)
            st = dot(kv_ref[band_of(plan, i), rows, :], w)
            s[rows, :] = st
            high = jnp.max(st.reshape(SUB // 8, 8, 2 * HALF), axis=0)
            peak = high if peak is None else jnp.maximum(peak, high)
            if weigh is not None:
                weigh(rows)
        old = jnp.concatenate([top[a], top[c]], axis=1)
        new = jnp.maximum(old, jnp.max(peak, axis=0, keepdims=True))
        top[a] = new[:, :HALF]
        top[c] = new[:, HALF:]
        h[0:1, :] = new
        h[1:2, :] = jnp.exp(old - new)

    def weigh(s, h, p, rows):
        p[rows, :] = jnp.exp(s[rows, :] - h[0:1, :]).astype(BF16)

    def gather(i, fade, p):
        o = dot(vt[band_of(plan, i)], p[...])
        for x, lanes in ((first_of(plan, i), slice(0, HALF)), (second_of(plan, i), slice(HALF, 2 * HALF))):
            acc[x] = acc[x] * fade[:, lanes] + o[:, lanes]

    scores(0, s0, h0)
    scores(1, s1, h1)
    weigh(s0, h0, p0, slice(0, BT))

    even, odd = (s0, h0, p0), (s1, h1, p1)

    def step(j, carry):
        for k in range(UNROLL):
            i = UNROLL * j + k
            (s, h, p), (s_next, h_next, p_next) = (even, odd) if k % 2 == 0 else (odd, even)
            fade = h[1:2, :]
            scores(i + 2, s, h, functools.partial(weigh, s_next, h_next, p_next))
            gather(i, fade, p)
        return carry

    lax.fori_loop(0, (number[0] + UNROLL - 1) // UNROLL, step, 0)

    def finish(x):
        total = acc[x, 64:65, :]
        attn_ref[x] = (acc[x, :64, :] * (1.0 / total)).astype(BF16)
        lse_ref[x] = top[x] + jnp.log(total)

    batched(TILES, 8, finish)
    lse_ref[TILES] = jnp.full((1, HALF), -LOW, F32)


def forward(plan, recv):
    return pl.pallas_call(
        forward_body,
        grid=(1,),
        in_specs=[SMEM, SMEM, whole(16, SEND_ROWS, 128)],
        out_specs=[
            whole(TILES, 64, HALF),
            whole(TILES + 1, 1, HALF),
            whole(BANDS, BT, 128),
            whole(BANDS, 64, BT),
            whole(TILES + 1, 64, HALF),
        ],
        out_shape=[
            jax.ShapeDtypeStruct((TILES, 64, HALF), BF16),
            jax.ShapeDtypeStruct((TILES + 1, 1, HALF), F32),
            jax.ShapeDtypeStruct((BANDS, BT, 128), BF16),
            jax.ShapeDtypeStruct((BANDS, 64, BT), BF16),
            jax.ShapeDtypeStruct((TILES + 1, 64, HALF), BF16),
        ],
        scratch_shapes=[
            pltpu.VMEM((BANDS, 64 + SUM_ROWS, BT), BF16),
            pltpu.VMEM((TILES + 1, 1, HALF), F32),
            pltpu.VMEM((TILES + 1, 64 + SUM_ROWS, HALF), F32),
            pltpu.VMEM((BT, 2 * HALF), F32),
            pltpu.VMEM((BT, 2 * HALF), F32),
            pltpu.VMEM((BT, 2 * HALF), BF16),
            pltpu.VMEM((BT, 2 * HALF), BF16),
            pltpu.VMEM((8, 2 * HALF), F32),
            pltpu.VMEM((8, 2 * HALF), F32),
        ],
        compiler_params=params(60),
        cost_estimate=cost(2.4e10, 2e7, 16e6),
        name="forward",
    )(*plan, recv)


def backward_body(last, plan, number, kv, kt, qt, dot_, attn, lse, dq_in, send_ref, dq_ref, delta, dkv, dq, s0, t0, s1, t1, p0, d0, p1, d1):
    rows = kv.shape[1]

    def prepare(x):
        delta[x] = jnp.sum(attn[x].astype(F32) * dot_[x].astype(F32), axis=0, keepdims=True)

    batched(TILES, 8, prepare)
    delta[TILES] = jnp.zeros((1, HALF), F32)
    dkv[...] = jnp.zeros(dkv.shape, F32)
    if dq_in is None:
        dq[...] = jnp.zeros(dq.shape, F32)
    else:
        dq[...] = dq_in[...]
    blank = jnp.zeros((64, 2 * HALF), BF16)

    def pair(ref, i):
        return jnp.concatenate([ref[first_of(plan, i)], ref[second_of(plan, i)]], axis=1)

    def pair_g(i):
        a, c = jnp.minimum(first_of(plan, i), TILES - 1), jnp.minimum(second_of(plan, i), TILES - 1)
        return jnp.concatenate([dot_[a], dot_[c]], axis=1)

    def scores(i, s, t, weigh=None):
        wq = jnp.concatenate([pair(qt, i), blank], axis=0)
        wg = jnp.concatenate([blank, pair_g(i)], axis=0)
        for low in range(0, rows, BACK_SUB):
            at = slice(low, low + BACK_SUB)
            band = kv[band_of(plan, i), at, :]
            s[at, :] = dot(band, wq)
            t[at, :] = dot(band, wg)
            if weigh is not None:
                weigh(at)

    def weigh(i, s, t, p_ref, d_ref, at):
        p = jnp.exp(s[at, :] - pair(lse, i))
        p_ref[at, :] = p.astype(BF16)
        d_ref[at, :] = (p * (t[at, :] - pair(delta, i))).astype(BF16)

    def gather(i, p_ref, d_ref):
        a, c, b = first_of(plan, i), second_of(plan, i), band_of(plan, i)
        part = dot(kt[b], d_ref[...])
        dq[a] += part[:, :HALF]
        dq[c] += part[:, HALF:]
        dkv[b, :64, :] += dot(pair(qt, i), d_ref[...], NT)
        dkv[b, 64:, :] += dot(pair_g(i), p_ref[...], NT)

    scores(0, s0, t0)
    scores(1, s1, t1)
    weigh(0, s0, t0, p0, d0, slice(0, rows))

    even, odd = (s0, t0, p0, d0), (s1, t1, p1, d1)

    def step(j, carry):
        for k in range(BACK_UNROLL):
            i = BACK_UNROLL * j + k
            now, later = (even, odd) if k % 2 == 0 else (odd, even)
            scores(i + 2, *now[:2], functools.partial(weigh, i + 1, *later))
            gather(i, *now[2:])
        return carry

    lax.fori_loop(0, (number[0] + BACK_UNROLL - 1) // BACK_UNROLL, step, 0)

    first = QUERY_ROWS if last else 0

    def finish(b):
        for j in range(rows // 128):
            at = first + j * 128
            send_ref[b, at : at + 128, :] = dkv[b, :, j * 128 : j * 128 + 128].astype(BF16)
        if last:
            for t in range(TILES_DEV):
                send_ref[b, t * 64 : t * 64 + 64, :] = (dq[b * TILES_DEV + t] * SCALE).astype(BF16)

    batched(BANDS, 4, finish)
    if not last:
        dq_ref[...] = dq[...]


def backward(chunk, plan, kv, kt, qt, dot_, attn, lse, dq_in=None):
    last = chunk == CHUNKS - 1
    if last:

        def body(*refs):
            return backward_body(True, *refs[:10], None, *refs[10:])
    else:

        def body(*refs):
            return backward_body(False, *refs[:8], None, *refs[8:])

    specs = [
        SMEM,
        SMEM,
        pl.BlockSpec((BANDS, ROWS, 128), lambda i: (0, chunk, 0)),
        pl.BlockSpec((BANDS, 64, ROWS), lambda i: (0, 0, chunk)),
        whole(TILES + 1, 64, HALF),
        whole(TILES, 64, HALF),
        whole(TILES, 64, HALF),
        whole(TILES + 1, 1, HALF),
    ]
    args = [*plan, kv, kt, qt, dot_, attn, lse]
    if last:
        specs.append(whole(TILES + 1, 64, HALF))
        args.append(dq_in)
        out_specs = [whole(BANDS, QUERY_ROWS + ROWS, 128)]
        out_shape = [jax.ShapeDtypeStruct((BANDS, END_ROWS, 128), BF16)]
    else:
        out_specs = [whole(BANDS, ROWS, 128), whole(TILES + 1, 64, HALF)]
        out_shape = [
            jax.ShapeDtypeStruct((BANDS, MID_ROWS, 128), BF16),
            jax.ShapeDtypeStruct((TILES + 1, 64, HALF), F32),
        ]
    return pl.pallas_call(
        body,
        grid=(1,),
        in_specs=specs,
        out_specs=out_specs,
        out_shape=out_shape,
        scratch_shapes=[
            pltpu.VMEM((TILES + 1, 1, HALF), F32),
            pltpu.VMEM((BANDS, 128, ROWS), F32),
            pltpu.VMEM((TILES + 1, 64, HALF), F32),
        ]
        + [pltpu.VMEM((ROWS, 2 * HALF), F32)] * 4
        + [pltpu.VMEM((ROWS, 2 * HALF), BF16)] * 4,
        compiler_params=params(60),
        cost_estimate=cost(5e10 / CHUNKS, 2e7, 16e6 / CHUNKS),
        name="backward",
    )(*args)


def attn_columns(recv, low):
    heads = [
        jnp.concatenate([recv[2 * h, pl.ds(low, 64), :], recv[2 * h + 1, pl.ds(low, 64), :]], axis=1)
        for h in range(HEADS)
    ]
    return jnp.concatenate(heads, axis=0)


def weight_body(recv, g_ref, unused, send_ref):
    g = g_ref[...]
    for t in range(TILES_DEV):
        term = dot(attn_columns(recv, t * 64), g[t * QROWS : (t + 1) * QROWS])
        total = term if t == 0 else total + term
    total = total.astype(BF16)
    for dest in range(16):
        for j in range(4):
            send_ref[dest, j * 32 : j * 32 + 32, :] = total[
                dest * 32 : dest * 32 + 32, j * 128 : j * 128 + 128
            ]


def weight_grad(recv, g, send):
    rows = TILES_DEV * QROWS
    steps = D // 512
    return pl.pallas_call(
        weight_body,
        grid=(steps,),
        in_specs=[
            pl.BlockSpec((16, QUERY_ROWS, 128), lambda j: (0, 0, 0)),
            pl.BlockSpec((rows, 512), lambda j: (0, j)),
            pl.BlockSpec(memory_space=pl.ANY),
        ],
        out_specs=pl.BlockSpec((16, 128, 128), lambda j: (0, ROWS // 128 + j, 0)),
        out_shape=jax.ShapeDtypeStruct((BANDS, MID_ROWS, 128), BF16),
        input_output_aliases={2: 0},
        compiler_params=params(60),
        cost_estimate=cost(2 * rows * D * HW, 5e6),
        name="weight_grad",
    )(recv, g, send)


def layer_body(recv, w_ref, layer_ref):
    low = pl.multiple_of(pl.program_id(0) * 64, 64)
    layer_ref[...] = dot(attn_columns(recv, low).T, w_ref[...]).astype(BF16)


def layer_output(recv, w):
    rows = TILES_DEV * QROWS
    return pl.pallas_call(
        layer_body,
        grid=(TILES_DEV,),
        in_specs=[
            pl.BlockSpec((16, QUERY_ROWS, 128), lambda t: (0, 0, 0)),
            pl.BlockSpec((HW, D), lambda t: (0, 0)),
        ],
        out_specs=pl.BlockSpec((QROWS, D), lambda t: (t, 0)),
        out_shape=jax.ShapeDtypeStruct((rows, D), BF16),
        compiler_params=params(60),
        cost_estimate=cost(2 * rows * D * HW, 4e6),
        name="layer_output",
    )(recv, w)


def unpack_body(mid, end, dq_ref, dk_ref, dv_ref):
    heads = []
    for head in range(2):
        blocks = []
        for t in range(TILES_DEV):
            for half in range(2):
                blocks.append(end[2 * head + half, t * 64 : t * 64 + 64, :])
        heads.append(jnp.concatenate(blocks, axis=1))
    dq_ref[...] = jnp.concatenate(heads, axis=0).T
    for chunk, part, low in ((0, mid, 0), (1, end, QUERY_ROWS)):
        for j in range(ROWS // 128):
            block = slice(low + j * 128, low + j * 128 + 128)
            take = [part[r, block, :].astype(F32) for r in range(4)]
            x, y = take[0] + take[1], take[2] + take[3]
            at = slice(chunk * ROWS + j * 128, chunk * ROWS + j * 128 + 128)
            dk_ref[at, :] = jnp.concatenate([x[:64], y[:64]], axis=0).astype(BF16).T
            dv_ref[at, :] = jnp.concatenate([x[64:], y[64:]], axis=0).astype(BF16).T


def unpack(mid, end):
    rows = TILES_DEV * QROWS
    return pl.pallas_call(
        unpack_body,
        grid=(4,),
        in_specs=[
            pl.BlockSpec((4, ROWS, 128), lambda p: (p, 0, 0)),
            pl.BlockSpec((4, END_ROWS, 128), lambda p: (p, 0, 0)),
        ],
        out_specs=[
            pl.BlockSpec((rows, 128), lambda p: (0, p)),
            pl.BlockSpec((BT, 128), lambda p: (0, p)),
            pl.BlockSpec((BT, 128), lambda p: (0, p)),
        ],
        out_shape=[
            jax.ShapeDtypeStruct((rows, HW), BF16),
            jax.ShapeDtypeStruct((BT, HW), BF16),
            jax.ShapeDtypeStruct((BT, HW), BF16),
        ],
        compiler_params=params(60),
        cost_estimate=cost(0, 8e6),
        name="unpack",
    )(mid, end)


def swap(x, axes="region"):
    return lax.all_to_all(x, axes, 0, 0, tiled=True)


def spread_body(*refs):
    shares, send_ref = refs[:-1], refs[-1]
    total = shares[0][...].astype(F32)
    for share in shares[1:]:
        total = total + share[...].astype(F32)
    total = total.astype(BF16)
    wide = jnp.concatenate([total[j * 32 : j * 32 + 32] for j in range(D // 128)], axis=1)
    for dest in range(16):
        send_ref[dest] = wide


def orbit_sum(share):
    size = lax.axis_size("orbit")
    shares = [share]
    for shift in range(1, size):
        shares.append(lax.ppermute(share, "orbit", [(i, (i + shift) % size) for i in range(size)]))
    return pl.pallas_call(
        spread_body,
        grid=(1,),
        in_specs=[whole(DW_ROWS, 128)] * size,
        out_specs=whole(16, 32, D),
        out_shape=jax.ShapeDtypeStruct((16, 32, D), BF16),
        compiler_params=params(16),
        cost_estimate=cost(0, 4e6),
        name="spread",
    )(*shares)


def per_device(queries, keys, values, block_lists, band_counts, cotangent, out_weight):
    rows = TILES_DEV * QROWS
    q, g = queries.reshape(rows, HW), cotangent.reshape(rows, D)
    k, v = keys.reshape(BT, HW), values.reshape(BT, HW)
    recv = swap(pack(q, k, v, block_lists.transpose(1, 0, 2), band_counts))
    lists = recv[:, LIST_ROW : LIST_ROW + TILES_DEV, :MAXB].astype(jnp.int32).reshape(TILES, MAXB)
    counts = recv[:, LIST_ROW + 8, :TILES_DEV].astype(jnp.int32).reshape(TILES)
    plan = plan_of(lists, counts)
    d_attn = dattn(out_weight, g)
    recv, d_attn = lax.optimization_barrier((recv, d_attn))
    d_attn = swap(d_attn).reshape(TILES, 64, HALF)

    attn, lse, kv, kt, qt = forward(plan, recv)
    attn_home = swap(attn.reshape(16, QUERY_ROWS, HALF))
    mid, dq = backward(0, plan, kv, kt, qt, d_attn, attn, lse)
    attn_home, mid = lax.optimization_barrier((attn_home, mid))
    mid = weight_grad(attn_home, g, mid)
    mid, dq = lax.optimization_barrier((mid, dq))
    mid = swap(mid)
    (end,) = backward(1, plan, kv, kt, qt, d_attn, attn, lse, dq)
    mid, end, attn_home = lax.optimization_barrier((mid, end, attn_home))
    end = swap(end)
    share = jnp.sum(mid[:, ROWS:].astype(F32), axis=0).astype(BF16)
    total = orbit_sum(share)
    layer = layer_output(attn_home, out_weight)
    end, total, layer = lax.optimization_barrier((end, total, layer))
    total = swap(total)
    d_q, d_k, d_v = unpack(mid, end)
    return (
        layer.reshape(1, TILES_DEV, QROWS, D),
        d_q.reshape(1, TILES_DEV, QROWS, HW),
        d_k.reshape(1, 1, BT, HW),
        d_v.reshape(1, 1, BT, HW),
        total.reshape(HW, D).astype(F32),
    )


def solution(mesh):
    four = P("orbit", "region", None, None)
    return jax.shard_map(
        per_device,
        mesh=mesh,
        in_specs=(four, four, four, P("orbit", "region", None), P("orbit", "region"), four, P()),
        out_specs=(four, four, four, four, P()),
        check_vma=False,
    )
```

```python
import functools

import jax
import jax.numpy as jnp
from jax import lax
from jax.experimental import pallas as pl
from jax.experimental.pallas import tpu as pltpu
from jax.sharding import PartitionSpec as P

HEADS = 8
HEAD_DIM = 64
BANDS = 16
BT = 512
QROWS = 256
HALF = 128
TILES_DEV = 3
TILES = 48
MAXB = 8
D = 1024
HW = 512
CHUNKS = 2
UNROLL = 16
BACK_UNROLL = 8
SUB = 128
BACK_SUB = 256
SUM_ROWS = 16
ROWS = BT // CHUNKS
QUERY_ROWS = TILES_DEV * 64
LIST_ROW = BT + QUERY_ROWS
SEND_ROWS = LIST_ROW + 16
DW_ROWS = HW * D // 16 // 128
MID_ROWS = ROWS + DW_ROWS
END_ROWS = QUERY_ROWS + ROWS
PAIRS = 224
SCALE = HEAD_DIM**-0.5
LOW = -1e30
BF16 = jnp.bfloat16
F32 = jnp.float32

NT = (((1,), (1,)), ((), ()))


def dot(a, b, dims=(((1,), (0,)), ((), ()))):
    return lax.dot_general(a, b, dims, preferred_element_type=F32)


def params(mib=56):
    return pltpu.CompilerParams(vmem_limit_bytes=mib << 20)


def cost(flops, nbytes, exps=0):
    return pl.CostEstimate(flops=int(flops), bytes_accessed=int(nbytes), transcendentals=int(exps))


def whole(*shape):
    return pl.BlockSpec(shape, lambda *_: (0,) * len(shape))


SMEM = pl.BlockSpec(memory_space=pltpu.SMEM)


def pack_body(q_ref, k_ref, v_ref, list_ref, count_ref, out_ref, rows_ref):
    rows_ref[...] = jnp.zeros(rows_ref.shape, F32)
    for t in range(TILES_DEV):
        rows_ref[t : t + 1, :MAXB] = list_ref[t].astype(F32)
    rows_ref[8:9, :TILES_DEV] = count_ref[...].astype(F32)
    lists = rows_ref[...].astype(BF16)
    kt = k_ref[...].T
    vt = v_ref[...].T
    qt = (q_ref[...].astype(F32) * SCALE).astype(BF16).T
    for head in range(2):
        rows = slice(head * 64, head * 64 + 64)
        for half in range(2):
            dest = 2 * head + half
            out_ref[dest, LIST_ROW:SEND_ROWS, :] = lists
            for j in range(4):
                lanes = slice(j * 128, j * 128 + 128)
                out_ref[dest, j * 128 : j * 128 + 64, :] = kt[rows, lanes]
                out_ref[dest, j * 128 + 64 : j * 128 + 128, :] = vt[rows, lanes]
            for t in range(TILES_DEV):
                low = t * QROWS + half * HALF
                out_ref[dest, BT + t * 64 : BT + t * 64 + 64, :] = qt[rows, low : low + HALF]


def pack(q, k, v, lists, counts):
    return pl.pallas_call(
        pack_body,
        grid=(4,),
        in_specs=[
            pl.BlockSpec((TILES_DEV * QROWS, 128), lambda p: (0, p)),
            pl.BlockSpec((BT, 128), lambda p: (0, p)),
            pl.BlockSpec((BT, 128), lambda p: (0, p)),
            pl.BlockSpec((TILES_DEV, 1, MAXB), lambda p: (0, 0, 0)),
            pl.BlockSpec((1, TILES_DEV), lambda p: (0, 0)),
        ],
        out_specs=pl.BlockSpec((4, SEND_ROWS, 128), lambda p: (p, 0, 0)),
        out_shape=jax.ShapeDtypeStruct((16, SEND_ROWS, 128), BF16),
        scratch_shapes=[pltpu.VMEM((16, 128), F32)],
        compiler_params=params(60),
        cost_estimate=cost(0, 8e6),
        name="pack",
    )(q, k, v, lists, counts)


def dattn_body(w_ref, g_ref, out_ref):
    dt = dot(w_ref[...], g_ref[...], NT).astype(BF16)
    for head in range(2):
        for half in range(2):
            for t in range(TILES_DEV):
                low = t * QROWS + half * HALF
                out_ref[2 * head + half, t * 64 : t * 64 + 64, :] = dt[
                    head * 64 : head * 64 + 64, low : low + HALF
                ]


def dattn(w, g):
    rows = TILES_DEV * QROWS
    return pl.pallas_call(
        dattn_body,
        grid=(4,),
        in_specs=[
            pl.BlockSpec((128, D), lambda p: (p, 0)),
            pl.BlockSpec((rows, D), lambda p: (0, 0)),
        ],
        out_specs=pl.BlockSpec((4, TILES_DEV * 64, 128), lambda p: (p, 0, 0)),
        out_shape=jax.ShapeDtypeStruct((16, TILES_DEV * 64, 128), BF16),
        compiler_params=params(60),
        cost_estimate=cost(2 * rows * D * HW, 4e6),
        name="dattn",
    )(w, g)


def plan_of(lists, counts):
    slots = jnp.arange(MAXB)[None, :] < counts[:, None]
    member = (
        (lists[:, :, None] == jnp.arange(BANDS)[None, None, :]) & slots[:, :, None]
    ).any(axis=1)
    member = member.T.astype(jnp.int32)
    place = jnp.cumsum(member, axis=1) - member
    size = (member.sum(axis=1) + 1) // 2
    base = jnp.cumsum(size) - size
    flat = base[:, None] + (place >> 1) + (place & 1) * PAIRS
    flat = jnp.where(member > 0, flat, -1)
    hit = flat[None] == jnp.arange(2 * PAIRS)[:, None, None]
    tile = jnp.arange(TILES)[None, None, :]
    band = jnp.arange(BANDS)[None, :, None]
    code = jnp.sum(jnp.where(hit, band * 64 + tile - TILES, 0), axis=(1, 2)) + TILES
    return code.astype(jnp.int32), size.sum().astype(jnp.int32).reshape(1)


def first_of(plan, i):
    return plan[i] & 63


def second_of(plan, i):
    return plan[PAIRS + i] & 63


def band_of(plan, i):
    return plan[i] >> 6


def batched(count, width, body):
    def step(j, carry):
        for k in range(width):
            body(j * width + k)
        return carry

    lax.fori_loop(0, count // width, step, 0)


def forward_body(plan, number, recv, attn_ref, lse_ref, kv_ref, kt_ref, qt_ref, vt, top, acc, s0, s1, p0, p1, h0, h1):
    def unpack_band(b):
        kvt = jnp.concatenate([recv[b, j * 128 : j * 128 + 128, :] for j in range(4)], axis=1)
        kv_ref[b] = kvt.T
        kt_ref[b] = kvt[:64]
        vt[b] = jnp.concatenate([kvt[64:], jnp.ones((SUM_ROWS, BT), BF16)], axis=0)
        for t in range(TILES_DEV):
            qt_ref[b * TILES_DEV + t] = recv[b, BT + t * 64 : BT + t * 64 + 64, :]

    batched(BANDS, 4, unpack_band)
    qt_ref[TILES] = jnp.zeros((64, HALF), BF16)
    top[...] = jnp.full(top.shape, LOW, F32)
    acc[...] = jnp.zeros(acc.shape, F32)
    blank = jnp.zeros((64, 2 * HALF), BF16)

    def scores(i, s, h, weigh=None):
        a, c = first_of(plan, i), second_of(plan, i)
        w = jnp.concatenate([jnp.concatenate([qt_ref[a], qt_ref[c]], axis=1), blank], axis=0)
        peak = None
        for low in range(0, BT, SUB):
            rows = slice(low, low + SUB)
            st = dot(kv_ref[band_of(plan, i), rows, :], w)
            s[rows, :] = st
            high = jnp.max(st.reshape(SUB // 8, 8, 2 * HALF), axis=0)
            peak = high if peak is None else jnp.maximum(peak, high)
            if weigh is not None:
                weigh(rows)
        old = jnp.concatenate([top[a], top[c]], axis=1)
        new = jnp.maximum(old, jnp.max(peak, axis=0, keepdims=True))
        top[a] = new[:, :HALF]
        top[c] = new[:, HALF:]
        h[0:1, :] = new
        h[1:2, :] = jnp.exp(old - new)

    def weigh(s, h, p, rows):
        p[rows, :] = jnp.exp(s[rows, :] - h[0:1, :]).astype(BF16)

    def gather(i, fade, p):
        o = dot(vt[band_of(plan, i)], p[...])
        for x, lanes in ((first_of(plan, i), slice(0, HALF)), (second_of(plan, i), slice(HALF, 2 * HALF))):
            acc[x] = acc[x] * fade[:, lanes] + o[:, lanes]

    scores(0, s0, h0)
    scores(1, s1, h1)
    weigh(s0, h0, p0, slice(0, BT))

    even, odd = (s0, h0, p0), (s1, h1, p1)

    def step(j, carry):
        for k in range(UNROLL):
            i = UNROLL * j + k
            (s, h, p), (s_next, h_next, p_next) = (even, odd) if k % 2 == 0 else (odd, even)
            fade = h[1:2, :]
            scores(i + 2, s, h, functools.partial(weigh, s_next, h_next, p_next))
            gather(i, fade, p)
        return carry

    lax.fori_loop(0, (number[0] + UNROLL - 1) // UNROLL, step, 0)

    def finish(x):
        total = acc[x, 64:65, :]
        attn_ref[x] = (acc[x, :64, :] * (1.0 / total)).astype(BF16)
        lse_ref[x] = top[x] + jnp.log(total)

    batched(TILES, 8, finish)
    lse_ref[TILES] = jnp.full((1, HALF), -LOW, F32)


def forward(plan, recv):
    return pl.pallas_call(
        forward_body,
        grid=(1,),
        in_specs=[SMEM, SMEM, whole(16, SEND_ROWS, 128)],
        out_specs=[
            whole(TILES, 64, HALF),
            whole(TILES + 1, 1, HALF),
            whole(BANDS, BT, 128),
            whole(BANDS, 64, BT),
            whole(TILES + 1, 64, HALF),
        ],
        out_shape=[
            jax.ShapeDtypeStruct((TILES, 64, HALF), BF16),
            jax.ShapeDtypeStruct((TILES + 1, 1, HALF), F32),
            jax.ShapeDtypeStruct((BANDS, BT, 128), BF16),
            jax.ShapeDtypeStruct((BANDS, 64, BT), BF16),
            jax.ShapeDtypeStruct((TILES + 1, 64, HALF), BF16),
        ],
        scratch_shapes=[
            pltpu.VMEM((BANDS, 64 + SUM_ROWS, BT), BF16),
            pltpu.VMEM((TILES + 1, 1, HALF), F32),
            pltpu.VMEM((TILES + 1, 64 + SUM_ROWS, HALF), F32),
            pltpu.VMEM((BT, 2 * HALF), F32),
            pltpu.VMEM((BT, 2 * HALF), F32),
            pltpu.VMEM((BT, 2 * HALF), BF16),
            pltpu.VMEM((BT, 2 * HALF), BF16),
            pltpu.VMEM((8, 2 * HALF), F32),
            pltpu.VMEM((8, 2 * HALF), F32),
        ],
        compiler_params=params(60),
        cost_estimate=cost(2.4e10, 2e7, 16e6),
        name="forward",
    )(*plan, recv)


def backward_body(last, plan, number, kv, kt, qt, dot_, attn, lse, dq_in, send_ref, dq_ref, delta, dkv, dq, s0, t0, s1, t1, p0, d0, p1, d1):
    rows = kv.shape[1]

    def prepare(x):
        delta[x] = jnp.sum(attn[x].astype(F32) * dot_[x].astype(F32), axis=0, keepdims=True)

    batched(TILES, 8, prepare)
    delta[TILES] = jnp.zeros((1, HALF), F32)
    dkv[...] = jnp.zeros(dkv.shape, F32)
    if dq_in is None:
        dq[...] = jnp.zeros(dq.shape, F32)
    else:
        dq[...] = dq_in[...]
    blank = jnp.zeros((64, 2 * HALF), BF16)

    def pair(ref, i):
        return jnp.concatenate([ref[first_of(plan, i)], ref[second_of(plan, i)]], axis=1)

    def pair_g(i):
        a, c = jnp.minimum(first_of(plan, i), TILES - 1), jnp.minimum(second_of(plan, i), TILES - 1)
        return jnp.concatenate([dot_[a], dot_[c]], axis=1)

    def scores(i, s, t, weigh=None):
        wq = jnp.concatenate([pair(qt, i), blank], axis=0)
        wg = jnp.concatenate([blank, pair_g(i)], axis=0)
        for low in range(0, rows, BACK_SUB):
            at = slice(low, low + BACK_SUB)
            band = kv[band_of(plan, i), at, :]
            s[at, :] = dot(band, wq)
            t[at, :] = dot(band, wg)
            if weigh is not None:
                weigh(at)

    def weigh(i, s, t, p_ref, d_ref, at):
        p = jnp.exp(s[at, :] - pair(lse, i))
        p_ref[at, :] = p.astype(BF16)
        d_ref[at, :] = (p * (t[at, :] - pair(delta, i))).astype(BF16)

    def gather(i, p_ref, d_ref):
        a, c, b = first_of(plan, i), second_of(plan, i), band_of(plan, i)
        part = dot(kt[b], d_ref[...])
        dq[a] += part[:, :HALF]
        dq[c] += part[:, HALF:]
        dkv[b, :64, :] += dot(pair(qt, i), d_ref[...], NT)
        dkv[b, 64:, :] += dot(pair_g(i), p_ref[...], NT)

    scores(0, s0, t0)
    scores(1, s1, t1)
    weigh(0, s0, t0, p0, d0, slice(0, rows))

    even, odd = (s0, t0, p0, d0), (s1, t1, p1, d1)

    def step(j, carry):
        for k in range(BACK_UNROLL):
            i = BACK_UNROLL * j + k
            now, later = (even, odd) if k % 2 == 0 else (odd, even)
            scores(i + 2, *now[:2], functools.partial(weigh, i + 1, *later))
            gather(i, *now[2:])
        return carry

    lax.fori_loop(0, (number[0] + BACK_UNROLL - 1) // BACK_UNROLL, step, 0)

    first = QUERY_ROWS if last else 0

    def finish(b):
        for j in range(rows // 128):
            at = first + j * 128
            send_ref[b, at : at + 128, :] = dkv[b, :, j * 128 : j * 128 + 128].astype(BF16)
        if last:
            for t in range(TILES_DEV):
                send_ref[b, t * 64 : t * 64 + 64, :] = (dq[b * TILES_DEV + t] * SCALE).astype(BF16)

    batched(BANDS, 4, finish)
    if not last:
        dq_ref[...] = dq[...]


def backward(chunk, plan, kv, kt, qt, dot_, attn, lse, dq_in=None):
    last = chunk == CHUNKS - 1
    if last:

        def body(*refs):
            return backward_body(True, *refs[:10], None, *refs[10:])
    else:

        def body(*refs):
            return backward_body(False, *refs[:8], None, *refs[8:])

    specs = [
        SMEM,
        SMEM,
        pl.BlockSpec((BANDS, ROWS, 128), lambda i: (0, chunk, 0)),
        pl.BlockSpec((BANDS, 64, ROWS), lambda i: (0, 0, chunk)),
        whole(TILES + 1, 64, HALF),
        whole(TILES, 64, HALF),
        whole(TILES, 64, HALF),
        whole(TILES + 1, 1, HALF),
    ]
    args = [*plan, kv, kt, qt, dot_, attn, lse]
    if last:
        specs.append(whole(TILES + 1, 64, HALF))
        args.append(dq_in)
        out_specs = [whole(BANDS, QUERY_ROWS + ROWS, 128)]
        out_shape = [jax.ShapeDtypeStruct((BANDS, END_ROWS, 128), BF16)]
    else:
        out_specs = [whole(BANDS, ROWS, 128), whole(TILES + 1, 64, HALF)]
        out_shape = [
            jax.ShapeDtypeStruct((BANDS, MID_ROWS, 128), BF16),
            jax.ShapeDtypeStruct((TILES + 1, 64, HALF), F32),
        ]
    return pl.pallas_call(
        body,
        grid=(1,),
        in_specs=specs,
        out_specs=out_specs,
        out_shape=out_shape,
        scratch_shapes=[
            pltpu.VMEM((TILES + 1, 1, HALF), F32),
            pltpu.VMEM((BANDS, 128, ROWS), F32),
            pltpu.VMEM((TILES + 1, 64, HALF), F32),
        ]
        + [pltpu.VMEM((ROWS, 2 * HALF), F32)] * 4
        + [pltpu.VMEM((ROWS, 2 * HALF), BF16)] * 4,
        compiler_params=params(60),
        cost_estimate=cost(5e10 / CHUNKS, 2e7, 16e6 / CHUNKS),
        name="backward",
    )(*args)


def attn_columns(recv, low):
    heads = [
        jnp.concatenate([recv[2 * h, pl.ds(low, 64), :], recv[2 * h + 1, pl.ds(low, 64), :]], axis=1)
        for h in range(HEADS)
    ]
    return jnp.concatenate(heads, axis=0)


def weight_body(recv, g_ref, unused, send_ref):
    g = g_ref[...]
    for t in range(TILES_DEV):
        term = dot(attn_columns(recv, t * 64), g[t * QROWS : (t + 1) * QROWS])
        total = term if t == 0 else total + term
    total = total.astype(BF16)
    for dest in range(16):
        for j in range(4):
            send_ref[dest, j * 32 : j * 32 + 32, :] = total[
                dest * 32 : dest * 32 + 32, j * 128 : j * 128 + 128
            ]


def weight_grad(recv, g, send):
    rows = TILES_DEV * QROWS
    steps = D // 512
    return pl.pallas_call(
        weight_body,
        grid=(steps,),
        in_specs=[
            pl.BlockSpec((16, QUERY_ROWS, 128), lambda j: (0, 0, 0)),
            pl.BlockSpec((rows, 512), lambda j: (0, j)),
            pl.BlockSpec(memory_space=pl.ANY),
        ],
        out_specs=pl.BlockSpec((16, 128, 128), lambda j: (0, ROWS // 128 + j, 0)),
        out_shape=jax.ShapeDtypeStruct((BANDS, MID_ROWS, 128), BF16),
        input_output_aliases={2: 0},
        compiler_params=params(60),
        cost_estimate=cost(2 * rows * D * HW, 5e6),
        name="weight_grad",
    )(recv, g, send)


def layer_body(recv, w_ref, layer_ref):
    low = pl.multiple_of(pl.program_id(0) * 64, 64)
    layer_ref[...] = dot(attn_columns(recv, low).T, w_ref[...]).astype(BF16)


def layer_output(recv, w):
    rows = TILES_DEV * QROWS
    return pl.pallas_call(
        layer_body,
        grid=(TILES_DEV,),
        in_specs=[
            pl.BlockSpec((16, QUERY_ROWS, 128), lambda t: (0, 0, 0)),
            pl.BlockSpec((HW, D), lambda t: (0, 0)),
        ],
        out_specs=pl.BlockSpec((QROWS, D), lambda t: (t, 0)),
        out_shape=jax.ShapeDtypeStruct((rows, D), BF16),
        compiler_params=params(60),
        cost_estimate=cost(2 * rows * D * HW, 4e6),
        name="layer_output",
    )(recv, w)


def unpack_body(mid, end, dq_ref, dk_ref, dv_ref):
    heads = []
    for head in range(2):
        blocks = []
        for t in range(TILES_DEV):
            for half in range(2):
                blocks.append(end[2 * head + half, t * 64 : t * 64 + 64, :])
        heads.append(jnp.concatenate(blocks, axis=1))
    dq_ref[...] = jnp.concatenate(heads, axis=0).T
    for chunk, part, low in ((0, mid, 0), (1, end, QUERY_ROWS)):
        for j in range(ROWS // 128):
            block = slice(low + j * 128, low + j * 128 + 128)
            take = [part[r, block, :].astype(F32) for r in range(4)]
            x, y = take[0] + take[1], take[2] + take[3]
            at = slice(chunk * ROWS + j * 128, chunk * ROWS + j * 128 + 128)
            dk_ref[at, :] = jnp.concatenate([x[:64], y[:64]], axis=0).astype(BF16).T
            dv_ref[at, :] = jnp.concatenate([x[64:], y[64:]], axis=0).astype(BF16).T


def unpack(mid, end):
    rows = TILES_DEV * QROWS
    return pl.pallas_call(
        unpack_body,
        grid=(4,),
        in_specs=[
            pl.BlockSpec((4, ROWS, 128), lambda p: (p, 0, 0)),
            pl.BlockSpec((4, END_ROWS, 128), lambda p: (p, 0, 0)),
        ],
        out_specs=[
            pl.BlockSpec((rows, 128), lambda p: (0, p)),
            pl.BlockSpec((BT, 128), lambda p: (0, p)),
            pl.BlockSpec((BT, 128), lambda p: (0, p)),
        ],
        out_shape=[
            jax.ShapeDtypeStruct((rows, HW), BF16),
            jax.ShapeDtypeStruct((BT, HW), BF16),
            jax.ShapeDtypeStruct((BT, HW), BF16),
        ],
        compiler_params=params(60),
        cost_estimate=cost(0, 8e6),
        name="unpack",
    )(mid, end)


def swap(x, axes="region"):
    return lax.all_to_all(x, axes, 0, 0, tiled=True)


def spread_body(*refs):
    shares, send_ref = refs[:-1], refs[-1]
    total = shares[0][...].astype(F32)
    for share in shares[1:]:
        total = total + share[...].astype(F32)
    total = total.astype(BF16)
    wide = jnp.concatenate([total[j * 32 : j * 32 + 32] for j in range(D // 128)], axis=1)
    for dest in range(16):
        send_ref[dest] = wide


def orbit_sum(share):
    size = lax.axis_size("orbit")
    shares = [share]
    for shift in range(1, size):
        shares.append(lax.ppermute(share, "orbit", [(i, (i + shift) % size) for i in range(size)]))
    return pl.pallas_call(
        spread_body,
        grid=(1,),
        in_specs=[whole(DW_ROWS, 128)] * size,
        out_specs=whole(16, 32, D),
        out_shape=jax.ShapeDtypeStruct((16, 32, D), BF16),
        compiler_params=params(16),
        cost_estimate=cost(0, 4e6),
        name="spread",
    )(*shares)


def per_device(queries, keys, values, block_lists, band_counts, cotangent, out_weight):
    rows = TILES_DEV * QROWS
    q, g = queries.reshape(rows, HW), cotangent.reshape(rows, D)
    k, v = keys.reshape(BT, HW), values.reshape(BT, HW)
    recv = swap(pack(q, k, v, block_lists.transpose(1, 0, 2), band_counts))
    lists = recv[:, LIST_ROW : LIST_ROW + TILES_DEV, :MAXB].astype(jnp.int32).reshape(TILES, MAXB)
    counts = recv[:, LIST_ROW + 8, :TILES_DEV].astype(jnp.int32).reshape(TILES)
    plan = plan_of(lists, counts)
    d_attn = dattn(out_weight, g)
    recv, d_attn = lax.optimization_barrier((recv, d_attn))
    d_attn = swap(d_attn).reshape(TILES, 64, HALF)

    attn, lse, kv, kt, qt = forward(plan, recv)
    attn_home = swap(attn.reshape(16, QUERY_ROWS, HALF))
    mid, dq = backward(0, plan, kv, kt, qt, d_attn, attn, lse)
    attn_home, mid = lax.optimization_barrier((attn_home, mid))
    mid = weight_grad(attn_home, g, mid)
    mid, dq = lax.optimization_barrier((mid, dq))
    mid = swap(mid)
    (end,) = backward(1, plan, kv, kt, qt, d_attn, attn, lse, dq)
    mid, end, attn_home = lax.optimization_barrier((mid, end, attn_home))
    end = swap(end)
    share = jnp.sum(mid[:, ROWS:].astype(F32), axis=0).astype(BF16)
    total = orbit_sum(share)
    layer = layer_output(attn_home, out_weight)
    end, total, layer = lax.optimization_barrier((end, total, layer))
    total = swap(total)
    d_q, d_k, d_v = unpack(mid, end)
    return (
        layer.reshape(1, TILES_DEV, QROWS, D),
        d_q.reshape(1, TILES_DEV, QROWS, HW),
        d_k.reshape(1, 1, BT, HW),
        d_v.reshape(1, 1, BT, HW),
        total.reshape(HW, D).astype(F32),
    )


def solution(mesh):
    four = P("orbit", "region", None, None)
    return jax.shard_map(
        per_device,
        mesh=mesh,
        in_specs=(four, four, four, P("orbit", "region", None), P("orbit", "region"), four, P()),
        out_specs=(four, four, four, four, P()),
        check_vma=False,
    )
```
